32 devices in a mesh: dp: 16 (over z, x, core), seq: 2 (over y).
Axes of the slice: x: 2, y: 2, z: 4, core: 2. Of those that a mesh axis runs over, the one named last changes fastest.
Arguments:
- tokens: bfloat16 [16, 2048, 256], P('dp', 'seq'), may hold values from -6 to 6
- masked: int32 [16, 2048], P('dp', 'seq'), may hold values 0 or 1
- mask_vector: bfloat16 [256], replicated, may hold values from -4 to 4
- qkv_weight: bfloat16 [2, 256, 768], replicated, may hold values from -0.375 to 0.375
- qv_bias: bfloat16 [2, 2, 256], replicated, may hold values from -2 to 2
- out_weight: bfloat16 [2, 256, 256], replicated, may hold values from -3 to 3
- out_bias: bfloat16 [2, 256], replicated, may hold values from -2 to 2
- norm_gain: bfloat16 [2, 2, 256], replicated, may hold values from 0.5 to 1.5
- norm_bias: bfloat16 [2, 2, 256], replicated, may hold values from -2 to 2
- up_weight: bfloat16 [2, 256, 512], replicated, may hold values from -0.375 to 0.375
- up_bias: bfloat16 [2, 512], replicated, may hold values from -2 to 2
- down_weight: bfloat16 [2, 512, 256], replicated, may hold values from -0.25 to 0.25
- down_bias: bfloat16 [2, 256], replicated, may hold values from -2 to 2
- cotangent: bfloat16 [16, 2048, 256], P('dp', 'seq'), may hold values from -6 to 6
Outputs:
- layer_outputs: bfloat16 [2, 16, 2048, 256], P(None, 'dp', 'seq')
- token_grad: float32 [16, 2048, 256], P('dp', 'seq')
- mask_vector_grad: float32 [256], replicated
- qkv_weight_grad: float32 [2, 256, 768], replicated
- qv_bias_grad: float32 [2, 2, 256], replicated
- out_weight_grad: float32 [2, 256, 256], replicated
- out_bias_grad: float32 [2, 256], replicated
- norm_gain_grad: float32 [2, 2, 256], replicated
- norm_bias_grad: float32 [2, 2, 256], replicated
- up_weight_grad: float32 [2, 256, 512], replicated
- up_bias_grad: float32 [2, 512], replicated
- down_weight_grad: float32 [2, 512, 256], replicated
- down_bias_grad: float32 [2, 256], replicated
The draws below stay inside these ranges and needn't reach their ends.
All inputs are finite; a program needn't handle non-finite values. No bound on the sum of `masked` on one device may be relied on, other than what follows from the above.
Results may differ from the reference program's by a relative error of at most 0.018.
Values may be sent and summed in bfloat16 or wider, within the bound.
A program may use at most 128 MiB of HBM per device.

```python
import jax
import jax.numpy as jnp
from jax import lax

D = 256
HEADS = 4
FF = 512
LENGTH = 2048
LAYERS = 2
CELLS = 16


def plant(values, rng, least, high):
    place = [jax.random.randint(jax.random.fold_in(rng, axis), (), 0, length) for axis, length in enumerate(values.shape)]
    widest = values.shape.index(max(values.shape))
    beside = place[:widest] + [(place[widest] + 1) % values.shape[widest]] + place[widest + 1:]
    return values.at[tuple(place)].set(least).at[tuple(beside)].set(high)


def levels(rng, dims, cuts, least, top_value):
    gain = 1.0
    for position, blocks in cuts:
        steps = jax.random.uniform(jax.random.fold_in(jax.random.fold_in(rng, 6), position), (blocks,), jnp.float32, least / len(cuts), top_value / len(cuts))
        gain = gain * jnp.repeat(jnp.exp(steps), dims[position] // blocks).reshape((-1,) + (1,) * (len(dims) - 1 - position))
    return gain


def scatter_about(rng, shape, scale, bound, shards=(), held_as=jnp.bfloat16):
    gain = levels(rng, shape, shards, -0.22, 0.18) if shards else 1.0
    result = jax.random.normal(rng, shape, jnp.float32) * scale * gain
    return jnp.minimum(jnp.maximum(result, -bound), bound).astype(held_as)


def setup_inputs(seed: int = 0) -> dict:
    key_of = jax.random.split(jax.random.key(seed), 15)
    return {
        "tokens": scatter_about(key_of[0], (CELLS, LENGTH, D), 1.0, 6.0, ((0, 16), (1, 2))),
        "masked": plant((jax.random.randint(key_of[1], (CELLS, LENGTH), 0, 100) < 15).astype(jnp.int32), jax.random.fold_in(key_of[1], 1), 0, 1),
        "mask_vector": scatter_about(key_of[2], (D,), 1.0, 4.0),
        "qkv_weight": scatter_about(key_of[3], (LAYERS, D, 3 * D), D ** -0.5, 0.375),
        "qv_bias": scatter_about(key_of[4], (LAYERS, 2, D), 0.3, 2.0),
        "out_weight": scatter_about(key_of[5], (LAYERS, D, D), (D // 64) ** -0.5, 3.0),
        "out_bias": scatter_about(key_of[6], (LAYERS, D), 0.3, 2.0),
        "norm_gain": jnp.clip(1.0 + 0.1 * jax.random.normal(key_of[7], (LAYERS, 2, D), jnp.float32), 0.5, 1.5).astype(jnp.bfloat16),
        "norm_bias": scatter_about(key_of[8], (LAYERS, 2, D), 0.3, 2.0),
        "up_weight": scatter_about(key_of[9], (LAYERS, D, FF), D ** -0.5, 0.375),
        "up_bias": scatter_about(key_of[10], (LAYERS, FF), 0.3, 2.0),
        "down_weight": scatter_about(key_of[11], (LAYERS, FF, D), FF ** -0.5, 0.25),
        "down_bias": scatter_about(key_of[12], (LAYERS, D), 0.3, 2.0),
        "cotangent": scatter_about(key_of[13], (CELLS, LENGTH, D), 1.0, 6.0, ((0, 16), (1, 2))),
    }


@jax.custom_vjp
def low(v):
    return lax.optimization_barrier(v.astype(jnp.bfloat16)).astype(jnp.float32)

@jax.custom_vjp
def low_back(v):
    return v

def low_keep(v):
    return (low(v), None)

def low_pass(kept, grad):
    return (grad,)

def back_keep(v):
    return (v, None)

def back_low(kept, grad):
    return (low(grad),)
low.defvjp(low_keep, low_pass)
low_back.defvjp(back_keep, back_low)

def product(left, right):
    return jnp.einsum('cpd,de->cpe', left, right, precision=lax.Precision.HIGHEST)

def layer_norm(rows, gain_row, shift_row):
    centre = rows - lax.optimization_barrier(jnp.mean(rows, axis=-1, keepdims=True))
    spread = lax.optimization_barrier(jnp.mean(centre * centre, axis=-1, keepdims=True))
    return centre * lax.rsqrt(spread + 1e-05) * gain_row + shift_row

def attend(packed):
    split_parts = packed.reshape(LENGTH, 3, HEADS, D // HEADS)
    queries = split_parts[:, 0]
    keys_all = split_parts[:, 1]
    values_all = split_parts[:, 2]
    raw_scores = jnp.einsum('qhd,khd->hqk', queries, keys_all, precision=lax.Precision.HIGHEST)
    scores = low_back(raw_scores * (D // HEADS) ** (-0.5))
    attn_probs = low(jax.nn.softmax(scores, axis=-1))
    attended = jnp.einsum('hqk,khd->qhd', attn_probs, values_all, precision=lax.Precision.HIGHEST)
    return low(low_back(attended.reshape(LENGTH, D)))

def apply_layer(hidden, params):
    qkv_mat, qv_shift, out_mat, out_shift, gain_pair, shift_pair, up_mat, up_shift, down_mat, down_shift = params
    qkv_shift = jnp.concatenate([qv_shift[0], jnp.zeros_like(qv_shift[0]), qv_shift[1]])
    rounded = low(hidden)
    projected = low(low_back(product(rounded, qkv_mat) + qkv_shift))
    attended = lax.map(jax.checkpoint(attend), projected)
    branch_out = low_back(product(attended, out_mat) + out_shift)
    normed = layer_norm(hidden + branch_out, gain_pair[0], shift_pair[0])
    pre_act = low_back(product(low(normed), up_mat) + up_shift)
    activated = low(jax.nn.gelu(pre_act))
    ffn_out = low_back(product(activated, down_mat) + down_shift)
    return layer_norm(normed + ffn_out, gain_pair[1], shift_pair[1])

def forward_pass(masked, token_rows, mask_row, stacks):
    hidden = jnp.where(masked[..., None] == 1, mask_row, token_rows)
    outputs = []
    for layer_index in range(LAYERS):
        hidden = apply_layer(hidden, tuple((weight_stack[layer_index] for weight_stack in stacks)))
        outputs.append(hidden)
    return jnp.stack(outputs)

def reference(tokens, masked, mask_vector, qkv_weight, qv_bias, out_weight, out_bias, norm_gain, norm_bias, up_weight, up_bias, down_weight, down_bias, cotangent):
    stacks = tuple((array.astype(jnp.float32) for array in (qkv_weight, qv_bias, out_weight, out_bias, norm_gain, norm_bias, up_weight, up_bias, down_weight, down_bias)))

    def forward_fixed(token_rows, mask_row, weight_stacks):
        return forward_pass(masked, token_rows, mask_row, weight_stacks)
    outputs, pullback = jax.vjp(forward_fixed, tokens.astype(jnp.float32), mask_vector.astype(jnp.float32), stacks)
    seeded = jnp.concatenate([jnp.zeros((LAYERS - 1,) + cotangent.shape, jnp.float32), cotangent.astype(jnp.float32)[None]], axis=0)
    token_grad, mask_grad, weight_grads = pullback(seeded)
    return (outputs.astype(jnp.bfloat16), token_grad, mask_grad, weight_grads[0], weight_grads[1], weight_grads[2], weight_grads[3], weight_grads[4], weight_grads[5], weight_grads[6], weight_grads[7], weight_grads[8], weight_grads[9])
```

```python
import functools
import math

import jax
import jax.numpy as jnp
from jax import lax
from jax.experimental import pallas as pl
from jax.experimental.pallas import tpu as pltpu
from jax.sharding import PartitionSpec as P

LAYERS = 2
HEAD = 64
BF = jnp.bfloat16
F32 = jnp.float32
MESH = pl.DeviceIdType.MESH
LOG2E = 1.4426950408889634
LN2 = 0.6931471805599453
EPS = 1e-05
HALVINGS = 5


def dot_nt(a, b):
    return lax.dot_general(a, b, (((1,), (1,)), ((), ())), preferred_element_type=F32)


def dot_nn(a, b):
    return lax.dot_general(a, b, (((1,), (0,)), ((), ())), preferred_element_type=F32)


def dot_tn(a, b):
    return lax.dot_general(a, b, (((0,), (0,)), ((), ())), preferred_element_type=F32)


def head_lanes(h, width):
    lanes = lax.broadcasted_iota(jnp.int32, (1, width), 1) % 128
    return (lanes < 64) if h % 2 == 0 else (lanes >= 64)


def row_sum(x):
    return jnp.sum(x, axis=0, keepdims=True)


def norm(r):
    c = r - jnp.mean(r, axis=1, keepdims=True)
    rs = lax.rsqrt(jnp.mean(c * c, axis=1, keepdims=True) + EPS)
    return c * rs, rs


def norm_back(t, xhat, rs):
    return rs * (
        t - jnp.mean(t, axis=1, keepdims=True) - xhat * jnp.mean(t * xhat, axis=1, keepdims=True)
    )


class Reduction:
    def __init__(self, acc, out, sbuf, rbuf, send, recv, layer, lo, rows, bits):
        self.acc, self.out, self.sbuf, self.rbuf = acc, out, sbuf, rbuf
        self.send, self.recv = send, recv
        self.layer, self.lo, self.rows, self.bits = layer, lo, rows, bits

    def copy(self, k, src, dst, peer):
        return pltpu.make_async_remote_copy(
            src_ref=src,
            dst_ref=dst,
            send_sem=self.send.at[k],
            recv_sem=self.recv.at[k],
            device_id=peer,
            device_id_type=MESH,
        )

    def steps(self):
        n_half = min(HALVINGS, len(self.bits))
        acc = self.acc.at[self.layer]
        out = self.out.at[self.layer]
        base, size, so = self.lo, self.rows, 0
        bases = []
        for k, (value, peer) in enumerate(self.bits):
            bases.append(base)
            if k < n_half:
                size //= 2
                give = pl.multiple_of(base + (1 - value) * size, 16)
                base = pl.multiple_of(base + value * size, 16)
            else:
                give = base
            place = pl.ds(so, size)
            self.sbuf[place, :] = acc[pl.ds(give, size), :].astype(BF)
            c = self.copy(k, self.sbuf.at[place], self.rbuf.at[place], peer)
            c.start()
            yield
            c.wait()
            acc[pl.ds(base, size), :] += self.rbuf[place, :].astype(F32)
            so += size
        out[pl.ds(base, size), :] = acc[pl.ds(base, size), :].astype(BF)
        for k in reversed(range(n_half)):
            here = out.at[pl.ds(base, size)]
            c = self.copy(len(self.bits) + k, here, here, self.bits[k][1])
            c.start()
            yield
            c.wait()
            base = bases[k]
            size *= 2


def drain(*generators):
    live = list(generators)
    while live:
        live = [g for g in live if next(g, "end") != "end"]


def advance(queue, count=1):
    for _ in range(count):
        while queue:
            if next(queue[0], "end") != "end":
                break
            queue.pop(0)


def main_kernel(sizes, qb_rows, rb_rows, *refs):
    (
        tok, msk, mv, wqkv, qvb, wo, bo, gains, biases, wu, bu, wd, bd, cot,
        lo, tg, red, small, saved,
        tokin, mskin, cotin, hb, hf, qs, kk, vx, vr, vo, om, ol, ox, oo, ff_,
        x1, r1s, x2, r2s, n1s, gs, gps, y1, t1s, y2, t2s, m1s, js, jps,
        dox, dot_t, q_t, dkv, skv, rkv, acc, sm, rsm, pslot, tgs,
        sb_e0, rb_e0, sb_q0, rb_q0, sb_e1, rb_e1, sb_q1, rb_q1,
        swap_send, swap_recv, kv_send, kv_recv, g_send, g_recv, p_sem, lo_sem,
        red_send, red_recv, sm_send, sm_recv,
    ) = refs
    dp_size, seq_size = sizes
    n, d = tok.shape
    ff = wu.shape[2]
    d_i, s_i = lax.axis_index("dp"), lax.axis_index("seq")
    core = d_i % 2
    mate = (d_i + 1 - 2 * core, s_i)
    cross = (d_i + 1 - 2 * core, 1 - s_i)
    swaps = core != s_i
    stays = core == s_i

    dp_bits = [1 << k for k in range(int(math.log2(dp_size)))]

    def dp_bit(b):
        v = (d_i // b) % 2
        return (v, (d_i + b - 2 * b * v, s_i))

    bits = [dp_bit(b) for b in dp_bits[:2]] + [(s_i, (d_i, 1 - s_i))] + [dp_bit(b) for b in dp_bits[2:]]

    barrier = pltpu.get_barrier_semaphore()
    peers = [peer for _, peer in bits] + [cross]
    for peer in peers:
        pl.semaphore_signal(barrier, inc=1, device_id=peer, device_id_type=MESH)
    pl.semaphore_wait(barrier, len(peers))

    def remote(src, dst, send, recv, peer):
        return pltpu.make_async_remote_copy(
            src_ref=src, dst_ref=dst, send_sem=send, recv_sem=recv, device_id=peer, device_id_type=MESH
        )

    def swap(i, src, dst):
        return remote(src, dst, swap_send.at[i], swap_recv.at[i], cross)

    arrive = [swap(0, tok, tokin), swap(1, msk, mskin), swap(2, cot, cotin)]

    @pl.when(swaps)
    def _():
        for c in arrive:
            c.start()

    @pl.when(stays)
    def _():
        tokin[...] = tok[...]
        mskin[...] = msk[...]
        cotin[...] = cot[...]

    for l in range(LAYERS):
        for half in range(2):
            for pair in range(2):
                vx[l, half, pair, :, 128:] = jnp.ones((n, 128), BF)

    @pl.when(swaps)
    def _():
        arrive[0].wait()
        arrive[1].wait()

    mask_rows = jnp.broadcast_to(mskin[...].astype(F32), (16, n)).astype(BF)
    first_row = (lax.broadcasted_iota(jnp.int32, (16, d), 0) == 0).astype(F32).astype(BF)
    is_masked = dot_tn(mask_rows, first_row)
    hb[0] = jnp.where(is_masked > 0.5, mv[...].astype(F32), tokin[...].astype(F32)).astype(BF)

    def gain(l, i):
        return gains[l, i : i + 1, :].astype(F32)

    def shift(l, i):
        return biases[l, i : i + 1, :].astype(F32)

    kv_copies = {}

    def project(l, rows):
        x = hb[l, rows, :]
        q = dot_nn(x, wqkv[l, :, :d]) + qvb[l, 0:1, :].astype(F32)
        qs[l, rows, :] = (q * (LOG2E * HEAD**-0.5)).astype(BF)
        kk[l, 0, rows, :] = dot_nn(x, wqkv[l, :, d : 2 * d]).astype(BF)
        v = (dot_nn(x, wqkv[l, :, 2 * d :]) + qvb[l, 1:2, :].astype(F32)).astype(BF)
        vo[rows, :] = v
        vx[l, 0, 0, rows, :128] = v[:, :128]
        vx[l, 0, 1, rows, :128] = v[:, 128:]

    def send_kv(l):
        copies = [
            remote(kk.at[l, 0], kk.at[l, 1], kv_send.at[l, 0], kv_recv.at[l, 0], mate),
            remote(vo, vr.at[l], kv_send.at[l, 1], kv_recv.at[l, 1], mate),
        ]
        for c in copies:
            c.start()
        kv_copies[l] = copies

    def take_kv(l):
        for c in kv_copies[l]:
            c.wait()
        vx[l, 1, 0, :, :128] = vr[l, :, :128]
        vx[l, 1, 1, :, :128] = vr[l, :, 128:]

    slot_busy = [None] * 4

    def slot_wait(h):
        if slot_busy[h] is not None:
            slot_busy[h].wait()
            slot_busy[h] = None

    def attend(l, half, qb):
        rows = slice(qb * qb_rows, (qb + 1) * qb_rows)

        def scores(h):
            c = slice(h // 2 * 128, h // 2 * 128 + 128)
            qm = jnp.where(head_lanes(h, 128), qs[l, rows, c], jnp.zeros((), BF))
            return dot_nt(qm, kk[l, half, :, c])

        kept = [None, None]
        s = scores(0)
        for h in range(4):
            top = jnp.max(s, axis=1, keepdims=True)
            following = scores(h + 1) if h < 3 else None
            e = jnp.exp2(s - top).astype(BF)
            slot_wait(h)
            pslot[h] = e
            out = pltpu.make_async_copy(pslot.at[h], saved.at[l, half, qb, h], p_sem.at[h])
            out.start()
            slot_busy[h] = out
            r = dot_nn(e, vx[l, half, h // 2])
            s = following
            kept[h % 2] = (r[:, :128], r[:, 128:], top)
            if h % 2 == 1:
                left = head_lanes(0, 128)
                c = slice(h // 2 * 128, h // 2 * 128 + 128)
                for place, i in ((om, 0), (ol, 1), (ox, 2)):
                    place[half, rows, c] = jnp.where(left, kept[0][i], kept[1][i])

    def join(l, rows):
        top = jnp.maximum(ox[0, rows, :], ox[1, rows, :])
        a0, a1 = jnp.exp2(ox[0, rows, :] - top), jnp.exp2(ox[1, rows, :] - top)
        inv = 1.0 / (ol[0, rows, :] * a0 + ol[1, rows, :] * a1)
        f0, f1 = a0 * inv, a1 * inv
        ff_[l, 0, rows, :] = f0
        ff_[l, 1, rows, :] = f1
        o = om[0, rows, :] * f0 + om[1, rows, :] * f1
        oo[l, rows, :] = o
        return o

    def dense_forward(l, rows, keep, krows):
        kx1, kr1, kx2, kr2, kn1, kg, kgp = keep
        o = join(l, rows)
        y = dot_nn(o.astype(BF), wo[l]) + bo[l : l + 1, :].astype(F32)
        h_in = hb[0, rows, :].astype(F32) if l == 0 else hf[rows, :]
        xh, rs = norm(h_in + y)
        kx1[krows, :] = xh
        kr1[krows, :] = rs
        n1 = xh * gain(l, 0) + shift(l, 0)
        n1b = n1.astype(BF)
        kn1[krows, :] = n1b
        u = dot_nn(n1b, wu[l]) + bu[l : l + 1, :].astype(F32)
        c0 = math.sqrt(2.0 / math.pi)
        u2 = u * u
        t = jnp.tanh(c0 * u * (1.0 + 0.044715 * u2))
        g = (0.5 * u * (1.0 + t)).astype(BF)
        kg[krows, :] = g
        kgp[krows, :] = (
            0.5 * (1.0 + t) + 0.5 * u * (1.0 - t * t) * (c0 * (1.0 + 3 * 0.044715 * u2))
        ).astype(BF)
        z, rs2 = norm(n1 + dot_nn(g, wd[l]) + bd[l : l + 1, :].astype(F32))
        kx2[krows, :] = z
        kr2[krows, :] = rs2
        h_out = z * gain(l, 1) + shift(l, 1)
        hb[l + 1, rows, :] = h_out.astype(BF)
        if l + 1 < LAYERS:
            hf[rows, :] = h_out

    def put(l, lo_row, value, first):
        span = slice(lo_row, lo_row + value.shape[0])
        acc[l, span, :] = value if first else acc[l, span, :] + value

    def put_small(l, row, value, first):
        span = slice(16 * l + row, 16 * l + row + 1)
        sm[span, :] = value if first else sm[span, :] + value

    same_head = (
        lax.broadcasted_iota(jnp.int32, (d, d), 0) // HEAD
        == lax.broadcasted_iota(jnp.int32, (d, d), 1) // HEAD
    ).astype(F32).astype(BF)

    def dense_backward(l, rows, g, keep, krows, first):
        kx1, kr1, kx2, kr2, kn1, kg, kgp = keep
        xh = kx2[krows, :]
        put_small(l, 4, row_sum(g * xh), first)
        put_small(l, 6, row_sum(g), first)
        dr2 = norm_back(g * gain(l, 1), xh, kr2[krows, :])
        df = dr2.astype(BF)
        put_small(l, 9, row_sum(df.astype(F32)), first)
        wgrad = dot_tn(kg[krows, :], df)
        for c in range(2):
            put(l, (12 + 2 * c) * 256, wgrad[:, c * 128 : c * 128 + 128], first)
        du = (kgp[krows, :].astype(F32) * dot_nt(df, wd[l])).astype(BF)
        dub = row_sum(du.astype(F32))
        put_small(l, 7, dub[:, :d], first)
        put_small(l, 8, dub[:, d:], first)
        wgrad = dot_tn(kn1[krows, :], du)
        for c in range(4):
            put(l, (8 + c) * 256, wgrad[:, c * 128 : c * 128 + 128], first)
        dn1 = dr2 + dot_nt(du, wu[l])
        xh = kx1[krows, :]
        put_small(l, 3, row_sum(dn1 * xh), first)
        put_small(l, 5, row_sum(dn1), first)
        dr1 = norm_back(dn1 * gain(l, 0), xh, kr1[krows, :])
        ox[0, rows, :] = dr1
        dy = dr1.astype(BF)
        put_small(l, 2, row_sum(dy.astype(F32)), first)
        o = oo[l, rows, :]
        wgrad = dot_tn(o.astype(BF), dy)
        for c in range(2):
            put(l, (6 + c) * 256, wgrad[:, c * 128 : c * 128 + 128], first)
        do = dot_nt(dy, wo[l])
        x = do * o
        hi = x.astype(BF)
        lo_part = (x - hi.astype(F32)).astype(BF)
        delta = dot_nn(hi, same_head) + dot_nn(lo_part, same_head)
        lane = lax.broadcasted_iota(jnp.int32, (1, d), 1) % HEAD
        for half in range(2):
            f = ff_[l, half, rows, :]
            dob = (do * f).astype(BF)
            x = -(delta * f)
            hi = x.astype(BF)
            lo_part = (x - hi.astype(F32)).astype(BF)
            extra = jnp.where(lane == 0, hi, jnp.where(lane == 1, lo_part, jnp.zeros((), BF)))
            for pair in range(2):
                c = slice(pair * 128, pair * 128 + 128)
                dox[half, pair, rows, :128] = dob[:, c]
                dox[half, pair, rows, 128:] = extra[:, c]

    def fetch(l, half, qb, h):
        c = pltpu.make_async_copy(saved.at[l, half, qb, h], pslot.at[h], p_sem.at[h])
        c.start()
        slot_busy[h] = c

    def attend_back(l, half, qb, following, first_half, ticks):
        rows = slice(qb * qb_rows, (qb + 1) * qb_rows)

        def prob_grad(h):
            x = jnp.where(head_lanes(h, 256), dox[half, h // 2, rows, :], jnp.zeros((), BF))
            return dot_nt(x, vx[l, half, h // 2])

        kept = [None, None]
        dp = prob_grad(0)
        for h in range(4):
            c = slice(h // 2 * 128, h // 2 * 128 + 128)
            hr = slice(h * HEAD, (h + 1) * HEAD)
            vrw = slice(d + h * HEAD, d + (h + 1) * HEAD)
            slot_wait(h)
            e = pslot[h]
            dv = dot_nn(dot_t[hr, rows], e)
            dpn = prob_grad(h + 1) if h < 3 else None
            ds = (e.astype(F32) * dp).astype(BF)
            dk = dot_nn(q_t[hr, rows], ds)
            if qb == 0:
                dkv[vrw, :] = dv
                dkv[hr, :] = dk
            else:
                dkv[vrw, :] += dv
                dkv[hr, :] += dk
            kept[h % 2] = dot_nn(ds, kk[l, half, :, c])
            dp = dpn
            if following is not None:
                fetch(*following, h)
            if h % 2 == 1:
                value = jnp.where(head_lanes(0, 128), kept[0], kept[1])
                om[0, rows, c] = value if first_half else om[0, rows, c] + value
                ticks()

    def flip(half):
        for pair in range(2):
            dot_t[pair * 128 : pair * 128 + 128, :] = dox[half, pair, :, :128].T

    def post(l):
        dqb = (om[0] * HEAD**-0.5).astype(BF)
        back[l].wait_recv()
        dk_all = dkv[:d, :] * LN2 + rkv[l, :d, :].astype(F32)
        dv_all = dkv[d:, :] + rkv[l, d:, :].astype(F32)
        dkb = dk_all.astype(BF).T
        dvb = dv_all.astype(BF).T
        x = hb[l]
        for j, part in enumerate((dqb, dkb, dvb)):
            wgrad = dot_tn(x, part)
            for c in range(2):
                put(l, (2 * j + c) * 256, wgrad[:, c * 128 : c * 128 + 128], True)
        put_small(l, 0, row_sum(dqb.astype(F32)), True)
        put_small(l, 1, row_sum(dvb.astype(F32)), True)
        dox[0, 0], dox[0, 1], dox[1, 0] = dqb, dkb, dvb

    def input_grad(l):
        total = ox[0]
        for j, part in enumerate((dox[0, 0], dox[0, 1], dox[1, 0])):
            total = total + dot_nt(part, wqkv[l, :, j * d : (j + 1) * d])
        return total

    n_qb = n // qb_rows
    n_rb = n // rb_rows
    keep0 = (x1, r1s, x2, r2s, n1s, gs, gps)
    keep1 = (y1, t1s, y2, t2s, m1s, js, jps)

    def deliver(l):
        c = swap(3 + l, hb.at[l + 1], lo.at[l])

        @pl.when(swaps)
        def _():
            c.start()

        here = pltpu.make_async_copy(hb.at[l + 1], lo.at[l], lo_sem.at[l])

        @pl.when(stays)
        def _():
            here.start()

        return c, here

    def reduction(l, lo_row, rows, sbuf, rbuf, i):
        return Reduction(
            acc, red, sbuf, rbuf, red_send.at[i], red_recv.at[i], l, lo_row, rows, bits
        ).steps()

    for rb in range(n_rb):
        project(0, slice(rb * rb_rows, (rb + 1) * rb_rows))
    send_kv(0)
    results = []
    queue = []
    back = {}
    for l in range(LAYERS):
        for qb in range(n_qb):
            attend(l, 0, qb)
        take_kv(l)
        for qb in range(n_qb):
            attend(l, 1, qb)
        if l == 0:
            for rb in range(n_rb):
                rows = slice(rb * rb_rows, (rb + 1) * rb_rows)
                dense_forward(0, rows, keep0, rows)
                project(1, rows)
            send_kv(1)
            results.append(deliver(0))

    @pl.when(swaps)
    def _():
        arrive[2].wait()

    for h in range(4):
        slot_wait(h)
        fetch(1, 1, 0, h)
    own = slice(0, rb_rows)
    for rb in range(n_rb):
        rows = slice(rb * rb_rows, (rb + 1) * rb_rows)
        dense_forward(1, rows, keep1, own)
        dense_backward(1, rows, cotin[rows, :].astype(F32), keep1, own, rb == 0)
    results.append(deliver(1))
    early = [reduction(1, 1536, 2560, sb_e1, rb_e1, 0), reduction(0, 1536, 2560, sb_e0, rb_e0, 2)]
    late = [reduction(1, 0, 1536, sb_q1, rb_q1, 1), reduction(0, 0, 1536, sb_q0, rb_q0, 3)]

    for l in reversed(range(LAYERS)):
        if l == 0:
            for rb in range(n_rb):
                rows = slice(rb * rb_rows, (rb + 1) * rb_rows)
                dense_backward(0, rows, ox[0, rows, :], keep0, rows, rb == 0)
                advance(queue)
        queue.append(early[1 - l])
        advance(queue)
        q_t[...] = qs[l].T
        order = [(half, qb) for half in (1, 0) for qb in range(n_qb)]
        for i, (half, qb) in enumerate(order):
            if qb == 0:
                flip(half)
            if i + 1 < len(order):
                following = (l, *order[i + 1])
            else:
                following = (0, 1, 0) if l == 1 else None
            attend_back(l, half, qb, following, half == 1, functools.partial(advance, queue))
            if half == 1 and qb == n_qb - 1:
                if l == 0:
                    back[1].wait_send()
                skv[:d, :] = (dkv[:d, :] * LN2).astype(BF)
                skv[d:, :] = dkv[d:, :].astype(BF)
                back[l] = remote(skv, rkv.at[l], g_send.at[l], g_recv.at[l], mate)
                back[l].start()
        post(l)
        queue.append(late[1 - l])
        if l == 1:
            advance(queue)
            ox[0] = input_grad(1)

    advance(queue)
    dh = input_grad(0)
    tgs[...] = dh.astype(BF)
    gone = swap(5, tgs, tg)
    kept_here = pltpu.make_async_copy(tgs, tg, lo_sem.at[2])

    @pl.when(swaps)
    def _():
        gone.start()

    @pl.when(stays)
    def _():
        kept_here.start()

    hi = dh.astype(BF)
    lo_part = (dh - hi.astype(F32)).astype(BF)
    sm[10:11, :] = (dot_nn(mask_rows, hi) + dot_nn(mask_rows, lo_part))[0:1, :]
    sm[11:16, :] = jnp.zeros((5, d), F32)
    sm[26:32, :] = jnp.zeros((6, d), F32)

    def small_steps():
        for k, (_, peer) in enumerate(bits):
            rsm[2 * k] = sm[...]
            c = remote(rsm.at[2 * k], rsm.at[2 * k + 1], sm_send.at[k], sm_recv.at[k], peer)
            c.start()
            yield
            c.wait()
            sm[...] += rsm[2 * k + 1]

    drain(*queue, small_steps())
    small[...] = sm[...]

    back[0].wait_send()

    @pl.when(swaps)
    def _():
        for c, _ in results:
            c.wait()
        gone.wait()

    @pl.when(stays)
    def _():
        for _, here in results:
            here.wait()
        kept_here.wait()


def spread_kernel(
    lo, tg, red, small, msk,
    o_lo, o_tg, o_mv, o_qkv, o_qvb, o_wo, o_bo, o_gain, o_bias, o_wu, o_bu, o_wd, o_bd,
    sem,
):
    move = pltpu.make_async_copy(lo, o_lo.at[:, 0], sem)
    move.start()
    n, d = tg.shape
    mask_rows = jnp.broadcast_to(msk[...].astype(F32), (16, n)).astype(BF)
    first_row = (lax.broadcasted_iota(jnp.int32, (16, d), 0) == 0).astype(F32).astype(BF)
    o_tg[0] = jnp.where(dot_tn(mask_rows, first_row) > 0.5, 0.0, tg[...].astype(F32))
    o_mv[...] = small[10:11, :]
    for l in range(LAYERS):

        def block(b, rows=256, l=l):
            return red[l, b * 256 : b * 256 + rows, :].astype(F32)

        def row(r, l=l):
            return small[16 * l + r : 16 * l + r + 1, :]

        for c in range(6):
            o_qkv[l, :, c * 128 : c * 128 + 128] = block(c)
        for c in range(2):
            o_wo[l, :, c * 128 : c * 128 + 128] = block(6 + c)
        for c in range(4):
            o_wu[l, :, c * 128 : c * 128 + 128] = block(8 + c)
        for c in range(2):
            o_wd[l, :, c * 128 : c * 128 + 128] = block(12 + 2 * c, 512)
        o_qvb[l, 0:1, :] = row(0)
        o_qvb[l, 1:2, :] = row(1)
        o_bo[l : l + 1, :] = row(2)
        o_gain[l, 0:1, :] = row(3)
        o_gain[l, 1:2, :] = row(4)
        o_bias[l, 0:1, :] = row(5)
        o_bias[l, 1:2, :] = row(6)
        o_bu[l : l + 1, :d] = row(7)
        o_bu[l : l + 1, d:] = row(8)
        o_bd[l : l + 1, :] = row(9)
    move.wait()


def shards(sizes, *args):
    (
        tokens, masked, mask_vector, qkv_weight, qv_bias, out_weight, out_bias, norm_gain,
        norm_bias, up_weight, up_bias, down_weight, down_bias, cotangent,
    ) = args
    _, n, d = tokens.shape
    ff = up_weight.shape[2]
    qb = min(512, n)
    rb = min(512, n)
    n_bits = int(math.log2(sizes[0] * sizes[1]))
    halvings = min(HALVINGS, n_bits)
    vmem, hbm = pl.BlockSpec(memory_space=pltpu.VMEM), pl.BlockSpec(memory_space=pl.ANY)
    V = pltpu.VMEM
    dma = pltpu.SemaphoreType.DMA

    def room(rows):
        return V((rows + max(0, n_bits - halvings - 1) * (rows >> halvings), 128), BF)

    def kept(rows):
        return [
            V((rows, d), F32), V((rows, 1), F32), V((rows, d), F32), V((rows, 1), F32),
            V((rows, d), BF), V((rows, ff), BF), V((rows, ff), BF),
        ]

    scratch = [
        V((n, d), BF), V((1, n), jnp.int32), V((n, d), BF),
        V((LAYERS + 1, n, d), BF), V((n, d), F32),
        V((LAYERS, n, d), BF), V((LAYERS, 2, n, d), BF), V((LAYERS, 2, 2, n, 256), BF),
        V((LAYERS, n, d), BF), V((n, d), BF),
        V((2, n, d), F32), V((2, n, d), F32), V((2, n, d), F32),
        V((LAYERS, n, d), F32), V((LAYERS, 2, n, d), F32),
        *kept(n), *kept(rb),
        V((2, 2, n, 256), BF), V((d, n), BF), V((d, n), BF),
        V((2 * d, n), F32), V((2 * d, n), BF), V((LAYERS, 2 * d, n), BF),
        V((LAYERS, 4096, 128), F32), V((32, d), F32), V((2 * n_bits, 32, d), F32),
        V((4, qb, n), BF), V((n, d), BF),
        *[room(rows) for rows in (2560, 2560, 1536, 1536) * LAYERS],
        dma((6,)), dma((6,)), dma((LAYERS, 2)), dma((LAYERS, 2)), dma((LAYERS,)), dma((LAYERS,)),
        dma((4,)), dma((3,)),
        dma((4, 2 * n_bits)), dma((4, 2 * n_bits)), dma((n_bits,)), dma((n_bits,)),
    ]
    lo, tg, red, small, _ = pl.pallas_call(
        functools.partial(main_kernel, sizes, qb, rb),
        out_shape=(
            jax.ShapeDtypeStruct((LAYERS, n, d), BF),
            jax.ShapeDtypeStruct((n, d), BF),
            jax.ShapeDtypeStruct((LAYERS, 4096, 128), BF),
            jax.ShapeDtypeStruct((32, d), F32),
            jax.ShapeDtypeStruct((LAYERS, 2, n // qb, 4, qb, n), BF),
        ),
        in_specs=[vmem] * 14,
        out_specs=(hbm, hbm, vmem, vmem, hbm),
        scratch_shapes=scratch,
        compiler_params=pltpu.CompilerParams(
            collective_id=0, has_side_effects=True, vmem_limit_bytes=63 << 20
        ),
        name="encoder",
    )(
        tokens[0], masked, mask_vector[None], qkv_weight, qv_bias, out_weight, out_bias,
        norm_gain, norm_bias, up_weight, up_bias, down_weight, down_bias, cotangent[0],
    )

    def f32(*shape):
        return jax.ShapeDtypeStruct(shape, F32)

    outs = pl.pallas_call(
        spread_kernel,
        out_shape=(
            jax.ShapeDtypeStruct((LAYERS, 1, n, d), BF),
            f32(1, n, d), f32(1, d), f32(LAYERS, d, 3 * d), f32(LAYERS, 2, d), f32(LAYERS, d, d),
            f32(LAYERS, d), f32(LAYERS, 2, d), f32(LAYERS, 2, d), f32(LAYERS, d, ff), f32(LAYERS, ff),
            f32(LAYERS, ff, d), f32(LAYERS, d),
        ),
        in_specs=[hbm, vmem, vmem, vmem, vmem],
        out_specs=(hbm, *[vmem] * 12),
        scratch_shapes=[dma],
        compiler_params=pltpu.CompilerParams(vmem_limit_bytes=48 << 20),
        name="spread",
    )(lo, tg, red, small, masked)
    return (*outs[:2], outs[2][0], *outs[3:])


def solution(mesh):
    rows = P("dp", "seq", None)
    in_specs = (rows, P("dp", "seq"), *[P()] * 11, rows)
    out_specs = (P(None, "dp", "seq", None), rows, *[P()] * 11)
    sizes = (mesh.shape["dp"], mesh.shape["seq"])
    return jax.shard_map(
        functools.partial(shards, sizes), mesh=mesh, in_specs=in_specs, out_specs=out_specs, check_vma=False
    )
```

```python
import functools
import math

import jax
import jax.numpy as jnp
from jax import lax
from jax.experimental import pallas as pl
from jax.experimental.pallas import tpu as pltpu
from jax.sharding import PartitionSpec as P

LAYERS = 2
HEAD = 64
BF = jnp.bfloat16
F32 = jnp.float32
MESH = pl.DeviceIdType.MESH
LOG2E = 1.4426950408889634
LN2 = 0.6931471805599453
EPS = 1e-05


def dot_nt(a, b):
    return lax.dot_general(a, b, (((1,), (1,)), ((), ())), preferred_element_type=F32)


def dot_nn(a, b):
    return lax.dot_general(a, b, (((1,), (0,)), ((), ())), preferred_element_type=F32)


def dot_tn(a, b):
    return lax.dot_general(a, b, (((0,), (0,)), ((), ())), preferred_element_type=F32)


def head_lanes(h, width):
    lanes = lax.broadcasted_iota(jnp.int32, (1, width), 1) % 128
    return (lanes < 64) if h % 2 == 0 else (lanes >= 64)


def row_sum(x):
    return jnp.sum(x, axis=0, keepdims=True)


def norm(r):
    c = r - jnp.mean(r, axis=1, keepdims=True)
    rs = lax.rsqrt(jnp.mean(c * c, axis=1, keepdims=True) + EPS)
    return c * rs, rs


def norm_back(t, xhat, rs):
    return rs * (
        t - jnp.mean(t, axis=1, keepdims=True) - xhat * jnp.mean(t * xhat, axis=1, keepdims=True)
    )


def flips(mask, count):
    return [i for i in range(count) if mask >> i & 1]


class Reduction:
    def __init__(self, acc, out, sbuf, rbuf, send, recv, layer, lo, rows, rounds, ticks):
        self.acc, self.out, self.sbuf, self.rbuf = acc, out, sbuf, rbuf
        self.send, self.recv = send, recv
        self.layer, self.lo, self.rows, self.rounds, self.ticks = layer, lo, rows, rounds, ticks
        self.sems = 0

    def copy(self, src, dst, peer):
        k = self.sems
        self.sems += 1
        return pltpu.make_async_remote_copy(
            src_ref=src,
            dst_ref=dst,
            send_sem=self.send.at[k],
            recv_sem=self.recv.at[k],
            device_id=peer,
            device_id_type=MESH,
        )

    def steps(self):
        acc, out = self.acc.at[self.layer], self.out.at[self.layer]
        base, size, so = self.lo, self.rows, 0
        bases = []
        for (split, values, peers), wait in zip(self.rounds, self.ticks):
            bases.append((base, size))
            count = len(values)
            part = size >> count if split else size
            copies, places = [], []
            for mask in range(1, 1 << count):
                give = base
                if split:
                    for i, v in enumerate(values):
                        give = give + (1 - v if mask >> i & 1 else v) * ((part << i))
                    give = pl.multiple_of(give, 16)
                place = pl.ds(so, part)
                so += part
                self.sbuf[place, :] = acc[pl.ds(give, part), :].astype(BF)
                c = self.copy(self.sbuf.at[place], self.rbuf.at[place], peers[mask])
                c.start()
                copies.append(c)
                places.append(place)
            if split:
                for i, v in enumerate(values):
                    base = base + v * (part << i)
                base = pl.multiple_of(base, 16)
                size = part
            for _ in range(wait):
                yield
            for c in copies:
                c.wait()
            mine = pl.ds(base, size)
            got = [self.rbuf[place, :].astype(F32) for place in places]
            held = acc[mine, :]
            if not split:
                held = held.astype(BF).astype(F32)
            if count == 1:
                acc[mine, :] = held + got[0]
            else:
                acc[mine, :] = (held + got[0]) + (got[1] + got[2])
        mine = pl.ds(base, size)
        out[mine, :] = acc[mine, :].astype(BF)
        for (split, values, peers), wait, (up_base, up_size) in reversed(
            list(zip(self.rounds, self.ticks, bases))
        ):
            if not split:
                continue
            here = out.at[pl.ds(base, size)]
            copies = [self.copy(here, here, peers[m]) for m in range(1, 1 << len(values))]
            for c in copies:
                c.start()
            for _ in range(wait):
                yield
            for c in copies:
                c.wait()
            base, size = up_base, up_size


def drain(*generators):
    live = list(generators)
    while live:
        live = [g for g in live if next(g, "end") != "end"]


def advance(queue):
    queue[:] = [g for g in queue if next(g, "end") != "end"]


def main_kernel(sizes, qb_rows, rb_rows, *refs):
    (
        tok, msk, mv, wqkv_in, qvb, wo_in, bo, gains, biases, wu_in, bu, wd_in, bd, cot,
        lo, tg, red, small, saved,
        wqkv, wo, wu, wd,
        mskin, cotin, hb, dr, qs, kk, vx, oo, ff_,
        x1, x2, rss, n1s, gs, gps, n1_last, rs_last,
        dox, dot_t, q_t, dkv, skv, rkv, acc, sm, rsm, probs,
        sb_e, sb_a, sb_b, rb_e, rb_a, rb_b,
        swap_send, swap_recv, kv_send, kv_recv, g_send, g_recv, p_sem, lo_sem,
        red_send, red_recv, sm_send, sm_recv, load_sem,
    ) = refs
    dp_size, seq_size = sizes
    n, d = tok.shape
    n_qb, n_rb = n // qb_rows, n // rb_rows
    d_i, s_i = lax.axis_index("dp"), lax.axis_index("seq")
    core = d_i % 2
    mate = (d_i + 1 - 2 * core, s_i)
    cross = (d_i + 1 - 2 * core, 1 - s_i)
    swaps = core != s_i
    stays = core == s_i
    apart = (core + s_i) % 2

    def place_bit(axis, b):
        return (axis, b, ((d_i if axis == "dp" else s_i) // b) % 2)

    def make_round(split, *placed):
        peers = [None]
        for mask in range(1, 1 << len(placed)):
            spot = {"dp": d_i, "seq": s_i}
            for i in flips(mask, len(placed)):
                axis, b, v = placed[i]
                spot[axis] = spot[axis] + b - 2 * b * v
            peers.append((spot["dp"], spot["seq"]))
        return (split, [v for _, _, v in placed], peers)

    further = int(math.log2(dp_size)) - 4
    near = [
        make_round(True, place_bit("dp", 1)),
        make_round(True, place_bit("dp", 2), place_bit("seq", 1)),
    ]
    far = [make_round(False, place_bit("dp", 16 << k)) for k in range(further)]
    line = [place_bit("dp", 4), place_bit("dp", 8)]
    rounds_big = [*near, make_round(True, *line), *far]
    rounds_low = [*near, make_round(False, *line), *far]

    loads = [
        pltpu.make_async_copy(src, dst, load_sem.at[i])
        for i, (src, dst) in enumerate(((wqkv_in, wqkv), (wo_in, wo), (wu_in, wu), (wd_in, wd)))
    ]
    for c in loads:
        c.start()
    barrier = pltpu.get_barrier_semaphore()
    peers = [peer for _, _, group in rounds_big for peer in group[1:]] + [cross]
    for peer in peers:
        pl.semaphore_signal(barrier, inc=1, device_id=peer, device_id_type=MESH)
    pl.semaphore_wait(barrier, len(peers))

    def remote(src, dst, send, recv, peer):
        return pltpu.make_async_remote_copy(
            src_ref=src, dst_ref=dst, send_sem=send, recv_sem=recv, device_id=peer, device_id_type=MESH
        )

    def swap(i, src, dst):
        return remote(src, dst, swap_send.at[i], swap_recv.at[i], cross)

    def part(rb):
        return pl.ds(rb * rb_rows, rb_rows)

    arrive_mask = swap(0, msk, mskin)
    arrive_cot = swap(1, cot, cotin)
    arrive = [swap(5 + rb, tok.at[part(rb)], hb.at[0, part(rb)]) for rb in range(n_rb)]
    here_tok = pltpu.make_async_copy(tok, hb.at[0], load_sem.at[4])
    here_cot = pltpu.make_async_copy(cot, cotin, lo_sem.at[3])

    @pl.when(swaps)
    def _():
        arrive_mask.start()
        for c in arrive:
            c.start()

    @pl.when(stays)
    def _():
        here_tok.start()
        here_cot.start()
        mskin[...] = msk[...]

    for l in range(LAYERS):
        for half in range(2):
            for pair in range(2):
                vx[l, half, pair, :, 128:] = jnp.ones((n, 128), BF)

    first_row = (lax.broadcasted_iota(jnp.int32, (16, d), 0) == 0).astype(F32).astype(BF)

    def mask_rows(rows):
        return jnp.broadcast_to(mskin[:, rows].astype(F32), (16, rows.stop - rows.start)).astype(BF)

    def gain(l, i):
        return gains[l, i : i + 1, :].astype(F32)

    def shift(l, i):
        return biases[l, i : i + 1, :].astype(F32)

    def v_sent():
        return dox.at[1, 0]

    def v_got(l):
        return dox.at[0, l]

    def block_rows(rb):
        return slice(rb * rb_rows, (rb + 1) * rb_rows)

    def embed(rb):
        rows = block_rows(rb)
        is_masked = dot_tn(mask_rows(rows), first_row) > 0.5
        x = jnp.where(is_masked, mv[...].astype(F32).reshape(1, d), hb[0, rows, :].astype(F32))
        hb[0, rows, :] = x.astype(BF)

    def project(l, rb):
        rows = block_rows(rb)
        x = hb[l, rows, :]
        q = dot_nn(x, wqkv[l, :, :d]) + qvb[l, 0:1, :].astype(F32)
        qs[l, rows, :] = (q * (LOG2E * HEAD**-0.5)).astype(BF)
        kk[l, 0, rows, :] = dot_nn(x, wqkv[l, :, d : 2 * d]).astype(BF)
        v = (dot_nn(x, wqkv[l, :, 2 * d :]) + qvb[l, 1:2, :].astype(F32)).astype(BF)
        v_sent()[rows, :] = v
        vx[l, 0, 0, rows, :128] = v[:, :128]
        vx[l, 0, 1, rows, :128] = v[:, 128:]

    def kv_copies(l):
        return [
            remote(kk.at[l, 0], kk.at[l, 1], kv_send.at[l, 0], kv_recv.at[l, 0], mate),
            remote(v_sent(), v_got(l), kv_send.at[l, 1], kv_recv.at[l, 1], mate),
        ]

    def send_kv(l):
        for c in kv_copies(l):
            c.start()

    def take_kv(l):
        for c in kv_copies(l):
            c.wait_recv()
        vx[l, 1, 0, :, :128] = v_got(l)[:, :128]
        vx[l, 1, 1, :, :128] = v_got(l)[:, 128:]

    def attend(l, half, qb, before):
        rows = slice(qb * qb_rows, (qb + 1) * qb_rows)

        def scores(h):
            c = slice(h // 2 * 128, h // 2 * 128 + 128)
            qm = jnp.where(head_lanes(h, 128), qs[l, rows, c], jnp.zeros((), BF))
            return dot_nt(qm, kk[l, half, :, c])

        kept = [None, None]
        s = scores(0)
        for h in range(4):
            top = jnp.max(s, axis=1, keepdims=True)
            following = scores(h + 1) if h < 3 else None
            e = jnp.exp2(s - top).astype(BF)
            probs[half, qb, h] = e
            r = dot_nn(e, vx[l, half, h // 2])
            s = following
            kept[h % 2] = (r[:, :128], r[:, 128:], top)
            if h % 2 == 1:
                left = head_lanes(0, 128)
                c = slice(h // 2 * 128, h // 2 * 128 + 128)
                o, total, top = (jnp.where(left, kept[0][i], kept[1][i]) for i in range(3))
                if before is None:
                    oo[l, rows, c] = o
                    ff_[l, 0, rows, c] = total
                    ff_[l, 1, rows, c] = top
                else:
                    total0, top0 = ff_[l, 0, rows, c], ff_[l, 1, rows, c]
                    both = jnp.maximum(top0, top)
                    a0, a1 = jnp.exp2(top0 - both), jnp.exp2(top - both)
                    inv = 1.0 / (total0 * a0 + total * a1)
                    ff_[l, before, rows, c] = a0 * inv
                    ff_[l, half, rows, c] = a1 * inv
                    oo[l, rows, c] = oo[l, rows, c] * (a0 * inv) + o * (a1 * inv)

    def dense_forward(l, rows, keep, krows):
        kx1, kx2, kr, kn1, kg, kgp = keep
        y = dot_nn(oo[l, rows, :].astype(BF), wo[l]) + bo[l : l + 1, :].astype(F32)
        h_in = hb[0, rows, :].astype(F32) if l == 0 else dr[rows, :]
        xh, rs = norm(h_in + y)
        kx1[krows, :] = xh
        kr[krows, 0:1] = rs
        n1 = xh * gain(l, 0) + shift(l, 0)
        n1b = n1.astype(BF)
        kn1[krows, :] = n1b
        u = dot_nn(n1b, wu[l]) + bu[l : l + 1, :].astype(F32)
        c0 = math.sqrt(2.0 / math.pi)
        u2 = u * u
        t = jnp.tanh(c0 * u * (1.0 + 0.044715 * u2))
        g = (0.5 * u * (1.0 + t)).astype(BF)
        kg[krows, :] = g
        kgp[krows, :] = (
            0.5 * (1.0 + t) + 0.5 * u * (1.0 - t * t) * (c0 * (1.0 + 3 * 0.044715 * u2))
        ).astype(BF)
        z, rs2 = norm(n1 + dot_nn(g, wd[l]) + bd[l : l + 1, :].astype(F32))
        kx2[krows, :] = z
        kr[krows, 1:2] = rs2
        h_out = z * gain(l, 1) + shift(l, 1)
        hb[l + 1, rows, :] = h_out.astype(BF)
        if l + 1 < LAYERS:
            dr[rows, :] = h_out

    def put(l, lo_row, value, first):
        span = slice(lo_row, lo_row + value.shape[0])
        acc[l, span, :] = value if first else acc[l, span, :] + value

    def put_small(l, row, value, first, c=slice(None)):
        span = slice(16 * l + row, 16 * l + row + 1)
        sm[span, c] = value if first else sm[span, c] + value

    same_head = (
        lax.broadcasted_iota(jnp.int32, (d, d), 0) // HEAD
        == lax.broadcasted_iota(jnp.int32, (d, d), 1) // HEAD
    ).astype(F32).astype(BF)

    def dense_backward(l, rows, g, keep, krows, first):
        kx1, kx2, kr, kn1, kg, kgp = keep
        xh = kx2[krows, :]
        put_small(l, 4, row_sum(g * xh), first)
        put_small(l, 6, row_sum(g), first)
        dr2 = norm_back(g * gain(l, 1), xh, kr[krows, 1:2])
        df = dr2.astype(BF)
        put_small(l, 9, row_sum(df.astype(F32)), first)
        wgrad = dot_tn(kg[krows, :], df)
        for c in range(2):
            put(l, (12 + 2 * c) * 256, wgrad[:, c * 128 : c * 128 + 128], first)
        du = (kgp[krows, :].astype(F32) * dot_nt(df, wd[l])).astype(BF)
        dub = row_sum(du.astype(F32))
        put_small(l, 7, dub[:, :d], first)
        put_small(l, 8, dub[:, d:], first)
        wgrad = dot_tn(kn1[krows, :], du)
        for c in range(4):
            put(l, (8 + c) * 256, wgrad[:, c * 128 : c * 128 + 128], first)
        dn1 = dr2 + dot_nt(du, wu[l])
        xh = kx1[krows, :]
        put_small(l, 3, row_sum(dn1 * xh), first)
        put_small(l, 5, row_sum(dn1), first)
        dr1 = norm_back(dn1 * gain(l, 0), xh, kr[krows, 0:1])
        dr[rows, :] = dr1
        dy = dr1.astype(BF)
        put_small(l, 2, row_sum(dy.astype(F32)), first)
        o = oo[l, rows, :]
        wgrad = dot_tn(o.astype(BF), dy)
        for c in range(2):
            put(l, (6 + c) * 256, wgrad[:, c * 128 : c * 128 + 128], first)
        do = dot_nt(dy, wo[l])
        x = do * o
        hi = x.astype(BF)
        lo_part = (x - hi.astype(F32)).astype(BF)
        delta = dot_nn(hi, same_head) + dot_nn(lo_part, same_head)
        lane = lax.broadcasted_iota(jnp.int32, (1, d), 1) % HEAD
        for half in range(2):
            f = ff_[l, half, rows, :]
            dob = (do * f).astype(BF)
            x = -(delta * f)
            hi = x.astype(BF)
            lo_part = (x - hi.astype(F32)).astype(BF)
            extra = jnp.where(lane == 0, hi, jnp.where(lane == 1, lo_part, jnp.zeros((), BF)))
            for pair in range(2):
                c = slice(pair * 128, pair * 128 + 128)
                dox[half, pair, rows, :128] = dob[:, c]
                dox[half, pair, rows, 128:] = extra[:, c]

    dq = ff_.at[1, 0]

    def attend_back(l, pair, half, ticks):
        c = slice(pair * 128, pair * 128 + 128)
        dot_t[half] = dox[half, pair, :, :128].T
        work = [(qb, side) for qb in range(n_qb) for side in range(2)]

        def rows_of(qb):
            return slice(qb * qb_rows, (qb + 1) * qb_rows)

        def prob_grad(qb, side):
            x = jnp.where(head_lanes(side, 256), dox[half, pair, rows_of(qb), :], jnp.zeros((), BF))
            return dot_nt(x, vx[l, half, pair])

        kept = [None, None]
        dp = prob_grad(*work[0])
        for i, (qb, side) in enumerate(work):
            rows = rows_of(qb)
            hr = slice(side * HEAD, (side + 1) * HEAD)
            krw = slice(pair * d + side * HEAD, pair * d + (side + 1) * HEAD)
            vrw = slice(pair * d + 128 + side * HEAD, pair * d + 128 + (side + 1) * HEAD)
            e = probs[half, qb, 2 * pair + side]
            dv = dot_nn(dot_t[half, hr, rows], e)
            dpn = prob_grad(*work[i + 1]) if i + 1 < len(work) else None
            ds = (e.astype(F32) * dp).astype(BF)
            dk = dot_nn(q_t[pair * 128 + side * HEAD : pair * 128 + (side + 1) * HEAD, rows], ds)
            if qb == 0:
                dkv[vrw, :] = dv
                dkv[krw, :] = dk
            else:
                dkv[vrw, :] += dv
                dkv[krw, :] += dk
            kept[side] = dot_nn(ds, kk[l, half, :, c])
            dp = dpn
            if side == 1:
                value = jnp.where(head_lanes(0, 128), kept[0], kept[1])
                dq[rows, c] = value if half == 1 else dq[rows, c] + value
                ticks()

    def pair_rows(pair):
        return slice(pair * d, (pair + 1) * d)

    def back_copy(l, pair):
        span = pl.ds(pair * d, d)
        return remote(skv.at[span], rkv.at[l, span], g_send.at[l, pair], g_recv.at[l, pair], mate)

    def send_back(l, pair):
        if l == 0:
            back_copy(1, pair).wait_send()
        r = pair * d
        skv[r : r + 128, :] = (dkv[r : r + 128, :] * LN2).astype(BF)
        skv[r + 128 : r + d, :] = dkv[r + 128 : r + d, :].astype(BF)
        back_copy(l, pair).start()

    def post(l, pair):
        r = pair * d
        c = slice(pair * 128, pair * 128 + 128)
        dqb = (dq[:, c] * HEAD**-0.5).astype(BF)
        back_copy(l, pair).wait_recv()
        dkb = (dkv[r : r + 128, :] * LN2 + rkv[l, r : r + 128, :].astype(F32)).astype(BF).T
        dvb = (dkv[r + 128 : r + d, :] + rkv[l, r + 128 : r + d, :].astype(F32)).astype(BF).T
        dqk = jnp.concatenate([dqb, dkb], axis=1)
        x = hb[l]
        wgrad = dot_tn(x, dqk)
        put(l, pair * 768, wgrad[:, :128], True)
        put(l, pair * 768 + 256, wgrad[:, 128:], True)
        put(l, pair * 768 + 512, dot_tn(x, dvb), True)
        put_small(l, 0, row_sum(dqb.astype(F32)), True, c)
        put_small(l, 1, row_sum(dvb.astype(F32)), True, c)
        dox[0, pair] = dqk
        dox[1, pair, :, :128] = dvb

    def input_grad(l):
        total = dr[...]
        for pair in range(2):
            c = slice(pair * 128, pair * 128 + 128)
            w = jnp.concatenate([wqkv[l, :, c], wqkv[l, :, d + c.start : d + c.stop]], axis=1)
            total = total + dot_nt(dox[0, pair], w)
        dv = jnp.concatenate([dox[1, 0, :, :128], dox[1, 1, :, :128]], axis=1)
        return total + dot_nt(dv, wqkv[l, :, 2 * d :])

    keep0 = (x1, x2, rss, n1s, gs, gps)
    f = wu.shape[2]
    keep1 = (
        dkv.at[:, 0:d], dkv.at[:, d : 2 * d], rs_last, n1_last,
        skv.at[:, 0:f], skv.at[:, f : 2 * f],
    )

    def deliver(l):
        c = swap(2 + l, hb.at[l + 1], lo.at[l])
        here = pltpu.make_async_copy(hb.at[l + 1], lo.at[l], lo_sem.at[l])

        @pl.when(swaps)
        def _():
            c.start()

        @pl.when(stays)
        def _():
            here.start()

        return c, here

    def reduction(l, lo_row, rows, big, sbuf, rbuf, i, ticks):
        return Reduction(
            acc, red, sbuf, rbuf, red_send.at[i], red_recv.at[i], l, lo_row, rows,
            rounds_big if big else rounds_low, ticks + (2,) * further,
        ).steps()

    groups = {}
    for l in range(LAYERS):
        groups[l, "dense"] = reduction(l, 1536, 2560, True, sb_e, rb_e, 3 * l, (1, 3, 2))
        groups[l, 0] = reduction(l, 0, 768, False, sb_a, rb_a.at[l], 3 * l + 1, (1, 2, 2))
        ticks = (1, 1, 1) if l == 0 else (1, 2, 2)
        groups[l, 1] = reduction(l, 768, 768, False, sb_b, rb_b.at[l], 3 * l + 2, ticks)

    @pl.when(swaps)
    def _():
        arrive_mask.wait()
        arrive[0].wait()

    @pl.when(stays)
    def _():
        here_tok.wait()

    for c in loads:
        c.wait()
    embed(0)
    project(0, 0)

    @pl.when(stays)
    def _():
        for rb in range(1, n_rb):
            embed(rb)
            project(0, rb)
        send_kv(0)

    @pl.when(swaps)
    def _():
        take_kv(0)

    attend(0, apart, 0, None)

    @pl.when(swaps)
    def _():
        for rb in range(1, n_rb):
            arrive[rb].wait()
            embed(rb)
            project(0, rb)
        send_kv(0)
        arrive_cot.start()

    for qb in range(1, n_qb):
        attend(0, apart, qb, None)
    keep_probs = [
        pltpu.make_async_copy(probs.at[half], saved.at[half], p_sem.at[i])
        for i, half in enumerate((apart, 1 - apart))
    ]
    keep_probs[0].start()

    @pl.when(stays)
    def _():
        take_kv(0)

    for qb in range(n_qb):
        attend(0, 1 - apart, qb, apart)
    keep_probs[1].start()
    for c in kv_copies(0):
        c.wait_send()
    for rb in range(n_rb):
        rows = block_rows(rb)
        dense_forward(0, rows, keep0, rows)
        project(1, rb)
    send_kv(1)
    results = [deliver(0)]
    for c in keep_probs:
        c.wait()
    for qb in range(n_qb):
        attend(1, 0, qb, None)
    take_kv(1)
    for qb in range(n_qb):
        attend(1, 1, qb, 0)
    for c in kv_copies(1):
        c.wait_send()

    @pl.when(swaps)
    def _():
        arrive_cot.wait()

    @pl.when(stays)
    def _():
        here_cot.wait()

    own = slice(0, rb_rows)
    for rb in range(n_rb):
        rows = block_rows(rb)
        dense_forward(1, rows, keep1, own)
        dense_backward(1, rows, cotin[rows, :].astype(F32), keep1, own, rb == 0)
    results.append(deliver(1))

    def fetch(pair, half):
        heads = pl.ds(2 * pair, 2)
        return pltpu.make_async_copy(
            saved.at[half, :, heads], probs.at[half, :, heads], p_sem.at[2 + 2 * pair + half]
        )

    queue = []
    tick = functools.partial(advance, queue)
    for l in reversed(range(LAYERS)):
        if l == 0:
            for rb in range(n_rb):
                rows = block_rows(rb)
                dense_backward(0, rows, dr[rows, :], keep0, rows, rb == 0)
                tick()
            drain(groups[1, "dense"])
        queue.append(groups[l, "dense"])
        tick()
        q_t[...] = qs[l].T
        for pair in range(2):
            for half in (1, 0):
                if l == 0:
                    fetch(pair, half).wait()
                attend_back(l, pair, half, tick)
                if l == 1:
                    fetch(pair, half).start()
                if half == 1:
                    send_back(l, pair)
            if l == 0:
                drain(groups[1, pair])
            post(l, pair)
            queue.append(groups[l, pair])
            tick()
        if l == 1:
            dr[...] = input_grad(1)
            tick()

    dh = input_grad(0)
    hi = dh.astype(BF)
    cotin[...] = hi
    lo_part = (dh - hi.astype(F32)).astype(BF)
    masks = mask_rows(slice(0, n))
    sm[10:11, :] = (dot_nn(masks, hi) + dot_nn(masks, lo_part))[0:1, :]
    sm[11:16, :] = jnp.zeros((5, d), F32)
    sm[26:32, :] = jnp.zeros((6, d), F32)

    def small_steps():
        k = 0
        for _, values, peers in rounds_big:
            rsm[2 * k] = sm[...]
            copies = []
            for m in range(1, 1 << len(values)):
                c = remote(rsm.at[2 * k], rsm.at[2 * (k + m) - 1], sm_send.at[k + m - 1], sm_recv.at[k + m - 1], peers[m])
                c.start()
                copies.append(c)
            yield
            for c in copies:
                c.wait()
            if len(values) == 1:
                sm[...] += rsm[2 * k + 1]
            else:
                sm[...] = (sm[...] + rsm[2 * k + 1]) + (rsm[2 * k + 3] + rsm[2 * k + 5])
            k += (1 << len(values)) - 1

    queue.append(small_steps())
    tick()
    tick()
    gone = swap(4, cotin, tg)
    kept_here = pltpu.make_async_copy(cotin, tg, lo_sem.at[2])

    @pl.when(swaps)
    def _():
        gone.start()

    @pl.when(stays)
    def _():
        kept_here.start()

    drain(*queue)
    small[...] = sm[...]
    for pair in range(2):
        back_copy(0, pair).wait_send()

    @pl.when(swaps)
    def _():
        for c, _ in results:
            c.wait()
        gone.wait()

    @pl.when(stays)
    def _():
        for _, here in results:
            here.wait()
        kept_here.wait()


def spread_kernel(
    lo, tg_in, red_in, small_in, msk,
    o_lo, o_tg, o_mv, o_qkv, o_qvb, o_wo, o_bo, o_gain, o_bias, o_wu, o_bu, o_wd, o_bd,
    tg, red, small, tgf, qkv, wo, wu, wd, low, sem,
):
    pairs = [(tg_in, tg), (small_in, small)]
    pairs += [(red_in.at[l, r], red.at[l, r]) for l in range(LAYERS) for r in (pl.ds(0, 1536), pl.ds(1536, 2560))]
    pairs += [(lo, low)]
    takes = [pltpu.make_async_copy(a, b, sem.at[i]) for i, (a, b) in enumerate(pairs)]
    for c in takes:
        c.start()
    gives = []

    def give(a, b):
        c = pltpu.make_async_copy(a, b, sem.at[len(takes) + len(gives)])
        c.start()
        gives.append(c)

    n, d = tg.shape
    mask_rows = jnp.broadcast_to(msk[...].astype(F32), (16, n)).astype(BF)
    first_row = (lax.broadcasted_iota(jnp.int32, (16, d), 0) == 0).astype(F32).astype(BF)
    is_masked = dot_tn(mask_rows, first_row) > 0.5
    takes[0].wait()
    tgf[...] = jnp.where(is_masked, 0.0, tg[...].astype(F32))
    give(tgf, o_tg.at[0])
    for l in range(LAYERS):

        def block(b, rows=256, l=l):
            return red[l, b * 256 : b * 256 + rows, :].astype(F32)

        takes[2 + 2 * l].wait()
        for c in range(6):
            qkv[l, :, c * 128 : c * 128 + 128] = block(c % 2 * 3 + c // 2)
        give(qkv.at[l], o_qkv.at[l])
        takes[3 + 2 * l].wait()
        for c in range(2):
            wo[l, :, c * 128 : c * 128 + 128] = block(6 + c)
        give(wo.at[l], o_wo.at[l])
        for c in range(4):
            wu[l, :, c * 128 : c * 128 + 128] = block(8 + c)
        give(wu.at[l], o_wu.at[l])
        for c in range(2):
            wd[l, :, c * 128 : c * 128 + 128] = block(12 + 2 * c, 512)
        give(wd.at[l], o_wd.at[l])
    takes[6].wait()
    give(low, o_lo.at[:, 0])
    takes[1].wait()
    o_mv[...] = small[10:11, :]
    for l in range(LAYERS):

        def row(r, l=l):
            return small[16 * l + r : 16 * l + r + 1, :]

        o_qvb[l, 0:1, :] = row(0)
        o_qvb[l, 1:2, :] = row(1)
        o_bo[l : l + 1, :] = row(2)
        o_gain[l, 0:1, :] = row(3)
        o_gain[l, 1:2, :] = row(4)
        o_bias[l, 0:1, :] = row(5)
        o_bias[l, 1:2, :] = row(6)
        o_bu[l : l + 1, :d] = row(7)
        o_bu[l : l + 1, d:] = row(8)
        o_bd[l : l + 1, :] = row(9)
    for c in gives:
        c.wait()


def shards(sizes, *args):
    (
        tokens, masked, mask_vector, qkv_weight, qv_bias, out_weight, out_bias, norm_gain,
        norm_bias, up_weight, up_bias, down_weight, down_bias, cotangent,
    ) = args
    _, n, d = tokens.shape
    ff = up_weight.shape[2]
    qb = min(512, n)
    rb = min(512, n)
    further = int(math.log2(sizes[0])) - 4
    n_copies = 7 + further
    vmem, hbm = pl.BlockSpec(memory_space=pltpu.VMEM), pl.BlockSpec(memory_space=pl.ANY)

    def room(rows, big):
        sent = rows // 2 + 3 * (rows // 8)
        return sent + (3 * (rows // 32) + further * (rows // 32) if big else (3 + further) * (rows // 8))

    V = pltpu.VMEM
    dma = pltpu.SemaphoreType.DMA

    scratch = [
        *[V(w.shape, BF) for w in (qkv_weight, out_weight, up_weight, down_weight)],
        V((1, n), jnp.int32), V((n, d), BF), V((LAYERS + 1, n, d), BF), V((n, d), F32),
        V((LAYERS, n, d), BF), V((LAYERS, 2, n, d), BF), V((LAYERS, 2, 2, n, 256), BF),
        V((LAYERS, n, d), F32), V((LAYERS, 2, n, d), F32),
        V((n, d), F32), V((n, d), F32), V((n, 2), F32),
        V((n, d), BF), V((n, ff), BF), V((n, ff), BF),
        V((rb, d), BF), V((rb, 2), F32),
        V((2, 2, n, 256), BF), V((2, 128, n), BF), V((d, n), BF),
        V((2 * d, n), F32), V((2 * d, n), BF), V((LAYERS, 2 * d, n), BF),
        V((LAYERS, 4096, 128), F32), V((32, d), F32), V((2 * n_copies, 32, d), F32),
        V((2, n // qb, 4, qb, n), BF),
        V((room(2560, True), 128), BF), V((room(768, False), 128), BF), V((room(768, False), 128), BF),
        V((room(2560, True), 128), BF),
        V((LAYERS, room(768, False), 128), BF), V((LAYERS, room(768, False), 128), BF),
        dma((5 + n // rb,)), dma((5 + n // rb,)), dma((LAYERS, 2)), dma((LAYERS, 2)), dma((LAYERS, 2)), dma((LAYERS, 2)),
        dma((6,)), dma((4,)),
        dma((6, 14 + further)), dma((6, 14 + further)), dma((n_copies,)), dma((n_copies,)),
        dma((5,)),
    ]
    lo, tg, red, small, _ = pl.pallas_call(
        functools.partial(main_kernel, sizes, qb, rb),
        out_shape=(
            jax.ShapeDtypeStruct((LAYERS, n, d), BF),
            jax.ShapeDtypeStruct((n, d), BF),
            jax.ShapeDtypeStruct((LAYERS, 4096, 128), BF),
            jax.ShapeDtypeStruct((32, d), F32),
            jax.ShapeDtypeStruct((2, n // qb, 4, qb, n), BF),
        ),
        in_specs=[hbm, *[vmem] * 2, hbm, vmem, hbm, *[vmem] * 3, hbm, vmem, hbm, vmem, hbm],
        out_specs=(hbm, hbm, vmem, vmem, hbm),
        scratch_shapes=scratch,
        compiler_params=pltpu.CompilerParams(
            collective_id=0, has_side_effects=True, vmem_limit_bytes=63 << 20
        ),
        name="encoder",
    )(
        tokens[0], masked, mask_vector, qkv_weight, qv_bias, out_weight, out_bias,
        norm_gain, norm_bias, up_weight, up_bias, down_weight, down_bias, cotangent[0],
    )

    def f32(*shape):
        return jax.ShapeDtypeStruct(shape, F32)

    outs = pl.pallas_call(
        spread_kernel,
        out_shape=(
            jax.ShapeDtypeStruct((LAYERS, 1, n, d), BF),
            f32(1, n, d), f32(1, d), f32(LAYERS, d, 3 * d), f32(LAYERS, 2, d), f32(LAYERS, d, d),
            f32(LAYERS, d), f32(LAYERS, 2, d), f32(LAYERS, 2, d), f32(LAYERS, d, ff), f32(LAYERS, ff),
            f32(LAYERS, ff, d), f32(LAYERS, d),
        ),
        in_specs=[hbm, hbm, hbm, hbm, vmem],
        out_specs=(hbm, hbm, vmem, hbm, vmem, hbm, *[vmem] * 3, hbm, vmem, hbm, vmem),
        scratch_shapes=[
            V((n, d), BF), V((LAYERS, 4096, 128), BF), V((32, d), F32), V((n, d), F32),
            V((LAYERS, d, 3 * d), F32), V((LAYERS, d, d), F32), V((LAYERS, d, ff), F32),
            V((LAYERS, ff, d), F32), V((LAYERS, n, d), BF), dma((17,)),
        ],
        compiler_params=pltpu.CompilerParams(vmem_limit_bytes=63 << 20),
        name="spread",
    )(lo, tg, red, small, masked)
    return (*outs[:2], outs[2][0], *outs[3:])


def solution(mesh):
    rows = P("dp", "seq", None)
    in_specs = (rows, P("dp", "seq"), *[P()] * 11, rows)
    out_specs = (P(None, "dp", "seq", None), rows, *[P()] * 11)
    sizes = (mesh.shape["dp"], mesh.shape["seq"])
    return jax.shard_map(
        functools.partial(shards, sizes), mesh=mesh, in_specs=in_specs, out_specs=out_specs, check_vma=False
    )
```

```python
import functools
import math

import jax
import jax.numpy as jnp
from jax import lax
from jax.experimental import pallas as pl
from jax.experimental.pallas import tpu as pltpu
from jax.sharding import PartitionSpec as P

LAYERS = 2
HEAD = 64
BF = jnp.bfloat16
F32 = jnp.float32
MESH = pl.DeviceIdType.MESH
LOG2E = 1.4426950408889634
LN2 = 0.6931471805599453
EPS = 1e-05


def dot_nt(a, b):
    return lax.dot_general(a, b, (((1,), (1,)), ((), ())), preferred_element_type=F32)


def dot_nn(a, b):
    return lax.dot_general(a, b, (((1,), (0,)), ((), ())), preferred_element_type=F32)


def dot_tn(a, b):
    return lax.dot_general(a, b, (((0,), (0,)), ((), ())), preferred_element_type=F32)


def head_lanes(h, width):
    lanes = lax.broadcasted_iota(jnp.int32, (1, width), 1) % 128
    return (lanes < 64) if h % 2 == 0 else (lanes >= 64)


def row_sum(x):
    return jnp.sum(x, axis=0, keepdims=True)


def norm(r):
    c = r - jnp.mean(r, axis=1, keepdims=True)
    rs = lax.rsqrt(jnp.mean(c * c, axis=1, keepdims=True) + EPS)
    return c * rs, rs


def norm_back(t, xhat, rs):
    return rs * (
        t - jnp.mean(t, axis=1, keepdims=True) - xhat * jnp.mean(t * xhat, axis=1, keepdims=True)
    )


def flips(mask, count):
    return [i for i in range(count) if mask >> i & 1]


class Reduction:
    def __init__(self, acc, out, sbuf, rbuf, send, recv, layer, lo, rows, rounds, ticks, so, finish):
        self.acc, self.out, self.sbuf, self.rbuf = acc, out, sbuf, rbuf
        self.so, self.finish = so, finish
        self.back_ticks = ticks[len(rounds) :]
        self.send, self.recv = send, recv
        self.layer, self.lo, self.rows, self.rounds, self.ticks = layer, lo, rows, rounds, ticks
        self.sems = 0

    def copy(self, src, dst, peer):
        k = self.sems
        self.sems += 1
        return pltpu.make_async_remote_copy(
            src_ref=src,
            dst_ref=dst,
            send_sem=self.send.at[k],
            recv_sem=self.recv.at[k],
            device_id=peer,
            device_id_type=MESH,
        )

    def steps(self):
        acc, out = self.acc.at[self.layer], self.out.at[self.layer]
        base, size, so = self.lo, self.rows, self.so
        bases = []
        for (split, values, peers), wait in zip(self.rounds, self.ticks):
            bases.append((base, size))
            count = len(values)
            part = size >> count if split else size
            copies, places = [], []
            for mask in range(1, 1 << count):
                give = base
                if split:
                    for i, v in enumerate(values):
                        give = give + (1 - v if mask >> i & 1 else v) * ((part << i))
                    give = pl.multiple_of(give, 16)
                place = pl.ds(so, part)
                so += part
                self.sbuf[place, :] = acc[pl.ds(give, part), :].astype(BF)
                c = self.copy(self.sbuf.at[place], self.rbuf.at[place], peers[mask])
                c.start()
                copies.append(c)
                places.append(place)
            if split:
                for i, v in enumerate(values):
                    base = base + v * (part << i)
                base = pl.multiple_of(base, 16)
                size = part
            for _ in range(wait):
                yield
            for c in copies:
                c.wait()
            mine = pl.ds(base, size)
            got = [self.rbuf[place, :].astype(F32) for place in places]
            held = acc[mine, :]
            if not split:
                held = held.astype(BF).astype(F32)
            if count == 1:
                acc[mine, :] = held + got[0]
            else:
                acc[mine, :] = (held + got[0]) + (got[1] + got[2])
        mine = pl.ds(base, size)
        out[mine, :] = acc[mine, :].astype(BF)
        back = [(r, b) for r, b in zip(self.rounds, bases) if r[0]]
        for ((_, values, peers), (up_base, up_size)), wait in zip(reversed(back), self.back_ticks):
            here = out.at[pl.ds(base, size)]
            copies = [self.copy(here, here, peers[m]) for m in range(1, 1 << len(values))]
            for c in copies:
                c.start()
            for _ in range(wait):
                yield
            for c in copies:
                c.wait()
            base, size = up_base, up_size
        self.finish()


def drain(*generators):
    live = list(generators)
    while live:
        live = [g for g in live if next(g, "end") != "end"]


def advance(queue):
    queue[:] = [g for g in queue if next(g, "end") != "end"]


def launch(queue, group, ahead=False):
    next(group)
    queue.insert(0 if ahead else len(queue), group)


def main_kernel(sizes, qb_rows, rb_rows, *refs):
    (
        tok, msk, mv_in, wqkv_in, qvb_in, wo_in, bo_in, gains_in, biases_in, wu_in, bu_in, wd_in, bd_in, cot,
        lo, tg, red_out, small, saved,
        mv, wqkv, qvb, wo, bo, gains, biases, wu, bu, wd, bd, red,
        mskin, cotin, hb, dr, qs, kk, vx, oo, ff_,
        x1, x2, rss, n1s, gs, gps, n1_last, rs_last,
        dox, dot_t, q_t, dkv, skv, rkv, acc, sm, rsm, probs,
        sb_e, sb_q, rb_e, rb_q,
        swap_send, swap_recv, kv_send, kv_recv, g_send, g_recv, p_sem, lo_sem,
        red_send, red_recv, red_done, sm_send, sm_recv, load_sem,
    ) = refs
    dp_size, seq_size = sizes
    n, d = tok.shape
    n_qb, n_rb = n // qb_rows, n // rb_rows
    d_i, s_i = lax.axis_index("dp"), lax.axis_index("seq")
    core = d_i % 2
    mate = (d_i + 1 - 2 * core, s_i)
    cross = (d_i + 1 - 2 * core, 1 - s_i)
    swaps = core != s_i
    stays = core == s_i
    apart = (core + s_i) % 2

    def place_bit(axis, b):
        return (axis, b, ((d_i if axis == "dp" else s_i) // b) % 2)

    def make_round(split, *placed):
        peers = [None]
        for mask in range(1, 1 << len(placed)):
            spot = {"dp": d_i, "seq": s_i}
            for i in flips(mask, len(placed)):
                axis, b, v = placed[i]
                spot[axis] = spot[axis] + b - 2 * b * v
            peers.append((spot["dp"], spot["seq"]))
        return (split, [v for _, _, v in placed], peers)

    further = int(math.log2(dp_size)) - 4
    near = [
        make_round(True, place_bit("dp", 1)),
        make_round(True, place_bit("dp", 2), place_bit("seq", 1)),
    ]
    far = [make_round(False, place_bit("dp", 16 << k)) for k in range(further)]
    line = [place_bit("dp", 4), place_bit("dp", 8)]
    rounds_big = [*near, make_round(True, *line), *far]
    rounds_low = [*near, make_round(False, *line), *far]

    barrier = pltpu.get_barrier_semaphore()
    peers = [peer for _, _, group in rounds_big for peer in group[1:]] + [cross]
    for peer in peers:
        pl.semaphore_signal(barrier, inc=1, device_id=peer, device_id_type=MESH)
    loads = [
        pltpu.make_async_copy(src, dst, load_sem.at[i])
        for i, (src, dst) in enumerate(
            (
                (wqkv_in, wqkv), (wo_in, wo), (wu_in, wu), (wd_in, wd), (mv_in, mv), (qvb_in, qvb),
                (bo_in, bo), (gains_in, gains), (biases_in, biases), (bu_in, bu), (bd_in, bd),
            )
        )
    ]
    for c in loads:
        c.start()
    for l in range(LAYERS):
        for half in range(2):
            for pair in range(2):
                vx[l, half, pair, :, 128:] = jnp.ones((n, 128), BF)
    pl.semaphore_wait(barrier, len(peers))

    def remote(src, dst, send, recv, peer):
        return pltpu.make_async_remote_copy(
            src_ref=src, dst_ref=dst, send_sem=send, recv_sem=recv, device_id=peer, device_id_type=MESH
        )

    def swap(i, src, dst):
        return remote(src, dst, swap_send.at[i], swap_recv.at[i], cross)

    def part(rb):
        return pl.ds(rb * rb_rows, rb_rows)

    arrive_mask = swap(0, msk, mskin)
    arrive_cot = swap(1, cot, cotin)
    arrive = [swap(5 + rb, tok.at[part(rb)], hb.at[0, part(rb)]) for rb in range(n_rb)]
    here_tok = pltpu.make_async_copy(tok, hb.at[0], load_sem.at[11])
    here_mask = pltpu.make_async_copy(msk, mskin, load_sem.at[12])
    here_cot = pltpu.make_async_copy(cot, cotin, lo_sem.at[3])

    @pl.when(swaps)
    def _():
        arrive_mask.start()
        for c in arrive:
            c.start()

    @pl.when(stays)
    def _():
        here_tok.start()
        here_mask.start()
        here_cot.start()

    first_row = (lax.broadcasted_iota(jnp.int32, (16, d), 0) == 0).astype(F32).astype(BF)

    def mask_rows(rows):
        return jnp.broadcast_to(mskin[:, rows].astype(F32), (16, rows.stop - rows.start)).astype(BF)

    def gain(l, i):
        return gains[l, i : i + 1, :].astype(F32)

    def shift(l, i):
        return biases[l, i : i + 1, :].astype(F32)

    def v_sent():
        return dox.at[1, 0]

    def v_got(l):
        return dox.at[0, l]

    def block_rows(rb):
        return slice(rb * rb_rows, (rb + 1) * rb_rows)

    def embed(rb):
        rows = block_rows(rb)
        is_masked = dot_tn(mask_rows(rows), first_row) > 0.5
        x = jnp.where(is_masked, mv[...].astype(F32).reshape(1, d), hb[0, rows, :].astype(F32))
        hb[0, rows, :] = x.astype(BF)

    def project(l, rb):
        rows = block_rows(rb)
        x = hb[l, rows, :]
        q = dot_nn(x, wqkv[l, :, :d]) + qvb[l, 0:1, :].astype(F32)
        qs[l, rows, :] = (q * (LOG2E * HEAD**-0.5)).astype(BF)
        kk[l, 0, rows, :] = dot_nn(x, wqkv[l, :, d : 2 * d]).astype(BF)
        v = (dot_nn(x, wqkv[l, :, 2 * d :]) + qvb[l, 1:2, :].astype(F32)).astype(BF)
        v_sent()[rows, :] = v
        vx[l, 0, 0, rows, :128] = v[:, :128]
        vx[l, 0, 1, rows, :128] = v[:, 128:]

    def kv_copies(l):
        return [
            remote(kk.at[l, 0], kk.at[l, 1], kv_send.at[l, 0], kv_recv.at[l, 0], mate),
            remote(v_sent(), v_got(l), kv_send.at[l, 1], kv_recv.at[l, 1], mate),
        ]

    def send_kv(l):
        for c in kv_copies(l):
            c.start()

    def take_kv(l):
        for c in kv_copies(l):
            c.wait_recv()
        vx[l, 1, 0, :, :128] = v_got(l)[:, :128]
        vx[l, 1, 1, :, :128] = v_got(l)[:, 128:]

    def attend(l, half, qb, before):
        rows = slice(qb * qb_rows, (qb + 1) * qb_rows)

        def scores(h):
            c = slice(h // 2 * 128, h // 2 * 128 + 128)
            qm = jnp.where(head_lanes(h, 128), qs[l, rows, c], jnp.zeros((), BF))
            return dot_nt(qm, kk[l, half, :, c])

        kept = [None, None]
        s = scores(0)
        for h in range(4):
            top = jnp.max(s, axis=1, keepdims=True)
            following = scores(h + 1) if h < 3 else None
            e = jnp.exp2(s - top).astype(BF)
            probs[half, qb, h] = e
            r = dot_nn(e, vx[l, half, h // 2])
            s = following
            kept[h % 2] = (r[:, :128], r[:, 128:], top)
            if h % 2 == 1:
                left = head_lanes(0, 128)
                c = slice(h // 2 * 128, h // 2 * 128 + 128)
                o, total, top = (jnp.where(left, kept[0][i], kept[1][i]) for i in range(3))
                if before is None:
                    oo[l, rows, c] = o
                    ff_[l, 0, rows, c] = total
                    ff_[l, 1, rows, c] = top
                else:
                    total0, top0 = ff_[l, 0, rows, c], ff_[l, 1, rows, c]
                    both = jnp.maximum(top0, top)
                    a0, a1 = jnp.exp2(top0 - both), jnp.exp2(top - both)
                    inv = 1.0 / (total0 * a0 + total * a1)
                    ff_[l, before, rows, c] = a0 * inv
                    ff_[l, half, rows, c] = a1 * inv
                    oo[l, rows, c] = oo[l, rows, c] * (a0 * inv) + o * (a1 * inv)

    def dense_forward(l, rows, keep, krows):
        kx1, kx2, kr, kn1, kg, kgp = keep
        y = dot_nn(oo[l, rows, :].astype(BF), wo[l]) + bo[l : l + 1, :].astype(F32)
        h_in = hb[0, rows, :].astype(F32) if l == 0 else dr[rows, :]
        xh, rs = norm(h_in + y)
        kx1[krows, :] = xh.astype(kx1.dtype)
        kr[krows, 0:1] = rs
        n1 = xh * gain(l, 0) + shift(l, 0)
        n1b = n1.astype(BF)
        kn1[krows, :] = n1b
        u = dot_nn(n1b, wu[l]) + bu[l : l + 1, :].astype(F32)
        c0 = math.sqrt(2.0 / math.pi)
        u2 = u * u
        t = jnp.tanh(c0 * u * (1.0 + 0.044715 * u2))
        g = (0.5 * u * (1.0 + t)).astype(BF)
        kg[krows, :] = g
        kgp[krows, :] = (
            0.5 * (1.0 + t) + 0.5 * u * (1.0 - t * t) * (c0 * (1.0 + 3 * 0.044715 * u2))
        ).astype(BF)
        z, rs2 = norm(n1 + dot_nn(g, wd[l]) + bd[l : l + 1, :].astype(F32))
        kx2[krows, :] = z.astype(kx2.dtype)
        kr[krows, 1:2] = rs2
        h_out = z * gain(l, 1) + shift(l, 1)
        hb[l + 1, rows, :] = h_out.astype(BF)
        if l + 1 < LAYERS:
            dr[rows, :] = h_out

    def put(l, lo_row, value, first):
        span = slice(lo_row, lo_row + value.shape[0])
        acc[l, span, :] = value if first else acc[l, span, :] + value

    def put_small(l, row, value, first, c=slice(None)):
        span = slice(16 * l + row, 16 * l + row + 1)
        sm[span, c] = value if first else sm[span, c] + value

    same_head = (
        lax.broadcasted_iota(jnp.int32, (d, d), 0) // HEAD
        == lax.broadcasted_iota(jnp.int32, (d, d), 1) // HEAD
    ).astype(F32).astype(BF)

    def dense_backward(l, rows, g, keep, krows, first):
        kx1, kx2, kr, kn1, kg, kgp = keep
        xh = kx2[krows, :].astype(F32)
        put_small(l, 4, row_sum(g * xh), first)
        put_small(l, 6, row_sum(g), first)
        dr2 = norm_back(g * gain(l, 1), xh, kr[krows, 1:2])
        df = dr2.astype(BF)
        put_small(l, 9, row_sum(df.astype(F32)), first)
        wgrad = dot_tn(kg[krows, :], df)
        for c in range(2):
            put(l, (12 + 2 * c) * 256, wgrad[:, c * 128 : c * 128 + 128], first)
        du = (kgp[krows, :].astype(F32) * dot_nt(df, wd[l])).astype(BF)
        dub = row_sum(du.astype(F32))
        put_small(l, 7, dub[:, :d], first)
        put_small(l, 8, dub[:, d:], first)
        wgrad = dot_tn(kn1[krows, :], du)
        for c in range(4):
            put(l, (8 + c) * 256, wgrad[:, c * 128 : c * 128 + 128], first)
        dn1 = dr2 + dot_nt(du, wu[l])
        xh = kx1[krows, :].astype(F32)
        put_small(l, 3, row_sum(dn1 * xh), first)
        put_small(l, 5, row_sum(dn1), first)
        dr1 = norm_back(dn1 * gain(l, 0), xh, kr[krows, 0:1])
        dr[rows, :] = dr1
        dy = dr1.astype(BF)
        put_small(l, 2, row_sum(dy.astype(F32)), first)
        o = oo[l, rows, :]
        wgrad = dot_tn(o.astype(BF), dy)
        for c in range(2):
            put(l, (6 + c) * 256, wgrad[:, c * 128 : c * 128 + 128], first)
        do = dot_nt(dy, wo[l])
        x = do * o
        hi = x.astype(BF)
        lo_part = (x - hi.astype(F32)).astype(BF)
        delta = dot_nn(hi, same_head) + dot_nn(lo_part, same_head)
        lane = lax.broadcasted_iota(jnp.int32, (1, d), 1) % HEAD
        for half in range(2):
            f = ff_[l, half, rows, :]
            dob = (do * f).astype(BF)
            x = -(delta * f)
            hi = x.astype(BF)
            lo_part = (x - hi.astype(F32)).astype(BF)
            extra = jnp.where(lane == 0, hi, jnp.where(lane == 1, lo_part, jnp.zeros((), BF)))
            for pair in range(2):
                c = slice(pair * 128, pair * 128 + 128)
                dox[half, pair, rows, :128] = dob[:, c]
                dox[half, pair, rows, 128:] = extra[:, c]

    dq = ff_.at[1, 0]

    def attend_back(l, pair, half, ticks):
        c = slice(pair * 128, pair * 128 + 128)
        dot_t[half] = dox[half, pair, :, :128].T
        work = [(qb, side) for qb in range(n_qb) for side in range(2)]

        def rows_of(qb):
            return slice(qb * qb_rows, (qb + 1) * qb_rows)

        def prob_grad(qb, side):
            x = jnp.where(head_lanes(side, 256), dox[half, pair, rows_of(qb), :], jnp.zeros((), BF))
            return dot_nt(x, vx[l, half, pair])

        kept = [None, None]
        dp = prob_grad(*work[0])
        for i, (qb, side) in enumerate(work):
            rows = rows_of(qb)
            hr = slice(side * HEAD, (side + 1) * HEAD)
            krw = slice(pair * d + side * HEAD, pair * d + (side + 1) * HEAD)
            vrw = slice(pair * d + 128 + side * HEAD, pair * d + 128 + (side + 1) * HEAD)
            e = probs[half, qb, 2 * pair + side]
            dv = dot_nn(dot_t[half, hr, rows], e)
            dpn = prob_grad(*work[i + 1]) if i + 1 < len(work) else None
            ds = (e.astype(F32) * dp).astype(BF)
            dk = dot_nn(q_t[pair * 128 + side * HEAD : pair * 128 + (side + 1) * HEAD, rows], ds)
            if qb == 0:
                dkv[vrw, :] = dv
                dkv[krw, :] = dk
            else:
                dkv[vrw, :] += dv
                dkv[krw, :] += dk
            kept[side] = dot_nn(ds, kk[l, half, :, c])
            dp = dpn
            if side == 1:
                value = jnp.where(head_lanes(0, 128), kept[0], kept[1])
                dq[rows, c] = value if half == 1 else dq[rows, c] + value
                ticks()

    def pair_rows(pair):
        return slice(pair * d, (pair + 1) * d)

    def back_copy(l, pair):
        span = pl.ds(pair * d, d)
        return remote(skv.at[span], rkv.at[l, span], g_send.at[l, pair], g_recv.at[l, pair], mate)

    def send_back(l, pair):
        if l == 0:
            back_copy(1, pair).wait_send()
        r = pair * d
        skv[r : r + 128, :] = (dkv[r : r + 128, :] * LN2).astype(BF)
        skv[r + 128 : r + d, :] = dkv[r + 128 : r + d, :].astype(BF)
        back_copy(l, pair).start()

    def post(l, pair):
        r = pair * d
        c = slice(pair * 128, pair * 128 + 128)
        dqb = (dq[:, c] * HEAD**-0.5).astype(BF)
        back_copy(l, pair).wait_recv()
        dkb = (dkv[r : r + 128, :] * LN2 + rkv[l, r : r + 128, :].astype(F32)).astype(BF).T
        dvb = (dkv[r + 128 : r + d, :] + rkv[l, r + 128 : r + d, :].astype(F32)).astype(BF).T
        dqk = jnp.concatenate([dqb, dkb], axis=1)
        x = hb[l]
        wgrad = dot_tn(x, dqk)
        put(l, pair * 768, wgrad[:, :128], True)
        put(l, pair * 768 + 256, wgrad[:, 128:], True)
        put(l, pair * 768 + 512, dot_tn(x, dvb), True)
        put_small(l, 0, row_sum(dqb.astype(F32)), True, c)
        put_small(l, 1, row_sum(dvb.astype(F32)), True, c)
        dox[0, pair] = dqk
        dox[1, pair, :, :128] = dvb

    def input_grad(l):
        total = dr[...]
        for pair in range(2):
            c = slice(pair * 128, pair * 128 + 128)
            w = jnp.concatenate([wqkv[l, :, c], wqkv[l, :, d + c.start : d + c.stop]], axis=1)
            total = total + dot_nt(dox[0, pair], w)
        dv = jnp.concatenate([dox[1, 0, :, :128], dox[1, 1, :, :128]], axis=1)
        return total + dot_nt(dv, wqkv[l, :, 2 * d :])

    keep0 = (x1, x2, rss, n1s, gs, gps)
    f = wu.shape[2]
    keep1 = (
        dkv.at[:, 0:d], dkv.at[:, d : 2 * d], rs_last, n1_last,
        skv.at[:, 0:f], skv.at[:, f : 2 * f],
    )

    def deliver(l):
        c = swap(2 + l, hb.at[l + 1], lo.at[l])
        here = pltpu.make_async_copy(hb.at[l + 1], lo.at[l], lo_sem.at[l])

        @pl.when(swaps)
        def _():
            c.start()

        @pl.when(stays)
        def _():
            here.start()

        return c, here

    finished = []

    def reduction(l, lo_row, rows, big, sbuf, rbuf, so, ticks, back_ticks):
        i = len(groups)
        span = pl.ds(lo_row, rows)
        c = pltpu.make_async_copy(red.at[l, span], red_out.at[l, span], red_done.at[i])

        def finish():
            c.start()
            finished.append(c)

        return Reduction(
            acc, red, sbuf, rbuf, red_send.at[i], red_recv.at[i], l, lo_row, rows,
            rounds_big if big else rounds_low, ticks + (2,) * further + back_ticks, so, finish,
        ).steps()

    groups = {}
    groups[1, "dense"] = reduction(1, 1536, 2560, True, sb_e, rb_e.at[1], 0, (1, 4, 2), (2, 4, 1))
    groups[1, "qkv"] = reduction(1, 0, 1536, True, sb_q, rb_q.at[1], 0, (1, 2, 2), (2, 3, 1))
    groups[0, "dense"] = reduction(0, 1536, 2560, True, sb_e, rb_e.at[0], 0, (1, 4, 3), (2, 3, 1))
    groups[0, 0] = reduction(0, 0, 768, False, sb_q, rb_q.at[0], 0, (1, 2, 2), (2, 1))
    groups[0, 1] = reduction(0, 768, 768, False, sb_q, rb_q.at[0], rb_q.shape[1] // 2, (1, 1, 1), (1, 1))

    @pl.when(swaps)
    def _():
        arrive_mask.wait()
        arrive[0].wait()

    @pl.when(stays)
    def _():
        here_tok.wait()
        here_mask.wait()

    for c in loads:
        c.wait()
    embed(0)
    project(0, 0)

    @pl.when(stays)
    def _():
        for rb in range(1, n_rb):
            embed(rb)
            project(0, rb)
        send_kv(0)

    @pl.when(swaps)
    def _():
        take_kv(0)

    attend(0, apart, 0, None)

    @pl.when(swaps)
    def _():
        for rb in range(1, n_rb):
            arrive[rb].wait()
            embed(rb)
            project(0, rb)
        send_kv(0)
        arrive_cot.start()

    for qb in range(1, n_qb):
        attend(0, apart, qb, None)
    keep_probs = [
        pltpu.make_async_copy(probs.at[half], saved.at[half], p_sem.at[i])
        for i, half in enumerate((apart, 1 - apart))
    ]
    keep_probs[0].start()

    @pl.when(stays)
    def _():
        take_kv(0)

    for qb in range(n_qb):
        attend(0, 1 - apart, qb, apart)
    keep_probs[1].start()
    for c in kv_copies(0):
        c.wait_send()
    for rb in range(n_rb):
        rows = block_rows(rb)
        dense_forward(0, rows, keep0, rows)
        project(1, rb)
    send_kv(1)
    results = [deliver(0)]
    for c in keep_probs:
        c.wait()
    for qb in range(n_qb):
        attend(1, 0, qb, None)
    take_kv(1)
    for qb in range(n_qb):
        attend(1, 1, qb, 0)
    for c in kv_copies(1):
        c.wait_send()

    @pl.when(swaps)
    def _():
        arrive_cot.wait()

    @pl.when(stays)
    def _():
        here_cot.wait()

    own = slice(0, rb_rows)
    for rb in range(n_rb):
        rows = block_rows(rb)
        dense_forward(1, rows, keep1, own)
        dense_backward(1, rows, cotin[rows, :].astype(F32), keep1, own, rb == 0)

    def fetch(pair, half):
        heads = pl.ds(2 * pair, 2)
        return pltpu.make_async_copy(
            saved.at[half, :, heads], probs.at[half, :, heads], p_sem.at[2 + 2 * pair + half]
        )

    queue = []
    tick = functools.partial(advance, queue)
    for l in reversed(range(LAYERS)):
        if l == 0:
            for rb in range(n_rb):
                rows = block_rows(rb)
                dense_backward(0, rows, dr[rows, :], keep0, rows, rb == 0)
                tick()
        launch(queue, groups[l, "dense"])
        q_t[...] = qs[l].T
        for pair in range(2):
            for half in (1, 0):
                if l == 0:
                    fetch(pair, half).wait()
                attend_back(l, pair, half, tick)
                if l == 1:
                    fetch(pair, half).start()
                if half == 1:
                    send_back(l, pair)
            post(l, pair)
            tick()
            if l == 0:
                launch(queue, groups[0, pair], pair == 1)
            elif pair == 0:
                results.append(deliver(1))
        if l == 1:
            launch(queue, groups[1, "qkv"])
            dr[...] = input_grad(1)
            tick()

    dh = input_grad(0)
    hi = dh.astype(BF)
    cotin[...] = hi
    lo_part = (dh - hi.astype(F32)).astype(BF)
    masks = mask_rows(slice(0, n))
    sm[10:11, :] = (dot_nn(masks, hi) + dot_nn(masks, lo_part))[0:1, :]
    sm[11:16, :] = jnp.zeros((5, d), F32)
    sm[26:32, :] = jnp.zeros((6, d), F32)

    def small_steps():
        k = 0
        for _, values, peers in rounds_big:
            rsm[2 * k] = sm[...]
            copies = []
            for m in range(1, 1 << len(values)):
                c = remote(rsm.at[2 * k], rsm.at[2 * (k + m) - 1], sm_send.at[k + m - 1], sm_recv.at[k + m - 1], peers[m])
                c.start()
                copies.append(c)
            yield
            for c in copies:
                c.wait()
            if len(values) == 1:
                sm[...] += rsm[2 * k + 1]
            else:
                sm[...] = (sm[...] + rsm[2 * k + 1]) + (rsm[2 * k + 3] + rsm[2 * k + 5])
            k += (1 << len(values)) - 1

    launch(queue, small_steps())
    tick()
    tick()
    gone = swap(4, cotin, tg)
    kept_here = pltpu.make_async_copy(cotin, tg, lo_sem.at[2])

    @pl.when(swaps)
    def _():
        gone.start()

    @pl.when(stays)
    def _():
        kept_here.start()

    drain(*queue)
    out = pltpu.make_async_copy(sm, small, lo_sem.at[4])
    out.start()
    for pair in range(2):
        back_copy(0, pair).wait_send()

    for c in finished:
        c.wait()
    out.wait()

    @pl.when(swaps)
    def _():
        for c, _ in results:
            c.wait()
        gone.wait()

    @pl.when(stays)
    def _():
        for _, here in results:
            here.wait()
        kept_here.wait()


def spread_kernel(
    lo_in, tg_in, red_in, small_in, msk_in,
    o_lo, o_tg, o_mv, o_qkv, o_qvb, o_wo, o_bo, o_gain, o_bias, o_wu, o_bu, o_wd, o_bd,
    lo, tg, red, small, msk, tgf, qkv, wo, wu, wd, mv, qvb, bo, gain, bias, bu, bd, sem,
):
    early, late = pl.ds(1536, 2560), pl.ds(0, 1536)
    order = [(1, early), (1, late), (0, early), (0, late)]
    pairs = [(red_in.at[l, r], red.at[l, r]) for l, r in order]
    pairs += [(msk_in, msk), (tg_in, tg), (small_in, small), (lo_in, lo)]
    takes = [pltpu.make_async_copy(a, b, sem.at[i]) for i, (a, b) in enumerate(pairs)]
    for c in takes:
        c.start()
    gives = []

    def give(a, b):
        c = pltpu.make_async_copy(a, b, sem.at[len(takes) + len(gives)])
        c.start()
        gives.append(c)

    n, d = tg.shape
    for i, (l, r) in enumerate(order):

        def block(b, rows=256, l=l):
            return red[l, b * 256 : b * 256 + rows, :].astype(F32)

        takes[i].wait()
        if r is early:
            for c in range(2):
                wd[l, :, c * 128 : c * 128 + 128] = block(12 + 2 * c, 512)
            give(wd.at[l], o_wd.at[l])
            for c in range(4):
                wu[l, :, c * 128 : c * 128 + 128] = block(8 + c)
            give(wu.at[l], o_wu.at[l])
            for c in range(2):
                wo[l, :, c * 128 : c * 128 + 128] = block(6 + c)
            give(wo.at[l], o_wo.at[l])
        else:
            for c in range(6):
                qkv[l, :, c * 128 : c * 128 + 128] = block(c % 2 * 3 + c // 2)
            give(qkv.at[l], o_qkv.at[l])
    takes[4].wait()
    takes[5].wait()
    mask_rows = jnp.broadcast_to(msk[...].astype(F32), (16, n)).astype(BF)
    first_row = (lax.broadcasted_iota(jnp.int32, (16, d), 0) == 0).astype(F32).astype(BF)
    is_masked = dot_tn(mask_rows, first_row) > 0.5
    tgf[...] = jnp.where(is_masked, 0.0, tg[...].astype(F32))
    give(tgf, o_tg.at[0])
    takes[6].wait()
    mv[...] = small[10:11, :]
    for l in range(LAYERS):

        def row(r, l=l):
            return small[16 * l + r : 16 * l + r + 1, :]

        qvb[l, 0:1, :] = row(0)
        qvb[l, 1:2, :] = row(1)
        bo[l : l + 1, :] = row(2)
        gain[l, 0:1, :] = row(3)
        gain[l, 1:2, :] = row(4)
        bias[l, 0:1, :] = row(5)
        bias[l, 1:2, :] = row(6)
        bu[l : l + 1, :d] = row(7)
        bu[l : l + 1, d:] = row(8)
        bd[l : l + 1, :] = row(9)
    for a, b in ((mv, o_mv), (qvb, o_qvb), (bo, o_bo), (gain, o_gain), (bias, o_bias), (bu, o_bu), (bd, o_bd)):
        give(a, b)
    takes[7].wait()
    give(lo, o_lo.at[:, 0])
    for c in gives:
        c.wait()


def shards(sizes, *args):
    (
        tokens, masked, mask_vector, qkv_weight, qv_bias, out_weight, out_bias, norm_gain,
        norm_bias, up_weight, up_bias, down_weight, down_bias, cotangent,
    ) = args
    _, n, d = tokens.shape
    ff = up_weight.shape[2]
    qb = min(512, n)
    rb = min(512, n)
    further = int(math.log2(sizes[0])) - 4
    n_copies = 7 + further
    hbm = pl.BlockSpec(memory_space=pl.ANY)

    def room(rows, big):
        sent = rows // 2 + 3 * (rows // 8)
        return sent + (3 * (rows // 32) + further * (rows // 32) if big else (3 + further) * (rows // 8))

    V = pltpu.VMEM
    dma = pltpu.SemaphoreType.DMA

    scratch = [
        *[
            V(w.shape, BF)
            for w in (
                mask_vector, qkv_weight, qv_bias, out_weight, out_bias, norm_gain, norm_bias, up_weight,
                up_bias, down_weight, down_bias,
            )
        ],
        V((LAYERS, 4096, 128), BF),
        V((1, n), jnp.int32), V((n, d), BF), V((LAYERS + 1, n, d), BF), V((n, d), F32),
        V((LAYERS, n, d), BF), V((LAYERS, 2, n, d), BF), V((LAYERS, 2, 2, n, 256), BF),
        V((LAYERS, n, d), F32), V((LAYERS, 2, n, d), F32),
        V((n, d), BF), V((n, d), BF), V((n, 2), F32),
        V((n, d), BF), V((n, ff), BF), V((n, ff), BF),
        V((rb, d), BF), V((rb, 2), F32),
        V((2, 2, n, 256), BF), V((2, 128, n), BF), V((d, n), BF),
        V((2 * d, n), F32), V((2 * d, n), BF), V((LAYERS, 2 * d, n), BF),
        V((LAYERS, 4096, 128), F32), V((32, d), F32), V((2 * n_copies, 32, d), F32),
        V((2, n // qb, 4, qb, n), BF),
        V((room(2560, True), 128), BF), V((2 * room(768, False), 128), BF),
        V((LAYERS, room(2560, True), 128), BF), V((LAYERS, 2 * room(768, False), 128), BF),
        dma((5 + n // rb,)), dma((5 + n // rb,)), dma((LAYERS, 2)), dma((LAYERS, 2)), dma((LAYERS, 2)), dma((LAYERS, 2)),
        dma((6,)), dma((5,)),
        dma((5, 14 + further)), dma((5, 14 + further)), dma((5,)), dma((n_copies,)), dma((n_copies,)),
        dma((13,)),
    ]
    lo, tg, red, small, _ = pl.pallas_call(
        functools.partial(main_kernel, sizes, qb, rb),
        out_shape=(
            jax.ShapeDtypeStruct((LAYERS, n, d), BF),
            jax.ShapeDtypeStruct((n, d), BF),
            jax.ShapeDtypeStruct((LAYERS, 4096, 128), BF),
            jax.ShapeDtypeStruct((32, d), F32),
            jax.ShapeDtypeStruct((2, n // qb, 4, qb, n), BF),
        ),
        in_specs=[hbm] * 14,
        out_specs=(hbm,) * 5,
        scratch_shapes=scratch,
        compiler_params=pltpu.CompilerParams(
            collective_id=0, has_side_effects=True, vmem_limit_bytes=63 << 20
        ),
        name="encoder",
    )(
        tokens[0], masked, mask_vector, qkv_weight, qv_bias, out_weight, out_bias,
        norm_gain, norm_bias, up_weight, up_bias, down_weight, down_bias, cotangent[0],
    )

    def f32(*shape):
        return jax.ShapeDtypeStruct(shape, F32)

    grads = (
        f32(1, d), f32(LAYERS, d, 3 * d), f32(LAYERS, 2, d), f32(LAYERS, d, d), f32(LAYERS, d),
        f32(LAYERS, 2, d), f32(LAYERS, 2, d), f32(LAYERS, d, ff), f32(LAYERS, ff),
        f32(LAYERS, ff, d), f32(LAYERS, d),
    )
    order = (1, 3, 7, 9, 0, 2, 4, 5, 6, 8, 10)
    outs = pl.pallas_call(
        spread_kernel,
        out_shape=(jax.ShapeDtypeStruct((LAYERS, 1, n, d), BF), f32(1, n, d), *grads),
        in_specs=[hbm] * 5,
        out_specs=(hbm,) * 13,
        scratch_shapes=[
            V((LAYERS, n, d), BF), V((n, d), BF), V((LAYERS, 4096, 128), BF), V((32, d), F32),
            V((1, n), jnp.int32), V((n, d), F32), *[V(grads[i].shape, F32) for i in order], dma((32,)),
        ],
        compiler_params=pltpu.CompilerParams(vmem_limit_bytes=63 << 20),
        name="spread",
    )(lo, tg, red, small, masked)
    return (*outs[:2], outs[2][0], *outs[3:])


def solution(mesh):
    rows = P("dp", "seq", None)
    in_specs = (rows, P("dp", "seq"), *[P()] * 11, rows)
    out_specs = (P(None, "dp", "seq", None), rows, *[P()] * 11)
    sizes = (mesh.shape["dp"], mesh.shape["seq"])
    return jax.shard_map(
        functools.partial(shards, sizes), mesh=mesh, in_specs=in_specs, out_specs=out_specs, check_vma=False
    )
```

```python
import functools
import math

import jax
import jax.numpy as jnp
from jax import lax
from jax.experimental import pallas as pl
from jax.experimental.pallas import tpu as pltpu
from jax.sharding import PartitionSpec as P

LAYERS = 2
HEAD = 64
BF = jnp.bfloat16
F32 = jnp.float32
MESH = pl.DeviceIdType.MESH
LOG2E = 1.4426950408889634
LN2 = 0.6931471805599453
EPS = 1e-05


def dot_nt(a, b):
    return lax.dot_general(a, b, (((1,), (1,)), ((), ())), preferred_element_type=F32)


def dot_nn(a, b):
    return lax.dot_general(a, b, (((1,), (0,)), ((), ())), preferred_element_type=F32)


def dot_tn(a, b):
    return lax.dot_general(a, b, (((0,), (0,)), ((), ())), preferred_element_type=F32)


def head_lanes(h, width):
    lanes = lax.broadcasted_iota(jnp.int32, (1, width), 1) % 128
    return (lanes < 64) if h % 2 == 0 else (lanes >= 64)


def row_sum(x):
    return jnp.sum(x, axis=0, keepdims=True)


def norm(r):
    c = r - jnp.mean(r, axis=1, keepdims=True)
    rs = lax.rsqrt(jnp.mean(c * c, axis=1, keepdims=True) + EPS)
    return c * rs, rs


def norm_back(t, xhat, rs):
    return rs * (
        t - jnp.mean(t, axis=1, keepdims=True) - xhat * jnp.mean(t * xhat, axis=1, keepdims=True)
    )


def flips(mask, count):
    return [i for i in range(count) if mask >> i & 1]


class Reduction:
    def __init__(self, acc, out, sbuf, rbuf, send, recv, layer, lo, rows, rounds, ticks, so, finish):
        self.acc, self.out, self.sbuf, self.rbuf = acc, out, sbuf, rbuf
        self.so, self.finish = so, finish
        self.back_ticks = ticks[len(rounds) :]
        self.send, self.recv = send, recv
        self.layer, self.lo, self.rows, self.rounds, self.ticks = layer, lo, rows, rounds, ticks
        self.sems = 0

    def copy(self, src, dst, peer):
        k = self.sems
        self.sems += 1
        return pltpu.make_async_remote_copy(
            src_ref=src,
            dst_ref=dst,
            send_sem=self.send.at[k],
            recv_sem=self.recv.at[k],
            device_id=peer,
            device_id_type=MESH,
        )

    def steps(self):
        acc, out = self.acc.at[self.layer], self.out.at[self.layer]
        base, size, so = self.lo, self.rows, self.so
        bases, sent = [], []
        for (split, values, peers), wait in zip(self.rounds, self.ticks):
            bases.append((base, size))
            count = len(values)
            part = size >> count if split else size
            copies, places = [], []
            for mask in range(1, 1 << count):
                give = base
                if split:
                    for i, v in enumerate(values):
                        give = give + (1 - v if mask >> i & 1 else v) * ((part << i))
                    give = pl.multiple_of(give, 16)
                place = pl.ds(so, part)
                so += part
                self.sbuf[place, :] = acc[pl.ds(give, part), :].astype(BF)
                c = self.copy(self.sbuf.at[place], self.rbuf.at[place], peers[mask])
                c.start()
                copies.append(c)
                places.append(place)
            if split:
                for i, v in enumerate(values):
                    base = base + v * (part << i)
                base = pl.multiple_of(base, 16)
                size = part
            for _ in range(wait):
                yield
            for c in copies:
                c.wait_recv()
            sent += copies
            mine = pl.ds(base, size)
            got = [self.rbuf[place, :].astype(F32) for place in places]
            held = acc[mine, :]
            if not split:
                held = held.astype(BF).astype(F32)
            if count == 1:
                acc[mine, :] = held + got[0]
            else:
                acc[mine, :] = (held + got[0]) + (got[1] + got[2])
        mine = pl.ds(base, size)
        out[mine, :] = acc[mine, :].astype(BF)
        for c in sent:
            c.wait_send()
        sent = []
        back = [(r, b) for r, b in zip(self.rounds, bases) if r[0]]
        for ((_, values, peers), (up_base, up_size)), wait in zip(reversed(back), self.back_ticks):
            if isinstance(wait, tuple):
                low = pl.multiple_of(up_base + values[0] * size, 16)
                lines = [pl.ds(pl.multiple_of(low + 2 * v * size, 16), size) for v in range(2)]
                plan = [([pl.ds(base, size)], [2], wait[0]), (lines, [1], wait[1])]
            else:
                plan = [([pl.ds(base, size)], range(1, 1 << len(values)), wait)]
            for places, masks, pause in plan:
                copies = [self.copy(out.at[p], out.at[p], peers[m]) for p in places for m in masks]
                for c in copies:
                    c.start()
                for _ in range(pause):
                    yield
                for c in copies:
                    c.wait_recv()
                sent += copies
            base, size = up_base, up_size
        for c in sent:
            c.wait_send()
        self.finish()


def drain(*generators):
    live = list(generators)
    while live:
        live = [g for g in live if next(g, "end") != "end"]


def advance(queue):
    queue[:] = [g for g in queue if next(g, "end") != "end"]


def launch(queue, group, ahead=False):
    next(group)
    queue.insert(0 if ahead else len(queue), group)


def main_kernel(sizes, qb_rows, rb_rows, *refs):
    (
        tok, msk, mv_in, wqkv_in, qvb_in, wo_in, bo_in, gains_in, biases_in, wu_in, bu_in, wd_in, bd_in, cot,
        lo, tg, red_out, small, saved,
        mv, wqkv, qvb, wo, bo, gains, biases, wu, bu, wd, bd, red,
        mskin, cotin, hb, dr, qs, kk, vx, oo, ff_,
        x1, x2, rss, n1s, gs, gps, n1_last, rs_last,
        dox, dot_t, q_t, dkv, skv, rkv, acc, sm, rsm, probs,
        sb_e, sb_q, rb_e, rb_q,
        swap_send, swap_recv, kv_send, kv_recv, g_send, g_recv, p_sem, lo_sem,
        red_send, red_recv, red_done, sm_send, sm_recv, load_sem,
    ) = refs
    dp_size, seq_size = sizes
    n, d = tok.shape
    n_qb, n_rb = n // qb_rows, n // rb_rows
    d_i, s_i = lax.axis_index("dp"), lax.axis_index("seq")
    core = d_i % 2
    mate = (d_i + 1 - 2 * core, s_i)
    cross = (d_i + 1 - 2 * core, 1 - s_i)
    swaps = core != s_i
    stays = core == s_i
    apart = (core + s_i) % 2

    def place_bit(axis, b):
        return (axis, b, ((d_i if axis == "dp" else s_i) // b) % 2)

    def make_round(split, *placed):
        peers = [None]
        for mask in range(1, 1 << len(placed)):
            spot = {"dp": d_i, "seq": s_i}
            for i in flips(mask, len(placed)):
                axis, b, v = placed[i]
                spot[axis] = spot[axis] + b - 2 * b * v
            peers.append((spot["dp"], spot["seq"]))
        return (split, [v for _, _, v in placed], peers)

    further = int(math.log2(dp_size)) - 4
    near = [
        make_round(True, place_bit("dp", 1)),
        make_round(True, place_bit("dp", 2), place_bit("seq", 1)),
    ]
    far = [make_round(False, place_bit("dp", 16 << k)) for k in range(further)]
    line = [place_bit("dp", 4), place_bit("dp", 8)]
    rounds_big = [*near, make_round(True, *line), *far]
    rounds_low = [*near, make_round(False, *line), *far]

    barrier = pltpu.get_barrier_semaphore()
    peers = [peer for _, _, group in reversed(rounds_big) for peer in group[1:]]
    peers.insert(0, cross)
    for peer in peers:
        pl.semaphore_signal(barrier, inc=1, device_id=peer, device_id_type=MESH)
    loads = [
        pltpu.make_async_copy(src, dst, load_sem.at[i])
        for i, (src, dst) in enumerate(
            (
                (wqkv_in, wqkv), (wo_in, wo), (wu_in, wu), (wd_in, wd), (mv_in, mv), (qvb_in, qvb),
                (bo_in, bo), (gains_in, gains), (biases_in, biases), (bu_in, bu), (bd_in, bd),
            )
        )
    ]
    for c in loads:
        c.start()
    for l in range(LAYERS):
        for half in range(2):
            for pair in range(2):
                vx[l, half, pair, :, 128:] = jnp.ones((n, 128), BF)
    pl.semaphore_wait(barrier, len(peers))

    def remote(src, dst, send, recv, peer):
        return pltpu.make_async_remote_copy(
            src_ref=src, dst_ref=dst, send_sem=send, recv_sem=recv, device_id=peer, device_id_type=MESH
        )

    def swap(i, src, dst):
        return remote(src, dst, swap_send.at[i], swap_recv.at[i], cross)

    def part(rb):
        return pl.ds(rb * rb_rows, rb_rows)

    arrive_mask = swap(0, msk, mskin)
    arrive_cot = swap(1, cot, cotin)
    arrive = [swap(5 + rb, tok.at[part(rb)], hb.at[0, part(rb)]) for rb in range(n_rb)]
    here_tok = pltpu.make_async_copy(tok, hb.at[0], load_sem.at[11])
    here_mask = pltpu.make_async_copy(msk, mskin, load_sem.at[12])
    here_cot = pltpu.make_async_copy(cot, cotin, lo_sem.at[3])

    @pl.when(swaps)
    def _():
        arrive_mask.start()
        for c in arrive:
            c.start()

    @pl.when(stays)
    def _():
        here_tok.start()
        here_mask.start()
        here_cot.start()

    first_row = (lax.broadcasted_iota(jnp.int32, (16, d), 0) == 0).astype(F32).astype(BF)

    def mask_rows(rows):
        return jnp.broadcast_to(mskin[:, rows].astype(F32), (16, rows.stop - rows.start)).astype(BF)

    def gain(l, i):
        return gains[l, i : i + 1, :].astype(F32)

    def shift(l, i):
        return biases[l, i : i + 1, :].astype(F32)

    def v_sent():
        return dox.at[1, 0]

    def v_got(l):
        return dox.at[0, l]

    def block_rows(rb):
        return slice(rb * rb_rows, (rb + 1) * rb_rows)

    def embed(rb):
        rows = block_rows(rb)
        is_masked = dot_tn(mask_rows(rows), first_row) > 0.5
        x = jnp.where(is_masked, mv[...].astype(F32).reshape(1, d), hb[0, rows, :].astype(F32))
        hb[0, rows, :] = x.astype(BF)

    def project(l, rb):
        rows = block_rows(rb)
        x = hb[l, rows, :]
        q = dot_nn(x, wqkv[l, :, :d]) + qvb[l, 0:1, :].astype(F32)
        qs[l, rows, :] = (q * (LOG2E * HEAD**-0.5)).astype(BF)
        kk[l, 0, rows, :] = dot_nn(x, wqkv[l, :, d : 2 * d]).astype(BF)
        v = (dot_nn(x, wqkv[l, :, 2 * d :]) + qvb[l, 1:2, :].astype(F32)).astype(BF)
        v_sent()[rows, :] = v
        vx[l, 0, 0, rows, :128] = v[:, :128]
        vx[l, 0, 1, rows, :128] = v[:, 128:]

    def kv_copies(l):
        return [
            remote(kk.at[l, 0], kk.at[l, 1], kv_send.at[l, 0], kv_recv.at[l, 0], mate),
            remote(v_sent(), v_got(l), kv_send.at[l, 1], kv_recv.at[l, 1], mate),
        ]

    def send_kv(l):
        for c in kv_copies(l):
            c.start()

    def take_kv(l):
        for c in kv_copies(l):
            c.wait_recv()
        vx[l, 1, 0, :, :128] = v_got(l)[:, :128]
        vx[l, 1, 1, :, :128] = v_got(l)[:, 128:]

    def attend(l, half, qb, before):
        rows = slice(qb * qb_rows, (qb + 1) * qb_rows)

        def scores(h):
            c = slice(h // 2 * 128, h // 2 * 128 + 128)
            qm = jnp.where(head_lanes(h, 128), qs[l, rows, c], jnp.zeros((), BF))
            return dot_nt(qm, kk[l, half, :, c])

        kept = [None, None]
        s = scores(0)
        for h in range(4):
            top = jnp.max(s, axis=1, keepdims=True)
            following = scores(h + 1) if h < 3 else None
            e = jnp.exp2(s - top).astype(BF)
            probs[half, qb, h] = e
            r = dot_nn(e, vx[l, half, h // 2])
            s = following
            kept[h % 2] = (r[:, :128], r[:, 128:], top)
            if h % 2 == 1:
                left = head_lanes(0, 128)
                c = slice(h // 2 * 128, h // 2 * 128 + 128)
                o, total, top = (jnp.where(left, kept[0][i], kept[1][i]) for i in range(3))
                if before is None:
                    oo[l, rows, c] = o
                    ff_[l, 0, rows, c] = total
                    ff_[l, 1, rows, c] = top
                else:
                    total0, top0 = ff_[l, 0, rows, c], ff_[l, 1, rows, c]
                    both = jnp.maximum(top0, top)
                    a0, a1 = jnp.exp2(top0 - both), jnp.exp2(top - both)
                    inv = 1.0 / (total0 * a0 + total * a1)
                    ff_[l, before, rows, c] = a0 * inv
                    ff_[l, half, rows, c] = a1 * inv
                    oo[l, rows, c] = oo[l, rows, c] * (a0 * inv) + o * (a1 * inv)

    def dense_forward(l, rows, keep, krows):
        kx1, kx2, kr, kn1, kg, kgp = keep
        y = dot_nn(oo[l, rows, :].astype(BF), wo[l]) + bo[l : l + 1, :].astype(F32)
        h_in = hb[0, rows, :].astype(F32) if l == 0 else dr[rows, :]
        xh, rs = norm(h_in + y)
        kx1[krows, :] = xh.astype(kx1.dtype)
        kr[krows, 0:1] = rs
        n1 = xh * gain(l, 0) + shift(l, 0)
        n1b = n1.astype(BF)
        kn1[krows, :] = n1b
        u = dot_nn(n1b, wu[l]) + bu[l : l + 1, :].astype(F32)
        c0 = math.sqrt(2.0 / math.pi)
        u2 = u * u
        t = jnp.tanh(c0 * u * (1.0 + 0.044715 * u2))
        g = (0.5 * u * (1.0 + t)).astype(BF)
        kg[krows, :] = g
        kgp[krows, :] = (
            0.5 * (1.0 + t) + 0.5 * u * (1.0 - t * t) * (c0 * (1.0 + 3 * 0.044715 * u2))
        ).astype(BF)
        z, rs2 = norm(n1 + dot_nn(g, wd[l]) + bd[l : l + 1, :].astype(F32))
        kx2[krows, :] = z.astype(kx2.dtype)
        kr[krows, 1:2] = rs2
        h_out = z * gain(l, 1) + shift(l, 1)
        hb[l + 1, rows, :] = h_out.astype(BF)
        if l + 1 < LAYERS:
            dr[rows, :] = h_out

    def put(l, lo_row, value, first):
        span = slice(lo_row, lo_row + value.shape[0])
        acc[l, span, :] = value if first else acc[l, span, :] + value

    def put_small(l, row, value, first, c=slice(None)):
        span = slice(16 * l + row, 16 * l + row + 1)
        sm[span, c] = value if first else sm[span, c] + value

    same_head = (
        lax.broadcasted_iota(jnp.int32, (d, d), 0) // HEAD
        == lax.broadcasted_iota(jnp.int32, (d, d), 1) // HEAD
    ).astype(F32).astype(BF)

    def dense_backward(l, rows, g, keep, krows, first):
        kx1, kx2, kr, kn1, kg, kgp = keep
        xh = kx2[krows, :].astype(F32)
        put_small(l, 4, row_sum(g * xh), first)
        put_small(l, 6, row_sum(g), first)
        dr2 = norm_back(g * gain(l, 1), xh, kr[krows, 1:2])
        df = dr2.astype(BF)
        put_small(l, 9, row_sum(df.astype(F32)), first)
        wgrad = dot_tn(kg[krows, :], df)
        for c in range(2):
            put(l, (12 + 2 * c) * 256, wgrad[:, c * 128 : c * 128 + 128], first)
        du = (kgp[krows, :].astype(F32) * dot_nt(df, wd[l])).astype(BF)
        dub = row_sum(du.astype(F32))
        put_small(l, 7, dub[:, :d], first)
        put_small(l, 8, dub[:, d:], first)
        wgrad = dot_tn(kn1[krows, :], du)
        for c in range(4):
            put(l, (8 + c) * 256, wgrad[:, c * 128 : c * 128 + 128], first)
        dn1 = dr2 + dot_nt(du, wu[l])
        xh = kx1[krows, :].astype(F32)
        put_small(l, 3, row_sum(dn1 * xh), first)
        put_small(l, 5, row_sum(dn1), first)
        dr1 = norm_back(dn1 * gain(l, 0), xh, kr[krows, 0:1])
        dr[rows, :] = dr1
        dy = dr1.astype(BF)
        put_small(l, 2, row_sum(dy.astype(F32)), first)
        o = oo[l, rows, :]
        wgrad = dot_tn(o.astype(BF), dy)
        for c in range(2):
            put(l, (6 + c) * 256, wgrad[:, c * 128 : c * 128 + 128], first)
        do = dot_nt(dy, wo[l])
        x = do * o
        hi = x.astype(BF)
        lo_part = (x - hi.astype(F32)).astype(BF)
        delta = dot_nn(hi, same_head) + dot_nn(lo_part, same_head)
        lane = lax.broadcasted_iota(jnp.int32, (1, d), 1) % HEAD
        for half in range(2):
            f = ff_[l, half, rows, :]
            dob = (do * f).astype(BF)
            x = -(delta * f)
            hi = x.astype(BF)
            lo_part = (x - hi.astype(F32)).astype(BF)
            extra = jnp.where(lane == 0, hi, jnp.where(lane == 1, lo_part, jnp.zeros((), BF)))
            for pair in range(2):
                c = slice(pair * 128, pair * 128 + 128)
                dox[half, pair, rows, :128] = dob[:, c]
                dox[half, pair, rows, 128:] = extra[:, c]

    dq = ff_.at[1, 0]

    def attend_back(l, pair, half, ticks):
        c = slice(pair * 128, pair * 128 + 128)
        dot_t[half] = dox[half, pair, :, :128].T
        work = [(qb, side) for qb in range(n_qb) for side in range(2)]

        def rows_of(qb):
            return slice(qb * qb_rows, (qb + 1) * qb_rows)

        def prob_grad(qb, side):
            x = jnp.where(head_lanes(side, 256), dox[half, pair, rows_of(qb), :], jnp.zeros((), BF))
            return dot_nt(x, vx[l, half, pair])

        kept = [None, None]
        dp = prob_grad(*work[0])
        for i, (qb, side) in enumerate(work):
            rows = rows_of(qb)
            hr = slice(side * HEAD, (side + 1) * HEAD)
            krw = slice(pair * d + side * HEAD, pair * d + (side + 1) * HEAD)
            vrw = slice(pair * d + 128 + side * HEAD, pair * d + 128 + (side + 1) * HEAD)
            e = probs[half, qb, 2 * pair + side]
            dv = dot_nn(dot_t[half, hr, rows], e)
            dpn = prob_grad(*work[i + 1]) if i + 1 < len(work) else None
            ds = (e.astype(F32) * dp).astype(BF)
            dk = dot_nn(q_t[pair * 128 + side * HEAD : pair * 128 + (side + 1) * HEAD, rows], ds)
            if qb == 0:
                dkv[vrw, :] = dv
                dkv[krw, :] = dk
            else:
                dkv[vrw, :] += dv
                dkv[krw, :] += dk
            kept[side] = dot_nn(ds, kk[l, half, :, c])
            dp = dpn
            if side == 1:
                value = jnp.where(head_lanes(0, 128), kept[0], kept[1])
                dq[rows, c] = value if half == 1 else dq[rows, c] + value
                ticks()

    def pair_rows(pair):
        return slice(pair * d, (pair + 1) * d)

    def back_copy(l, pair):
        span = pl.ds(pair * d, d)
        return remote(skv.at[span], rkv.at[l, span], g_send.at[l, pair], g_recv.at[l, pair], mate)

    def send_back(l, pair):
        if l == 0:
            back_copy(1, pair).wait_send()
        r = pair * d
        skv[r : r + 128, :] = (dkv[r : r + 128, :] * LN2).astype(BF)
        skv[r + 128 : r + d, :] = dkv[r + 128 : r + d, :].astype(BF)
        back_copy(l, pair).start()

    def post(l, pair):
        r = pair * d
        c = slice(pair * 128, pair * 128 + 128)
        dqb = (dq[:, c] * HEAD**-0.5).astype(BF)
        back_copy(l, pair).wait_recv()
        dkb = (dkv[r : r + 128, :] * LN2 + rkv[l, r : r + 128, :].astype(F32)).astype(BF).T
        dvb = (dkv[r + 128 : r + d, :] + rkv[l, r + 128 : r + d, :].astype(F32)).astype(BF).T
        dqk = jnp.concatenate([dqb, dkb], axis=1)
        x = hb[l]
        wgrad = dot_tn(x, dqk)
        put(l, pair * 768, wgrad[:, :128], True)
        put(l, pair * 768 + 256, wgrad[:, 128:], True)
        put(l, pair * 768 + 512, dot_tn(x, dvb), True)
        put_small(l, 0, row_sum(dqb.astype(F32)), True, c)
        put_small(l, 1, row_sum(dvb.astype(F32)), True, c)
        dox[0, pair] = dqk
        dox[1, pair, :, :128] = dvb

    def input_grad(l):
        total = dr[...]
        for pair in range(2):
            c = slice(pair * 128, pair * 128 + 128)
            w = jnp.concatenate([wqkv[l, :, c], wqkv[l, :, d + c.start : d + c.stop]], axis=1)
            total = total + dot_nt(dox[0, pair], w)
        dv = jnp.concatenate([dox[1, 0, :, :128], dox[1, 1, :, :128]], axis=1)
        return total + dot_nt(dv, wqkv[l, :, 2 * d :])

    keep0 = (x1, x2, rss, n1s, gs, gps)
    f = wu.shape[2]

    def keep1(rb):
        low = skv if rb == 0 else rkv.at[0]
        return (
            dkv.at[:, rb * d : rb * d + d], dkv.at[:, (2 + rb) * d : (3 + rb) * d], rs_last.at[rb],
            n1_last.at[rb], low.at[:, 0:f], low.at[:, f : 2 * f],
        )

    def deliver(l):
        c = swap(2 + l, hb.at[l + 1], lo.at[l])
        here = pltpu.make_async_copy(hb.at[l + 1], lo.at[l], lo_sem.at[l])

        @pl.when(swaps)
        def _():
            c.start()

        @pl.when(stays)
        def _():
            here.start()

        return c, here

    finished = []

    def reduction(l, lo_row, rows, big, sbuf, rbuf, so, ticks, back_ticks):
        i = len(groups)
        span = pl.ds(lo_row, rows)
        c = pltpu.make_async_copy(red.at[l, span], red_out.at[l, span], red_done.at[i])

        def finish():
            c.start()
            finished.append(c)

        return Reduction(
            acc, red, sbuf, rbuf, red_send.at[i], red_recv.at[i], l, lo_row, rows,
            rounds_big if big else rounds_low, ticks + (2,) * further + back_ticks, so, finish,
        ).steps()

    groups = {}
    groups[1, "dense"] = reduction(1, 1536, 2560, True, sb_e, rb_e.at[1], 0, (2, 3, 2), (2, 4, 2))
    groups[1, "qkv"] = reduction(1, 0, 1536, True, sb_q, rb_q.at[1], 0, (1, 4, 3), (2, 2, 1))
    groups[0, "dense"] = reduction(0, 1536, 2560, True, sb_e, rb_e.at[0], 0, (2, 3, 2), (2, 3, 1))
    groups[0, 0] = reduction(0, 0, 768, False, sb_q, rb_q.at[0], 0, (2, 2, 2), (2, 1))
    groups[0, 1] = reduction(0, 768, 768, False, sb_q, rb_q.at[0], rb_q.shape[1] // 2, (1, 1, 1), (1, 1))

    @pl.when(swaps)
    def _():
        arrive_mask.wait()
        arrive[0].wait()

    @pl.when(stays)
    def _():
        here_tok.wait()
        here_mask.wait()

    for c in loads:
        c.wait()
    embed(0)
    project(0, 0)

    @pl.when(stays)
    def _():
        for rb in range(1, n_rb):
            embed(rb)
            project(0, rb)
        send_kv(0)

    @pl.when(swaps)
    def _():
        take_kv(0)

    attend(0, apart, 0, None)

    @pl.when(swaps)
    def _():
        for rb in range(1, n_rb):
            arrive[rb].wait()
            embed(rb)
            project(0, rb)
        send_kv(0)
        arrive_cot.start()

    for qb in range(1, n_qb):
        attend(0, apart, qb, None)
    keep_probs = [
        pltpu.make_async_copy(probs.at[half], saved.at[half], p_sem.at[i])
        for i, half in enumerate((apart, 1 - apart))
    ]
    keep_probs[0].start()

    @pl.when(stays)
    def _():
        take_kv(0)

    for qb in range(n_qb):
        attend(0, 1 - apart, qb, apart)
    keep_probs[1].start()
    for c in kv_copies(0):
        c.wait_send()
    for rb in range(n_rb):
        rows = block_rows(rb)
        dense_forward(0, rows, keep0, rows)
        project(1, rb)
    send_kv(1)
    results = [deliver(0)]
    for c in keep_probs:
        c.wait()
    for qb in range(n_qb):
        attend(1, 0, qb, None)
    take_kv(1)
    for qb in range(n_qb):
        attend(1, 1, qb, 0)
    for c in kv_copies(1):
        c.wait_send()

    @pl.when(swaps)
    def _():
        arrive_cot.wait()

    @pl.when(stays)
    def _():
        here_cot.wait()

    own = slice(0, rb_rows)
    for rb in range(n_rb):
        rows = block_rows(rb)
        dense_forward(1, rows, keep1(rb), own)
    for rb in range(n_rb):
        rows = block_rows(rb)
        dense_backward(1, rows, cotin[rows, :].astype(F32), keep1(rb), own, rb == 0)

    def fetch(pair, half):
        heads = pl.ds(2 * pair, 2)
        return pltpu.make_async_copy(
            saved.at[half, :, heads], probs.at[half, :, heads], p_sem.at[2 + 2 * pair + half]
        )

    queue = []
    tick = functools.partial(advance, queue)
    for l in reversed(range(LAYERS)):
        if l == 0:
            for rb in range(n_rb):
                rows = block_rows(rb)
                dense_backward(0, rows, dr[rows, :], keep0, rows, rb == 0)
                tick()
        launch(queue, groups[l, "dense"])
        q_t[...] = qs[l].T
        for pair in range(2):
            for half in (1, 0):
                if l == 0:
                    fetch(pair, half).wait()
                attend_back(l, pair, half, tick)
                if l == 1:
                    fetch(pair, half).start()
                if half == 1:
                    send_back(l, pair)
            post(l, pair)
            tick()
            if l == 0:
                launch(queue, groups[0, pair], pair == 1)
            elif pair == 0:
                results.append(deliver(1))
        if l == 1:
            launch(queue, groups[1, "qkv"])
            dr[...] = input_grad(1)
            tick()

    dh = input_grad(0)
    hi = dh.astype(BF)
    cotin[...] = hi
    tick()
    gone = swap(4, cotin, tg)
    kept_here = pltpu.make_async_copy(cotin, tg, lo_sem.at[2])

    @pl.when(swaps)
    def _():
        gone.start()

    @pl.when(stays)
    def _():
        kept_here.start()

    lo_part = (dh - hi.astype(F32)).astype(BF)
    masks = mask_rows(slice(0, n))
    sm[10:11, :] = (dot_nn(masks, hi) + dot_nn(masks, lo_part))[0:1, :]
    sm[11:16, :] = jnp.zeros((5, d), F32)
    sm[26:32, :] = jnp.zeros((6, d), F32)

    def small_steps():
        k = 0
        for _, values, peers in rounds_big:
            rsm[2 * k] = sm[...]
            copies = []
            for m in range(1, 1 << len(values)):
                c = remote(rsm.at[2 * k], rsm.at[2 * (k + m) - 1], sm_send.at[k + m - 1], sm_recv.at[k + m - 1], peers[m])
                c.start()
                copies.append(c)
            yield
            for c in copies:
                c.wait()
            if len(values) == 1:
                sm[...] += rsm[2 * k + 1]
            else:
                sm[...] = (sm[...] + rsm[2 * k + 1]) + (rsm[2 * k + 3] + rsm[2 * k + 5])
            k += (1 << len(values)) - 1

    launch(queue, small_steps())
    drain(*queue)
    out = pltpu.make_async_copy(sm, small, lo_sem.at[4])
    out.start()
    for pair in range(2):
        back_copy(0, pair).wait_send()

    for c in finished:
        c.wait()
    out.wait()

    @pl.when(swaps)
    def _():
        for c, _ in results:
            c.wait()
        gone.wait()

    @pl.when(stays)
    def _():
        for _, here in results:
            here.wait()
        kept_here.wait()


def spread_kernel(
    lo_in, tg_in, red_in, small_in, msk_in,
    o_lo, o_tg, o_mv, o_qkv, o_qvb, o_wo, o_bo, o_gain, o_bias, o_wu, o_bu, o_wd, o_bd,
    lo, tg, red, small, msk, tgf, qkv, wo, wu, wd, mv, qvb, bo, gain, bias, bu, bd, sem,
):
    early, late = pl.ds(1536, 2560), pl.ds(0, 1536)
    order = [(1, early), (1, late), (0, early), (0, late)]
    pairs = [(red_in.at[l, r], red.at[l, r]) for l, r in order]
    pairs += [(msk_in, msk), (tg_in, tg), (small_in, small), (lo_in, lo)]
    takes = [pltpu.make_async_copy(a, b, sem.at[i]) for i, (a, b) in enumerate(pairs)]
    for c in takes:
        c.start()
    gives = []

    def give(a, b):
        c = pltpu.make_async_copy(a, b, sem.at[len(takes) + len(gives)])
        c.start()
        gives.append(c)

    n, d = tg.shape
    for i, (l, r) in enumerate(order):

        def block(b, rows=256, l=l):
            return red[l, b * 256 : b * 256 + rows, :].astype(F32)

        takes[i].wait()
        if r is early:
            for c in range(2):
                wd[l, :, c * 128 : c * 128 + 128] = block(12 + 2 * c, 512)
            give(wd.at[l], o_wd.at[l])
            for c in range(4):
                wu[l, :, c * 128 : c * 128 + 128] = block(8 + c)
            give(wu.at[l], o_wu.at[l])
            for c in range(2):
                wo[l, :, c * 128 : c * 128 + 128] = block(6 + c)
            give(wo.at[l], o_wo.at[l])
        else:
            for c in range(6):
                qkv[l, :, c * 128 : c * 128 + 128] = block(c % 2 * 3 + c // 2)
            give(qkv.at[l], o_qkv.at[l])
    takes[4].wait()
    takes[5].wait()
    mask_rows = jnp.broadcast_to(msk[...].astype(F32), (16, n)).astype(BF)
    first_row = (lax.broadcasted_iota(jnp.int32, (16, d), 0) == 0).astype(F32).astype(BF)
    is_masked = dot_tn(mask_rows, first_row) > 0.5
    tgf[...] = jnp.where(is_masked, 0.0, tg[...].astype(F32))
    give(tgf, o_tg.at[0])
    takes[6].wait()
    mv[...] = small[10:11, :]
    for l in range(LAYERS):

        def row(r, l=l):
            return small[16 * l + r : 16 * l + r + 1, :]

        qvb[l, 0:1, :] = row(0)
        qvb[l, 1:2, :] = row(1)
        bo[l : l + 1, :] = row(2)
        gain[l, 0:1, :] = row(3)
        gain[l, 1:2, :] = row(4)
        bias[l, 0:1, :] = row(5)
        bias[l, 1:2, :] = row(6)
        bu[l : l + 1, :d] = row(7)
        bu[l : l + 1, d:] = row(8)
        bd[l : l + 1, :] = row(9)
    for a, b in ((mv, o_mv), (qvb, o_qvb), (bo, o_bo), (gain, o_gain), (bias, o_bias), (bu, o_bu), (bd, o_bd)):
        give(a, b)
    takes[7].wait()
    give(lo, o_lo.at[:, 0])
    for c in gives:
        c.wait()


def shards(sizes, *args):
    (
        tokens, masked, mask_vector, qkv_weight, qv_bias, out_weight, out_bias, norm_gain,
        norm_bias, up_weight, up_bias, down_weight, down_bias, cotangent,
    ) = args
    _, n, d = tokens.shape
    ff = up_weight.shape[2]
    qb = min(512, n)
    rb = min(512, n)
    further = int(math.log2(sizes[0])) - 4
    n_copies = 7 + further
    hbm = pl.BlockSpec(memory_space=pl.ANY)

    def room(rows, big):
        sent = rows // 2 + 3 * (rows // 8)
        return sent + (3 * (rows // 32) + further * (rows // 32) if big else (3 + further) * (rows // 8))

    V = pltpu.VMEM
    dma = pltpu.SemaphoreType.DMA

    scratch = [
        *[
            V(w.shape, BF)
            for w in (
                mask_vector, qkv_weight, qv_bias, out_weight, out_bias, norm_gain, norm_bias, up_weight,
                up_bias, down_weight, down_bias,
            )
        ],
        V((LAYERS, 4096, 128), BF),
        V((1, n), jnp.int32), V((n, d), BF), V((LAYERS + 1, n, d), BF), V((n, d), F32),
        V((LAYERS, n, d), BF), V((LAYERS, 2, n, d), BF), V((LAYERS, 2, 2, n, 256), BF),
        V((LAYERS, n, d), F32), V((LAYERS, 2, n, d), F32),
        V((n, d), BF), V((n, d), BF), V((n, 2), F32),
        V((n, d), BF), V((n, ff), BF), V((n, ff), BF),
        V((n // rb, rb, d), BF), V((n // rb, rb, 2), F32),
        V((2, 2, n, 256), BF), V((2, 128, n), BF), V((d, n), BF),
        V((2 * d, n), F32), V((2 * d, n), BF), V((LAYERS, 2 * d, n), BF),
        V((LAYERS, 4096, 128), F32), V((32, d), F32), V((2 * n_copies, 32, d), F32),
        V((2, n // qb, 4, qb, n), BF),
        V((room(2560, True), 128), BF), V((2 * room(768, False), 128), BF),
        V((LAYERS, room(2560, True), 128), BF), V((LAYERS, 2 * room(768, False), 128), BF),
        dma((5 + n // rb,)), dma((5 + n // rb,)), dma((LAYERS, 2)), dma((LAYERS, 2)), dma((LAYERS, 2)), dma((LAYERS, 2)),
        dma((6,)), dma((5,)),
        dma((5, 14 + further)), dma((5, 14 + further)), dma((5,)), dma((n_copies,)), dma((n_copies,)),
        dma((13,)),
    ]
    lo, tg, red, small, _ = pl.pallas_call(
        functools.partial(main_kernel, sizes, qb, rb),
        out_shape=(
            jax.ShapeDtypeStruct((LAYERS, n, d), BF),
            jax.ShapeDtypeStruct((n, d), BF),
            jax.ShapeDtypeStruct((LAYERS, 4096, 128), BF),
            jax.ShapeDtypeStruct((32, d), F32),
            jax.ShapeDtypeStruct((2, n // qb, 4, qb, n), BF),
        ),
        in_specs=[hbm] * 14,
        out_specs=(hbm,) * 5,
        scratch_shapes=scratch,
        compiler_params=pltpu.CompilerParams(
            collective_id=0, has_side_effects=True, vmem_limit_bytes=63 << 20
        ),
        name="encoder",
    )(
        tokens[0], masked, mask_vector, qkv_weight, qv_bias, out_weight, out_bias,
        norm_gain, norm_bias, up_weight, up_bias, down_weight, down_bias, cotangent[0],
    )

    def f32(*shape):
        return jax.ShapeDtypeStruct(shape, F32)

    grads = (
        f32(1, d), f32(LAYERS, d, 3 * d), f32(LAYERS, 2, d), f32(LAYERS, d, d), f32(LAYERS, d),
        f32(LAYERS, 2, d), f32(LAYERS, 2, d), f32(LAYERS, d, ff), f32(LAYERS, ff),
        f32(LAYERS, ff, d), f32(LAYERS, d),
    )
    order = (1, 3, 7, 9, 0, 2, 4, 5, 6, 8, 10)
    outs = pl.pallas_call(
        spread_kernel,
        out_shape=(jax.ShapeDtypeStruct((LAYERS, 1, n, d), BF), f32(1, n, d), *grads),
        in_specs=[hbm] * 5,
        out_specs=(hbm,) * 13,
        scratch_shapes=[
            V((LAYERS, n, d), BF), V((n, d), BF), V((LAYERS, 4096, 128), BF), V((32, d), F32),
            V((1, n), jnp.int32), V((n, d), F32), *[V(grads[i].shape, F32) for i in order], dma((32,)),
        ],
        compiler_params=pltpu.CompilerParams(vmem_limit_bytes=63 << 20),
        name="spread",
    )(lo, tg, red, small, masked)
    return (*outs[:2], outs[2][0], *outs[3:])


def solution(mesh):
    rows = P("dp", "seq", None)
    in_specs = (rows, P("dp", "seq"), *[P()] * 11, rows)
    out_specs = (P(None, "dp", "seq", None), rows, *[P()] * 11)
    sizes = (mesh.shape["dp"], mesh.shape["seq"])
    return jax.shard_map(
        functools.partial(shards, sizes), mesh=mesh, in_specs=in_specs, out_specs=out_specs, check_vma=False
    )
```

```python
import functools
import math

import jax
import jax.numpy as jnp
from jax import lax
from jax.experimental import pallas as pl
from jax.experimental.pallas import tpu as pltpu
from jax.sharding import PartitionSpec as P

LAYERS = 2
HEAD = 64
BF = jnp.bfloat16
F32 = jnp.float32
MESH = pl.DeviceIdType.MESH
LOG2E = 1.4426950408889634
LN2 = 0.6931471805599453
EPS = 1e-05
TG_PARTS = 4
TG_PLAN = ((), (0, 1), (2, 3))


def dot_nt(a, b):
    return lax.dot_general(a, b, (((1,), (1,)), ((), ())), preferred_element_type=F32)


def dot_nn(a, b):
    return lax.dot_general(a, b, (((1,), (0,)), ((), ())), preferred_element_type=F32)


def dot_tn(a, b):
    return lax.dot_general(a, b, (((0,), (0,)), ((), ())), preferred_element_type=F32)


def head_lanes(h, width):
    lanes = lax.broadcasted_iota(jnp.int32, (1, width), 1) % 128
    return (lanes < 64) if h % 2 == 0 else (lanes >= 64)


def row_sum(x):
    return jnp.sum(x, axis=0, keepdims=True)


def norm(r):
    c = r - jnp.mean(r, axis=1, keepdims=True)
    rs = lax.rsqrt(jnp.mean(c * c, axis=1, keepdims=True) + EPS)
    return c * rs, rs


def norm_back(t, xhat, rs):
    return rs * (
        t - jnp.mean(t, axis=1, keepdims=True) - xhat * jnp.mean(t * xhat, axis=1, keepdims=True)
    )


def flips(mask, count):
    return [i for i in range(count) if mask >> i & 1]


class Reduction:
    def __init__(self, acc, out, sbuf, rbuf, send, recv, layer, lo, rows, rounds, ticks, so, finish):
        self.acc, self.out, self.sbuf, self.rbuf = acc, out, sbuf, rbuf
        self.so, self.finish = so, finish
        self.back_ticks = ticks[len(rounds) :]
        self.send, self.recv = send, recv
        self.layer, self.lo, self.rows, self.rounds, self.ticks = layer, lo, rows, rounds, ticks
        self.sems = 0

    def copy(self, src, dst, peer):
        k = self.sems
        self.sems += 1
        return pltpu.make_async_remote_copy(
            src_ref=src,
            dst_ref=dst,
            send_sem=self.send.at[k],
            recv_sem=self.recv.at[k],
            device_id=peer,
            device_id_type=MESH,
        )

    def steps(self):
        acc, out = self.acc.at[self.layer], self.out.at[self.layer]
        base, size, so = self.lo, self.rows, self.so
        bases, sent = [], []
        for (split, values, peers), wait in zip(self.rounds, self.ticks):
            bases.append((base, size))
            count = len(values)
            part = size >> count if split else size
            copies, places = [], []
            for mask in range(1, 1 << count):
                give = base
                if split:
                    for i, v in enumerate(values):
                        give = give + (1 - v if mask >> i & 1 else v) * ((part << i))
                    give = pl.multiple_of(give, 16)
                place = pl.ds(so, part)
                so += part
                self.sbuf[place, :] = acc[pl.ds(give, part), :].astype(BF)
                c = self.copy(self.sbuf.at[place], self.rbuf.at[place], peers[mask])
                c.start()
                copies.append(c)
                places.append(place)
            if split:
                for i, v in enumerate(values):
                    base = base + v * (part << i)
                base = pl.multiple_of(base, 16)
                size = part
            for _ in range(wait):
                yield
            for c in copies:
                c.wait_recv()
            sent += copies
            mine = pl.ds(base, size)
            got = [self.rbuf[place, :].astype(F32) for place in places]
            held = acc[mine, :]
            if not split:
                held = held.astype(BF).astype(F32)
            if count == 1:
                acc[mine, :] = held + got[0]
            else:
                acc[mine, :] = (held + got[0]) + (got[1] + got[2])
        mine = pl.ds(base, size)
        out[mine, :] = acc[mine, :].astype(BF)
        for c in sent:
            c.wait_send()
        sent = []
        back = [(r, b) for r, b in zip(self.rounds, bases) if r[0]]
        for ((_, values, peers), (up_base, up_size)), wait in zip(reversed(back), self.back_ticks):
            if isinstance(wait, tuple):
                low = pl.multiple_of(up_base + values[0] * size, 16)
                lines = [pl.ds(pl.multiple_of(low + 2 * v * size, 16), size) for v in range(2)]
                plan = [([pl.ds(base, size)], [2], wait[0]), (lines, [1], wait[1])]
            else:
                plan = [([pl.ds(base, size)], range(1, 1 << len(values)), wait)]
            for places, masks, pause in plan:
                copies = [self.copy(out.at[p], out.at[p], peers[m]) for p in places for m in masks]
                for c in copies:
                    c.start()
                for _ in range(pause):
                    yield
                for c in copies:
                    c.wait_recv()
                sent += copies
            base, size = up_base, up_size
        for c in sent:
            c.wait_send()
        self.finish()


def drain(*generators):
    live = list(generators)
    while live:
        live = [g for g in live if next(g, "end") != "end"]


def advance(queue):
    queue[:] = [g for g in queue if next(g, "end") != "end"]


def launch(queue, group, ahead=False):
    next(group)
    queue.insert(0 if ahead else len(queue), group)


def main_kernel(sizes, qb_rows, rb_rows, *refs):
    (
        tok, msk, mv_in, wqkv_in, qvb_in, wo_in, bo_in, gains_in, biases_in, wu_in, bu_in, wd_in, bd_in, cot,
        lo, tg, red_out, small, saved,
        mv, wqkv, qvb, wo, bo, gains, biases, wu, bu, wd, bd, red,
        mskin, cotin, hb, dr, qs, kk, vx, oo, ff_,
        x1, x2, rss, n1s, gs, gps, n1_last, rs_last,
        dox, dot_t, q_t, dkv, skv, rkv, acc, sm, rsm, probs,
        sb_e, sb_q, rb_e, rb_q,
        swap_send, swap_recv, kv_send, kv_recv, g_send, g_recv, p_sem, lo_sem,
        red_send, red_recv, red_done, sm_send, sm_recv, load_sem,
    ) = refs
    dp_size, seq_size = sizes
    n, d = tok.shape
    n_qb, n_rb = n // qb_rows, n // rb_rows
    d_i, s_i = lax.axis_index("dp"), lax.axis_index("seq")
    core = d_i % 2
    mate = (d_i + 1 - 2 * core, s_i)
    cross = (d_i + 1 - 2 * core, 1 - s_i)
    swaps = core != s_i
    stays = core == s_i
    apart = (core + s_i) % 2

    def place_bit(axis, b):
        return (axis, b, ((d_i if axis == "dp" else s_i) // b) % 2)

    def make_round(split, *placed):
        peers = [None]
        for mask in range(1, 1 << len(placed)):
            spot = {"dp": d_i, "seq": s_i}
            for i in flips(mask, len(placed)):
                axis, b, v = placed[i]
                spot[axis] = spot[axis] + b - 2 * b * v
            peers.append((spot["dp"], spot["seq"]))
        return (split, [v for _, _, v in placed], peers)

    further = int(math.log2(dp_size)) - 4
    near = [
        make_round(True, place_bit("dp", 1)),
        make_round(True, place_bit("dp", 2), place_bit("seq", 1)),
    ]
    far = [make_round(False, place_bit("dp", 16 << k)) for k in range(further)]
    line = [place_bit("dp", 4), place_bit("dp", 8)]
    rounds_big = [*near, make_round(True, *line), *far]
    rounds_low = [*near, make_round(False, *line), *far]

    barrier = pltpu.get_barrier_semaphore()
    peers = [peer for _, _, group in reversed(rounds_big) for peer in group[1:]]
    peers.insert(0, cross)
    for peer in peers:
        pl.semaphore_signal(barrier, inc=1, device_id=peer, device_id_type=MESH)
    loads = [
        pltpu.make_async_copy(src, dst, load_sem.at[i])
        for i, (src, dst) in enumerate(
            (
                (wqkv_in, wqkv), (wo_in, wo), (wu_in, wu), (wd_in, wd), (mv_in, mv), (qvb_in, qvb),
                (bo_in, bo), (gains_in, gains), (biases_in, biases), (bu_in, bu), (bd_in, bd),
            )
        )
    ]
    for c in loads:
        c.start()
    for l in range(LAYERS):
        for half in range(2):
            for pair in range(2):
                vx[l, half, pair, :, 128:] = jnp.ones((n, 128), BF)
    pl.semaphore_wait(barrier, len(peers))

    def remote(src, dst, send, recv, peer):
        return pltpu.make_async_remote_copy(
            src_ref=src, dst_ref=dst, send_sem=send, recv_sem=recv, device_id=peer, device_id_type=MESH
        )

    def swap(i, src, dst):
        return remote(src, dst, swap_send.at[i], swap_recv.at[i], cross)

    def part(rb):
        return pl.ds(rb * rb_rows, rb_rows)

    arrive_mask = swap(0, msk, mskin)
    arrive_cot = swap(1, cot, cotin)
    arrive = [swap(5 + rb, tok.at[part(rb)], hb.at[0, part(rb)]) for rb in range(n_rb)]
    here_tok = pltpu.make_async_copy(tok, hb.at[0], load_sem.at[11])
    here_mask = pltpu.make_async_copy(msk, mskin, load_sem.at[12])
    here_cot = pltpu.make_async_copy(cot, cotin, lo_sem.at[3])

    @pl.when(swaps)
    def _():
        arrive_mask.start()
        arrive[0].start()

    @pl.when(stays)
    def _():
        here_tok.start()
        here_mask.start()
        here_cot.start()

    first_row = (lax.broadcasted_iota(jnp.int32, (16, d), 0) == 0).astype(F32).astype(BF)

    def mask_rows(rows):
        return jnp.broadcast_to(mskin[:, rows].astype(F32), (16, rows.stop - rows.start)).astype(BF)

    def gain(l, i):
        return gains[l, i : i + 1, :].astype(F32)

    def shift(l, i):
        return biases[l, i : i + 1, :].astype(F32)

    def v_sent():
        return dox.at[1, 0]

    def v_got(l):
        return dox.at[0, l]

    def block_rows(rb):
        return slice(rb * rb_rows, (rb + 1) * rb_rows)

    def embed(rb):
        rows = block_rows(rb)
        is_masked = dot_tn(mask_rows(rows), first_row) > 0.5
        x = jnp.where(is_masked, mv[...].astype(F32).reshape(1, d), hb[0, rows, :].astype(F32))
        hb[0, rows, :] = x.astype(BF)

    def project(l, rb):
        rows = block_rows(rb)
        x = hb[l, rows, :]
        q = dot_nn(x, wqkv[l, :, :d]) + qvb[l, 0:1, :].astype(F32)
        qs[l, rows, :] = (q * (LOG2E * HEAD**-0.5)).astype(BF)
        kk[l, 0, rows, :] = dot_nn(x, wqkv[l, :, d : 2 * d]).astype(BF)
        v = (dot_nn(x, wqkv[l, :, 2 * d :]) + qvb[l, 1:2, :].astype(F32)).astype(BF)
        v_sent()[rows, :] = v
        vx[l, 0, 0, rows, :128] = v[:, :128]
        vx[l, 0, 1, rows, :128] = v[:, 128:]

    def kv_copies(l):
        return [
            remote(kk.at[l, 0], kk.at[l, 1], kv_send.at[l, 0], kv_recv.at[l, 0], mate),
            remote(v_sent(), v_got(l), kv_send.at[l, 1], kv_recv.at[l, 1], mate),
        ]

    def send_kv(l):
        for c in kv_copies(l):
            c.start()

    def take_kv(l):
        for c in kv_copies(l):
            c.wait_recv()
        vx[l, 1, 0, :, :128] = v_got(l)[:, :128]
        vx[l, 1, 1, :, :128] = v_got(l)[:, 128:]

    def attend(l, half, qb, before):
        rows = slice(qb * qb_rows, (qb + 1) * qb_rows)

        def scores(h):
            c = slice(h // 2 * 128, h // 2 * 128 + 128)
            qm = jnp.where(head_lanes(h, 128), qs[l, rows, c], jnp.zeros((), BF))
            return dot_nt(qm, kk[l, half, :, c])

        kept = [None, None]
        s = scores(0)
        for h in range(4):
            top = jnp.max(s, axis=1, keepdims=True)
            following = scores(h + 1) if h < 3 else None
            e = jnp.exp2(s - top).astype(BF)
            probs[half, qb, h] = e
            r = dot_nn(e, vx[l, half, h // 2])
            s = following
            kept[h % 2] = (r[:, :128], r[:, 128:], top)
            if h % 2 == 1:
                left = head_lanes(0, 128)
                c = slice(h // 2 * 128, h // 2 * 128 + 128)
                o, total, top = (jnp.where(left, kept[0][i], kept[1][i]) for i in range(3))
                if before is None:
                    oo[l, rows, c] = o
                    ff_[l, 0, rows, c] = total
                    ff_[l, 1, rows, c] = top
                else:
                    total0, top0 = ff_[l, 0, rows, c], ff_[l, 1, rows, c]
                    both = jnp.maximum(top0, top)
                    a0, a1 = jnp.exp2(top0 - both), jnp.exp2(top - both)
                    inv = 1.0 / (total0 * a0 + total * a1)
                    ff_[l, before, rows, c] = a0 * inv
                    ff_[l, half, rows, c] = a1 * inv
                    oo[l, rows, c] = oo[l, rows, c] * (a0 * inv) + o * (a1 * inv)

    def dense_forward(l, rows, keep, krows):
        kx1, kx2, kr, kn1, kg, kgp = keep
        y = dot_nn(oo[l, rows, :].astype(BF), wo[l]) + bo[l : l + 1, :].astype(F32)
        h_in = hb[0, rows, :].astype(F32) if l == 0 else dr[rows, :]
        xh, rs = norm(h_in + y)
        kx1[krows, :] = xh.astype(kx1.dtype)
        kr[krows, 0:1] = rs
        n1 = xh * gain(l, 0) + shift(l, 0)
        n1b = n1.astype(BF)
        kn1[krows, :] = n1b
        u = dot_nn(n1b, wu[l]) + bu[l : l + 1, :].astype(F32)
        c0 = math.sqrt(2.0 / math.pi)
        u2 = u * u
        t = jnp.tanh(c0 * u * (1.0 + 0.044715 * u2))
        g = (0.5 * u * (1.0 + t)).astype(BF)
        kg[krows, :] = g
        kgp[krows, :] = (
            0.5 * (1.0 + t) + 0.5 * u * (1.0 - t * t) * (c0 * (1.0 + 3 * 0.044715 * u2))
        ).astype(BF)
        z, rs2 = norm(n1 + dot_nn(g, wd[l]) + bd[l : l + 1, :].astype(F32))
        kx2[krows, :] = z.astype(kx2.dtype)
        kr[krows, 1:2] = rs2
        h_out = z * gain(l, 1) + shift(l, 1)
        hb[l + 1, rows, :] = h_out.astype(BF)
        if l + 1 < LAYERS:
            dr[rows, :] = h_out

    def put(l, lo_row, value, first):
        span = slice(lo_row, lo_row + value.shape[0])
        acc[l, span, :] = value if first else acc[l, span, :] + value

    def put_small(l, row, value, first, c=slice(None)):
        span = slice(16 * l + row, 16 * l + row + 1)
        sm[span, c] = value if first else sm[span, c] + value

    same_head = (
        lax.broadcasted_iota(jnp.int32, (d, d), 0) // HEAD
        == lax.broadcasted_iota(jnp.int32, (d, d), 1) // HEAD
    ).astype(F32).astype(BF)

    def dense_backward(l, rows, g, keep, krows, first):
        kx1, kx2, kr, kn1, kg, kgp = keep
        xh = kx2[krows, :].astype(F32)
        put_small(l, 4, row_sum(g * xh), first)
        put_small(l, 6, row_sum(g), first)
        dr2 = norm_back(g * gain(l, 1), xh, kr[krows, 1:2])
        df = dr2.astype(BF)
        put_small(l, 9, row_sum(df.astype(F32)), first)
        wgrad = dot_tn(kg[krows, :], df)
        for c in range(2):
            put(l, (12 + 2 * c) * 256, wgrad[:, c * 128 : c * 128 + 128], first)
        du = (kgp[krows, :].astype(F32) * dot_nt(df, wd[l])).astype(BF)
        dub = row_sum(du.astype(F32))
        put_small(l, 7, dub[:, :d], first)
        put_small(l, 8, dub[:, d:], first)
        wgrad = dot_tn(kn1[krows, :], du)
        for c in range(4):
            put(l, (8 + c) * 256, wgrad[:, c * 128 : c * 128 + 128], first)
        dn1 = dr2 + dot_nt(du, wu[l])
        xh = kx1[krows, :].astype(F32)
        put_small(l, 3, row_sum(dn1 * xh), first)
        put_small(l, 5, row_sum(dn1), first)
        dr1 = norm_back(dn1 * gain(l, 0), xh, kr[krows, 0:1])
        dr[rows, :] = dr1
        dy = dr1.astype(BF)
        put_small(l, 2, row_sum(dy.astype(F32)), first)
        o = oo[l, rows, :]
        wgrad = dot_tn(o.astype(BF), dy)
        for c in range(2):
            put(l, (6 + c) * 256, wgrad[:, c * 128 : c * 128 + 128], first)
        do = dot_nt(dy, wo[l])
        x = do * o
        hi = x.astype(BF)
        lo_part = (x - hi.astype(F32)).astype(BF)
        delta = dot_nn(hi, same_head) + dot_nn(lo_part, same_head)
        lane = lax.broadcasted_iota(jnp.int32, (1, d), 1) % HEAD
        for half in range(2):
            f = ff_[l, half, rows, :]
            dob = (do * f).astype(BF)
            x = -(delta * f)
            hi = x.astype(BF)
            lo_part = (x - hi.astype(F32)).astype(BF)
            extra = jnp.where(lane == 0, hi, jnp.where(lane == 1, lo_part, jnp.zeros((), BF)))
            for pair in range(2):
                c = slice(pair * 128, pair * 128 + 128)
                dox[half, pair, rows, :128] = dob[:, c]
                dox[half, pair, rows, 128:] = extra[:, c]

    dq = ff_.at[1, 0]

    def attend_back(l, pair, half, ticks):
        c = slice(pair * 128, pair * 128 + 128)
        dot_t[half] = dox[half, pair, :, :128].T
        work = [(qb, side) for qb in range(n_qb) for side in range(2)]

        def rows_of(qb):
            return slice(qb * qb_rows, (qb + 1) * qb_rows)

        def prob_grad(qb, side):
            x = jnp.where(head_lanes(side, 256), dox[half, pair, rows_of(qb), :], jnp.zeros((), BF))
            return dot_nt(x, vx[l, half, pair])

        kept = [None, None]
        dp = prob_grad(*work[0])
        for i, (qb, side) in enumerate(work):
            rows = rows_of(qb)
            hr = slice(side * HEAD, (side + 1) * HEAD)
            krw = slice(pair * d + side * HEAD, pair * d + (side + 1) * HEAD)
            vrw = slice(pair * d + 128 + side * HEAD, pair * d + 128 + (side + 1) * HEAD)
            e = probs[half, qb, 2 * pair + side]
            dv = dot_nn(dot_t[half, hr, rows], e)
            dpn = prob_grad(*work[i + 1]) if i + 1 < len(work) else None
            ds = (e.astype(F32) * dp).astype(BF)
            dk = dot_nn(q_t[pair * 128 + side * HEAD : pair * 128 + (side + 1) * HEAD, rows], ds)
            if qb == 0:
                dkv[vrw, :] = dv
                dkv[krw, :] = dk
            else:
                dkv[vrw, :] += dv
                dkv[krw, :] += dk
            kept[side] = dot_nn(ds, kk[l, half, :, c])
            dp = dpn
            if side == 1:
                value = jnp.where(head_lanes(0, 128), kept[0], kept[1])
                dq[rows, c] = value if half == 1 else dq[rows, c] + value
                ticks()

    def pair_rows(pair):
        return slice(pair * d, (pair + 1) * d)

    def back_copy(l, pair):
        span = pl.ds(pair * d, d)
        return remote(skv.at[span], rkv.at[l, span], g_send.at[l, pair], g_recv.at[l, pair], mate)

    def send_back(l, pair):
        if l == 0:
            back_copy(1, pair).wait_send()
        r = pair * d
        skv[r : r + 128, :] = (dkv[r : r + 128, :] * LN2).astype(BF)
        skv[r + 128 : r + d, :] = dkv[r + 128 : r + d, :].astype(BF)
        back_copy(l, pair).start()

    def post(l, pair):
        r = pair * d
        c = slice(pair * 128, pair * 128 + 128)
        dqb = (dq[:, c] * HEAD**-0.5).astype(BF)
        back_copy(l, pair).wait_recv()
        dkb = (dkv[r : r + 128, :] * LN2 + rkv[l, r : r + 128, :].astype(F32)).astype(BF).T
        dvb = (dkv[r + 128 : r + d, :] + rkv[l, r + 128 : r + d, :].astype(F32)).astype(BF).T
        dqk = jnp.concatenate([dqb, dkb], axis=1)
        x = hb[l]
        wgrad = dot_tn(x, dqk)
        put(l, pair * 768, wgrad[:, :128], True)
        put(l, pair * 768 + 256, wgrad[:, 128:], True)
        put(l, pair * 768 + 512, dot_tn(x, dvb), True)
        put_small(l, 0, row_sum(dqb.astype(F32)), True, c)
        put_small(l, 1, row_sum(dvb.astype(F32)), True, c)
        dox[0, pair] = dqk
        dox[1, pair, :, :128] = dvb

    def input_grad(l):
        total = dr[...]
        for pair in range(2):
            c = slice(pair * 128, pair * 128 + 128)
            w = jnp.concatenate([wqkv[l, :, c], wqkv[l, :, d + c.start : d + c.stop]], axis=1)
            total = total + dot_nt(dox[0, pair], w)
        dv = jnp.concatenate([dox[1, 0, :, :128], dox[1, 1, :, :128]], axis=1)
        return total + dot_nt(dv, wqkv[l, :, 2 * d :])

    keep0 = (x1, x2, rss, n1s, gs, gps)
    f = wu.shape[2]

    def keep1(rb):
        low = skv if rb == 0 else rkv.at[0]
        return (
            dkv.at[:, rb * d : rb * d + d], dkv.at[:, (2 + rb) * d : (3 + rb) * d], rs_last.at[rb],
            n1_last.at[rb], low.at[:, 0:f], low.at[:, f : 2 * f],
        )

    def deliver(l):
        c = swap(2 + l, hb.at[l + 1], lo.at[l])
        here = pltpu.make_async_copy(hb.at[l + 1], lo.at[l], lo_sem.at[l])

        @pl.when(swaps)
        def _():
            c.start()

        @pl.when(stays)
        def _():
            here.start()

        return c, here

    finished = []

    def reduction(l, lo_row, rows, big, sbuf, rbuf, so, ticks, back_ticks):
        i = len(groups)
        span = pl.ds(lo_row, rows)
        c = pltpu.make_async_copy(red.at[l, span], red_out.at[l, span], red_done.at[i])

        def finish():
            c.start()
            finished.append(c)

        return Reduction(
            acc, red, sbuf, rbuf, red_send.at[i], red_recv.at[i], l, lo_row, rows,
            rounds_big if big else rounds_low, ticks + (2,) * further + back_ticks, so, finish,
        ).steps()

    groups = {}
    groups[1, "dense"] = reduction(1, 1536, 2560, True, sb_e, rb_e.at[1], 0, (2, 3, 2), (2, 4, 2))
    groups[1, "qkv"] = reduction(1, 0, 1536, True, sb_q, rb_q.at[1], 0, (3, 2, 3), (2, 2, 1))
    groups[0, "dense"] = reduction(0, 1536, 2560, True, sb_e, rb_e.at[0], 0, (2, 3, 2), (2, 3, 1))
    groups[0, 0] = reduction(0, 0, 768, False, sb_q, rb_q.at[0], 0, (2, 2, 2), (2, 1))
    groups[0, 1] = reduction(0, 768, 768, False, sb_q, rb_q.at[0], rb_q.shape[1] // 2, (1, 1, 1), (1, 1))

    @pl.when(swaps)
    def _():
        for before, after in zip(arrive, arrive[1:]):
            before.wait_send()
            after.start()
        arrive_mask.wait()
        arrive[0].wait_recv()

    @pl.when(stays)
    def _():
        here_tok.wait()
        here_mask.wait()

    for c in loads:
        c.wait()
    embed(0)
    project(0, 0)

    @pl.when(stays)
    def _():
        for rb in range(1, n_rb):
            embed(rb)
            project(0, rb)
        send_kv(0)

    @pl.when(swaps)
    def _():
        take_kv(0)

    attend(0, apart, 0, None)

    @pl.when(swaps)
    def _():
        for rb in range(1, n_rb):
            arrive[rb].wait_recv()
            embed(rb)
            project(0, rb)
        send_kv(0)
        arrive_cot.start()

    for qb in range(1, n_qb):
        attend(0, apart, qb, None)
    keep_probs = [
        pltpu.make_async_copy(probs.at[half], saved.at[half], p_sem.at[i])
        for i, half in enumerate((apart, 1 - apart))
    ]
    keep_probs[0].start()

    @pl.when(stays)
    def _():
        take_kv(0)

    for qb in range(n_qb):
        attend(0, 1 - apart, qb, apart)
    keep_probs[1].start()
    for c in kv_copies(0):
        c.wait_send()
    for rb in range(n_rb):
        rows = block_rows(rb)
        dense_forward(0, rows, keep0, rows)
        project(1, rb)
    send_kv(1)
    results = [deliver(0)]
    for c in keep_probs:
        c.wait()
    for qb in range(n_qb):
        attend(1, 0, qb, None)
    take_kv(1)
    for qb in range(n_qb):
        attend(1, 1, qb, 0)
    for c in kv_copies(1):
        c.wait_send()

    @pl.when(swaps)
    def _():
        arrive[-1].wait_send()
        arrive_cot.wait()

    @pl.when(stays)
    def _():
        here_cot.wait()

    own = slice(0, rb_rows)
    for rb in range(n_rb):
        rows = block_rows(rb)
        dense_forward(1, rows, keep1(rb), own)
    for rb in range(n_rb):
        rows = block_rows(rb)
        dense_backward(1, rows, cotin[rows, :].astype(F32), keep1(rb), own, rb == 0)

    def fetch(pair, half):
        heads = pl.ds(2 * pair, 2)
        return pltpu.make_async_copy(
            saved.at[half, :, heads], probs.at[half, :, heads], p_sem.at[2 + 2 * pair + half]
        )

    queue = []
    tick = functools.partial(advance, queue)
    for l in reversed(range(LAYERS)):
        if l == 0:
            for rb in range(n_rb):
                rows = block_rows(rb)
                dense_backward(0, rows, dr[rows, :], keep0, rows, rb == 0)
                tick()
        launch(queue, groups[l, "dense"])
        q_t[...] = qs[l].T
        for pair in range(2):
            for half in (1, 0):
                if l == 0:
                    fetch(pair, half).wait()
                attend_back(l, pair, half, tick)
                if l == 1:
                    fetch(pair, half).start()
                if half == 1:
                    send_back(l, pair)
            post(l, pair)
            tick()
            if l == 0:
                launch(queue, groups[0, pair], pair == 1)
            elif pair == 0:
                results.append(deliver(1))
        if l == 1:
            launch(queue, groups[1, "qkv"])
            dr[...] = input_grad(1)
            tick()

    tg_rows = n // TG_PARTS
    tg_out = [
        swap(5 + n_rb + i, cotin.at[pl.ds(i * tg_rows, tg_rows)], tg.at[pl.ds(i * tg_rows, tg_rows)])
        for i in range(TG_PARTS)
    ]
    tg_here = pltpu.make_async_copy(cotin, tg, lo_sem.at[2])

    def send_tg(*parts):
        @pl.when(swaps)
        def _():
            for i in parts:
                tg_out[i].start()

    dh = input_grad(0)
    hi = dh.astype(BF)
    cotin[...] = hi
    send_tg(*TG_PLAN[0])

    @pl.when(stays)
    def _():
        tg_here.start()

    lo_part = (dh - hi.astype(F32)).astype(BF)
    masks = mask_rows(slice(0, n))
    sm[10:11, :] = (dot_nn(masks, hi) + dot_nn(masks, lo_part))[0:1, :]
    sm[11:16, :] = jnp.zeros((5, d), F32)
    sm[26:32, :] = jnp.zeros((6, d), F32)

    def small_steps():
        k = 0
        for _, values, peers in rounds_big:
            rsm[2 * k] = sm[...]
            copies = []
            for m in range(1, 1 << len(values)):
                c = remote(rsm.at[2 * k], rsm.at[2 * (k + m) - 1], sm_send.at[k + m - 1], sm_recv.at[k + m - 1], peers[m])
                c.start()
                copies.append(c)
            yield
            for c in copies:
                c.wait()
            if len(values) == 1:
                sm[...] += rsm[2 * k + 1]
            else:
                sm[...] = (sm[...] + rsm[2 * k + 1]) + (rsm[2 * k + 3] + rsm[2 * k + 5])
            k += (1 << len(values)) - 1

    launch(queue, small_steps())
    for parts in TG_PLAN[1:]:
        tick()
        send_tg(*parts)
    drain(*queue)
    out = pltpu.make_async_copy(sm, small, lo_sem.at[4])
    out.start()
    for pair in range(2):
        back_copy(0, pair).wait_send()

    for c in finished:
        c.wait()
    out.wait()

    @pl.when(swaps)
    def _():
        for c, _ in results:
            c.wait()
        for c in tg_out:
            c.wait()

    @pl.when(stays)
    def _():
        for _, here in results:
            here.wait()
        tg_here.wait()


def spread_kernel(
    lo_in, tg_in, red_in, small_in, msk_in,
    o_lo, o_tg, o_mv, o_qkv, o_qvb, o_wo, o_bo, o_gain, o_bias, o_wu, o_bu, o_wd, o_bd,
    lo, tg, red, small, msk, tgf, qkv, wo, wu, wd, mv, qvb, bo, gain, bias, bu, bd, sem,
):
    early, late = pl.ds(1536, 2560), pl.ds(0, 1536)
    order = [(1, early), (1, late), (0, early), (0, late)]
    pairs = [(red_in.at[l, r], red.at[l, r]) for l, r in order]
    pairs += [(msk_in, msk), (tg_in, tg), (small_in, small), (lo_in, lo)]
    takes = [pltpu.make_async_copy(a, b, sem.at[i]) for i, (a, b) in enumerate(pairs)]
    for c in takes:
        c.start()
    gives = []

    def give(a, b):
        c = pltpu.make_async_copy(a, b, sem.at[len(takes) + len(gives)])
        c.start()
        gives.append(c)

    n, d = tg.shape
    for i, (l, r) in enumerate(order):

        def block(b, rows=256, l=l):
            return red[l, b * 256 : b * 256 + rows, :].astype(F32)

        takes[i].wait()
        if r is early:
            for c in range(2):
                wd[l, :, c * 128 : c * 128 + 128] = block(12 + 2 * c, 512)
            give(wd.at[l], o_wd.at[l])
            for c in range(4):
                wu[l, :, c * 128 : c * 128 + 128] = block(8 + c)
            give(wu.at[l], o_wu.at[l])
            for c in range(2):
                wo[l, :, c * 128 : c * 128 + 128] = block(6 + c)
            give(wo.at[l], o_wo.at[l])
        else:
            for c in range(6):
                qkv[l, :, c * 128 : c * 128 + 128] = block(c % 2 * 3 + c // 2)
            give(qkv.at[l], o_qkv.at[l])
    takes[4].wait()
    takes[5].wait()
    mask_rows = jnp.broadcast_to(msk[...].astype(F32), (16, n)).astype(BF)
    first_row = (lax.broadcasted_iota(jnp.int32, (16, d), 0) == 0).astype(F32).astype(BF)
    is_masked = dot_tn(mask_rows, first_row) > 0.5
    tgf[...] = jnp.where(is_masked, 0.0, tg[...].astype(F32))
    give(tgf, o_tg.at[0])
    takes[6].wait()
    mv[...] = small[10:11, :]
    for l in range(LAYERS):

        def row(r, l=l):
            return small[16 * l + r : 16 * l + r + 1, :]

        qvb[l, 0:1, :] = row(0)
        qvb[l, 1:2, :] = row(1)
        bo[l : l + 1, :] = row(2)
        gain[l, 0:1, :] = row(3)
        gain[l, 1:2, :] = row(4)
        bias[l, 0:1, :] = row(5)
        bias[l, 1:2, :] = row(6)
        bu[l : l + 1, :d] = row(7)
        bu[l : l + 1, d:] = row(8)
        bd[l : l + 1, :] = row(9)
    for a, b in ((mv, o_mv), (qvb, o_qvb), (bo, o_bo), (gain, o_gain), (bias, o_bias), (bu, o_bu), (bd, o_bd)):
        give(a, b)
    takes[7].wait()
    give(lo, o_lo.at[:, 0])
    for c in gives:
        c.wait()


def shards(sizes, *args):
    (
        tokens, masked, mask_vector, qkv_weight, qv_bias, out_weight, out_bias, norm_gain,
        norm_bias, up_weight, up_bias, down_weight, down_bias, cotangent,
    ) = args
    _, n, d = tokens.shape
    ff = up_weight.shape[2]
    qb = min(512, n)
    rb = min(512, n)
    further = int(math.log2(sizes[0])) - 4
    n_copies = 7 + further
    hbm = pl.BlockSpec(memory_space=pl.ANY)

    def room(rows, big):
        sent = rows // 2 + 3 * (rows // 8)
        return sent + (3 * (rows // 32) + further * (rows // 32) if big else (3 + further) * (rows // 8))

    V = pltpu.VMEM
    dma = pltpu.SemaphoreType.DMA

    scratch = [
        *[
            V(w.shape, BF)
            for w in (
                mask_vector, qkv_weight, qv_bias, out_weight, out_bias, norm_gain, norm_bias, up_weight,
                up_bias, down_weight, down_bias,
            )
        ],
        V((LAYERS, 4096, 128), BF),
        V((1, n), jnp.int32), V((n, d), BF), V((LAYERS + 1, n, d), BF), V((n, d), F32),
        V((LAYERS, n, d), BF), V((LAYERS, 2, n, d), BF), V((LAYERS, 2, 2, n, 256), BF),
        V((LAYERS, n, d), F32), V((LAYERS, 2, n, d), F32),
        V((n, d), BF), V((n, d), BF), V((n, 2), F32),
        V((n, d), BF), V((n, ff), BF), V((n, ff), BF),
        V((n // rb, rb, d), BF), V((n // rb, rb, 2), F32),
        V((2, 2, n, 256), BF), V((2, 128, n), BF), V((d, n), BF),
        V((2 * d, n), F32), V((2 * d, n), BF), V((LAYERS, 2 * d, n), BF),
        V((LAYERS, 4096, 128), F32), V((32, d), F32), V((2 * n_copies, 32, d), F32),
        V((2, n // qb, 4, qb, n), BF),
        V((room(2560, True), 128), BF), V((2 * room(768, False), 128), BF),
        V((LAYERS, room(2560, True), 128), BF), V((LAYERS, 2 * room(768, False), 128), BF),
        dma((5 + n // rb + TG_PARTS,)), dma((5 + n // rb + TG_PARTS,)), dma((LAYERS, 2)), dma((LAYERS, 2)), dma((LAYERS, 2)), dma((LAYERS, 2)),
        dma((6,)), dma((5,)),
        dma((5, 14 + further)), dma((5, 14 + further)), dma((5,)), dma((n_copies,)), dma((n_copies,)),
        dma((13,)),
    ]
    lo, tg, red, small, _ = pl.pallas_call(
        functools.partial(main_kernel, sizes, qb, rb),
        out_shape=(
            jax.ShapeDtypeStruct((LAYERS, n, d), BF),
            jax.ShapeDtypeStruct((n, d), BF),
            jax.ShapeDtypeStruct((LAYERS, 4096, 128), BF),
            jax.ShapeDtypeStruct((32, d), F32),
            jax.ShapeDtypeStruct((2, n // qb, 4, qb, n), BF),
        ),
        in_specs=[hbm] * 14,
        out_specs=(hbm,) * 5,
        scratch_shapes=scratch,
        compiler_params=pltpu.CompilerParams(
            collective_id=0, has_side_effects=True, vmem_limit_bytes=63 << 20
        ),
        name="encoder",
    )(
        tokens[0], masked, mask_vector, qkv_weight, qv_bias, out_weight, out_bias,
        norm_gain, norm_bias, up_weight, up_bias, down_weight, down_bias, cotangent[0],
    )

    def f32(*shape):
        return jax.ShapeDtypeStruct(shape, F32)

    grads = (
        f32(1, d), f32(LAYERS, d, 3 * d), f32(LAYERS, 2, d), f32(LAYERS, d, d), f32(LAYERS, d),
        f32(LAYERS, 2, d), f32(LAYERS, 2, d), f32(LAYERS, d, ff), f32(LAYERS, ff),
        f32(LAYERS, ff, d), f32(LAYERS, d),
    )
    order = (1, 3, 7, 9, 0, 2, 4, 5, 6, 8, 10)
    outs = pl.pallas_call(
        spread_kernel,
        out_shape=(jax.ShapeDtypeStruct((LAYERS, 1, n, d), BF), f32(1, n, d), *grads),
        in_specs=[hbm] * 5,
        out_specs=(hbm,) * 13,
        scratch_shapes=[
            V((LAYERS, n, d), BF), V((n, d), BF), V((LAYERS, 4096, 128), BF), V((32, d), F32),
            V((1, n), jnp.int32), V((n, d), F32), *[V(grads[i].shape, F32) for i in order], dma((32,)),
        ],
        compiler_params=pltpu.CompilerParams(vmem_limit_bytes=63 << 20),
        name="spread",
    )(lo, tg, red, small, masked)
    return (*outs[:2], outs[2][0], *outs[3:])


def solution(mesh):
    rows = P("dp", "seq", None)
    in_specs = (rows, P("dp", "seq"), *[P()] * 11, rows)
    out_specs = (P(None, "dp", "seq", None), rows, *[P()] * 11)
    sizes = (mesh.shape["dp"], mesh.shape["seq"])
    return jax.shard_map(
        functools.partial(shards, sizes), mesh=mesh, in_specs=in_specs, out_specs=out_specs, check_vma=False
    )
```

```python
import functools
import math

import jax
import jax.numpy as jnp
from jax import lax
from jax.experimental import pallas as pl
from jax.experimental.pallas import tpu as pltpu
from jax.sharding import PartitionSpec as P

LAYERS = 2
HEAD = 64
BF = jnp.bfloat16
F32 = jnp.float32
MESH = pl.DeviceIdType.MESH
SCALE = 1.4426950408889634 * HEAD**-0.5
EPS = 1e-05
TG_PARTS = 4
TG_PLAN = ((), (0, 1), (2, 3))


def dot_nt(a, b):
    return lax.dot_general(a, b, (((1,), (1,)), ((), ())), preferred_element_type=F32)


def dot_nn(a, b):
    return lax.dot_general(a, b, (((1,), (0,)), ((), ())), preferred_element_type=F32)


def dot_tn(a, b):
    return lax.dot_general(a, b, (((0,), (0,)), ((), ())), preferred_element_type=F32)


def head_lanes(h, width):
    lanes = lax.broadcasted_iota(jnp.int32, (1, width), 1) % 128
    return (lanes < 64) if h % 2 == 0 else (lanes >= 64)


def row_sum(x):
    return jnp.sum(x, axis=0, keepdims=True)


def norm(r):
    c = r - jnp.mean(r, axis=1, keepdims=True)
    rs = lax.rsqrt(jnp.mean(c * c, axis=1, keepdims=True) + EPS)
    return c * rs, rs


def norm_back(t, xhat, rs):
    return rs * (
        t - jnp.mean(t, axis=1, keepdims=True) - xhat * jnp.mean(t * xhat, axis=1, keepdims=True)
    )


def flips(mask, count):
    return [i for i in range(count) if mask >> i & 1]


class Reduction:
    def __init__(self, acc, out, sbuf, rbuf, send, recv, layer, lo, rows, rounds, ticks, so, finish):
        self.acc, self.out, self.sbuf, self.rbuf = acc, out, sbuf, rbuf
        self.so, self.finish = so, finish
        self.back_ticks = ticks[len(rounds) :]
        self.send, self.recv = send, recv
        self.layer, self.lo, self.rows, self.rounds, self.ticks = layer, lo, rows, rounds, ticks
        self.sems = 0

    def copy(self, src, dst, peer):
        k = self.sems
        self.sems += 1
        return pltpu.make_async_remote_copy(
            src_ref=src,
            dst_ref=dst,
            send_sem=self.send.at[k],
            recv_sem=self.recv.at[k],
            device_id=peer,
            device_id_type=MESH,
        )

    def steps(self):
        acc, out = self.acc.at[self.layer], self.out.at[self.layer]
        base, size, so = self.lo, self.rows, self.so
        bases, sent = [], []
        for (split, values, peers), wait in zip(self.rounds, self.ticks):
            bases.append((base, size))
            count = len(values)
            part = size >> count if split else size
            copies, places = [], []
            for mask in range(1, 1 << count):
                give = base
                if split:
                    for i, v in enumerate(values):
                        give = give + (1 - v if mask >> i & 1 else v) * ((part << i))
                    give = pl.multiple_of(give, 16)
                place = pl.ds(so, part)
                so += part
                self.sbuf[place, :] = acc[pl.ds(give, part), :].astype(BF)
                c = self.copy(self.sbuf.at[place], self.rbuf.at[place], peers[mask])
                c.start()
                copies.append(c)
                places.append(place)
            if split:
                for i, v in enumerate(values):
                    base = base + v * (part << i)
                base = pl.multiple_of(base, 16)
                size = part
            for _ in range(wait):
                yield
            for c in copies:
                c.wait_recv()
            sent += copies
            mine = pl.ds(base, size)
            got = [self.rbuf[place, :].astype(F32) for place in places]
            held = acc[mine, :]
            if not split:
                held = held.astype(BF).astype(F32)
            if count == 1:
                acc[mine, :] = held + got[0]
            else:
                acc[mine, :] = (held + got[0]) + (got[1] + got[2])
        mine = pl.ds(base, size)
        out[mine, :] = acc[mine, :].astype(BF)
        for c in sent:
            c.wait_send()
        sent = []
        back = [(r, b) for r, b in zip(self.rounds, bases) if r[0]]
        for ((_, values, peers), (up_base, up_size)), wait in zip(reversed(back), self.back_ticks):
            if isinstance(wait, tuple):
                low = pl.multiple_of(up_base + values[0] * size, 16)
                lines = [pl.ds(pl.multiple_of(low + 2 * v * size, 16), size) for v in range(2)]
                plan = [([pl.ds(base, size)], [2], wait[0]), (lines, [1], wait[1])]
            else:
                plan = [([pl.ds(base, size)], range(1, 1 << len(values)), wait)]
            for places, masks, pause in plan:
                copies = [self.copy(out.at[p], out.at[p], peers[m]) for p in places for m in masks]
                for c in copies:
                    c.start()
                for _ in range(pause):
                    yield
                for c in copies:
                    c.wait_recv()
                sent += copies
            base, size = up_base, up_size
        for c in sent:
            c.wait_send()
        self.finish()


def drain(*generators):
    live = list(generators)
    while live:
        live = [g for g in live if next(g, "end") != "end"]


def advance(queue):
    queue[:] = [g for g in queue if next(g, "end") != "end"]


def launch(queue, group, ahead=False):
    next(group)
    queue.insert(0 if ahead else len(queue), group)


def main_kernel(sizes, qb_rows, rb_rows, *refs):
    (
        tok, msk, mv_in, wqkv_in, qvb_in, wo_in, bo_in, gains_in, biases_in, wu_in, bu_in, wd_in, bd_in, cot,
        lo, tg, red_out, small, saved,
        mv, wqkv, qvb, wo, bo, gains, biases, wu, bu, wd, bd, red,
        mskin, cotin, hb, dr, qs, kk, vx, oo, ff_,
        x1, x2, rss, n1s, gs, gps, n1_last, rs_last,
        dox, dot_t, q_t, dkv, skv, rkv, acc, sm, rsm, probs,
        sb_e, sb_q, rb_e, rb_q,
        swap_send, swap_recv, kv_send, kv_recv, g_send, g_recv, p_sem, lo_sem,
        red_send, red_recv, red_done, sm_send, sm_recv, load_sem,
    ) = refs
    dp_size, seq_size = sizes
    n, d = tok.shape
    n_qb, n_rb = n // qb_rows, n // rb_rows
    d_i, s_i = lax.axis_index("dp"), lax.axis_index("seq")
    core = d_i % 2
    mate = (d_i + 1 - 2 * core, s_i)
    cross = (d_i + 1 - 2 * core, 1 - s_i)
    swaps = core != s_i
    stays = core == s_i
    apart = (core + s_i) % 2

    def place_bit(axis, b):
        return (axis, b, ((d_i if axis == "dp" else s_i) // b) % 2)

    def make_round(split, *placed):
        peers = [None]
        for mask in range(1, 1 << len(placed)):
            spot = {"dp": d_i, "seq": s_i}
            for i in flips(mask, len(placed)):
                axis, b, v = placed[i]
                spot[axis] = spot[axis] + b - 2 * b * v
            peers.append((spot["dp"], spot["seq"]))
        return (split, [v for _, _, v in placed], peers)

    further = int(math.log2(dp_size)) - 4
    near = [
        make_round(True, place_bit("dp", 1)),
        make_round(True, place_bit("dp", 2), place_bit("seq", 1)),
    ]
    far = [make_round(False, place_bit("dp", 16 << k)) for k in range(further)]
    line = [place_bit("dp", 4), place_bit("dp", 8)]
    rounds_big = [*near, make_round(True, *line), *far]
    rounds_low = [*near, make_round(False, *line), *far]

    barrier = pltpu.get_barrier_semaphore()
    peers = [peer for _, _, group in reversed(rounds_big) for peer in group[1:]]
    peers.insert(0, cross)
    for peer in peers:
        pl.semaphore_signal(barrier, inc=1, device_id=peer, device_id_type=MESH)
    loads = [
        pltpu.make_async_copy(src, dst, load_sem.at[i])
        for i, (src, dst) in enumerate(
            (
                (wqkv_in, wqkv), (wo_in, wo), (wu_in, wu), (wd_in, wd), (mv_in, mv), (qvb_in, qvb),
                (bo_in, bo), (gains_in, gains), (biases_in, biases), (bu_in, bu), (bd_in, bd),
            )
        )
    ]
    for c in loads:
        c.start()
    for l in range(LAYERS):
        for half in range(2):
            for pair in range(2):
                vx[l, half, pair, :, 128:] = jnp.ones((n, 128), BF)
    pl.semaphore_wait(barrier, len(peers))

    def remote(src, dst, send, recv, peer):
        return pltpu.make_async_remote_copy(
            src_ref=src, dst_ref=dst, send_sem=send, recv_sem=recv, device_id=peer, device_id_type=MESH
        )

    def swap(i, src, dst):
        return remote(src, dst, swap_send.at[i], swap_recv.at[i], cross)

    def part(rb):
        return pl.ds(rb * rb_rows, rb_rows)

    arrive_mask = swap(0, msk, mskin)
    arrive_cot = swap(1, cot, cotin)
    arrive = [swap(5 + rb, tok.at[part(rb)], hb.at[0, part(rb)]) for rb in range(n_rb)]
    here_tok = pltpu.make_async_copy(tok, hb.at[0], load_sem.at[11])
    here_mask = pltpu.make_async_copy(msk, mskin, load_sem.at[12])
    here_cot = pltpu.make_async_copy(cot, cotin, lo_sem.at[3])

    @pl.when(swaps)
    def _():
        arrive_mask.start()
        arrive[0].start()

    @pl.when(stays)
    def _():
        here_tok.start()
        here_mask.start()
        here_cot.start()

    first_row = (lax.broadcasted_iota(jnp.int32, (16, d), 0) == 0).astype(F32).astype(BF)

    def mask_rows(rows):
        return jnp.broadcast_to(mskin[:, rows].astype(F32), (16, rows.stop - rows.start)).astype(BF)

    def gain(l, i):
        return gains[l, i : i + 1, :].astype(F32)

    def shift(l, i):
        return biases[l, i : i + 1, :].astype(F32)

    def v_sent():
        return dox.at[1, 0]

    def v_got(l):
        return dox.at[0, l]

    def block_rows(rb):
        return slice(rb * rb_rows, (rb + 1) * rb_rows)

    def embed(rb):
        rows = block_rows(rb)
        is_masked = dot_tn(mask_rows(rows), first_row) > 0.5
        x = jnp.where(is_masked, mv[...].astype(F32).reshape(1, d), hb[0, rows, :].astype(F32))
        hb[0, rows, :] = x.astype(BF)

    def project(l, rb):
        rows = block_rows(rb)
        x = hb[l, rows, :]
        q = dot_nn(x, wqkv[l, :, :d]) + qvb[l, 0:1, :].astype(F32)
        qs[l, rows, :] = q.astype(BF)
        kk[l, 0, rows, :] = dot_nn(x, wqkv[l, :, d : 2 * d]).astype(BF)
        v = (dot_nn(x, wqkv[l, :, 2 * d :]) + qvb[l, 1:2, :].astype(F32)).astype(BF)
        v_sent()[rows, :] = v
        vx[l, 0, 0, rows, :128] = v[:, :128]
        vx[l, 0, 1, rows, :128] = v[:, 128:]

    def kv_copies(l):
        return [
            remote(kk.at[l, 0], kk.at[l, 1], kv_send.at[l, 0], kv_recv.at[l, 0], mate),
            remote(v_sent(), v_got(l), kv_send.at[l, 1], kv_recv.at[l, 1], mate),
        ]

    def send_kv(l):
        for c in kv_copies(l):
            c.start()

    def take_kv(l):
        for c in kv_copies(l):
            c.wait_recv()
        vx[l, 1, 0, :, :128] = v_got(l)[:, :128]
        vx[l, 1, 1, :, :128] = v_got(l)[:, 128:]

    def attend(l, half, qb, before):
        rows = slice(qb * qb_rows, (qb + 1) * qb_rows)

        def scores(h):
            c = slice(h // 2 * 128, h // 2 * 128 + 128)
            qm = jnp.where(head_lanes(h, 128), qs[l, rows, c], jnp.zeros((), BF))
            return dot_nt(qm, kk[l, half, :, c])

        kept = [None, None]
        s = scores(0)
        for h in range(4):
            top = jnp.max(s, axis=1, keepdims=True)
            following = scores(h + 1) if h < 3 else None
            e = jnp.exp2((s - top) * SCALE).astype(BF)
            probs[half, qb, h] = e
            r = dot_nn(e, vx[l, half, h // 2])
            s = following
            kept[h % 2] = (r[:, :128], r[:, 128:], top)
            if h % 2 == 1:
                left = head_lanes(0, 128)
                c = slice(h // 2 * 128, h // 2 * 128 + 128)
                o, total, top = (jnp.where(left, kept[0][i], kept[1][i]) for i in range(3))
                if before is None:
                    oo[l, rows, c] = o
                    ff_[l, 0, rows, c] = total
                    ff_[l, 1, rows, c] = top
                else:
                    total0, top0 = ff_[l, 0, rows, c], ff_[l, 1, rows, c]
                    both = jnp.maximum(top0, top)
                    a0, a1 = jnp.exp2((top0 - both) * SCALE), jnp.exp2((top - both) * SCALE)
                    inv = 1.0 / (total0 * a0 + total * a1)
                    ff_[l, before, rows, c] = a0 * inv
                    ff_[l, half, rows, c] = a1 * inv
                    oo[l, rows, c] = oo[l, rows, c] * (a0 * inv) + o * (a1 * inv)

    def dense_forward(l, rows, keep, krows):
        kx1, kx2, kr, kn1, kg, kgp = keep
        y = dot_nn(oo[l, rows, :].astype(BF), wo[l]) + bo[l : l + 1, :].astype(F32)
        h_in = hb[0, rows, :].astype(F32) if l == 0 else dr[rows, :]
        xh, rs = norm(h_in + y)
        kx1[krows, :] = xh.astype(kx1.dtype)
        kr[krows, 0:1] = rs
        n1 = xh * gain(l, 0) + shift(l, 0)
        n1b = n1.astype(BF)
        kn1[krows, :] = n1b
        u = dot_nn(n1b, wu[l]) + bu[l : l + 1, :].astype(F32)
        c0 = math.sqrt(2.0 / math.pi)
        u2 = u * u
        t = jnp.tanh(c0 * u * (1.0 + 0.044715 * u2))
        g = (0.5 * u * (1.0 + t)).astype(BF)
        kg[krows, :] = g
        kgp[krows, :] = (
            0.5 * (1.0 + t) + 0.5 * u * (1.0 - t * t) * (c0 * (1.0 + 3 * 0.044715 * u2))
        ).astype(BF)
        z, rs2 = norm(n1 + dot_nn(g, wd[l]) + bd[l : l + 1, :].astype(F32))
        kx2[krows, :] = z.astype(kx2.dtype)
        kr[krows, 1:2] = rs2
        h_out = z * gain(l, 1) + shift(l, 1)
        hb[l + 1, rows, :] = h_out.astype(BF)
        if l + 1 < LAYERS:
            dr[rows, :] = h_out

    def put(l, lo_row, value, first):
        span = slice(lo_row, lo_row + value.shape[0])
        acc[l, span, :] = value if first else acc[l, span, :] + value

    def put_small(l, row, value, first, c=slice(None)):
        span = slice(16 * l + row, 16 * l + row + 1)
        sm[span, c] = value if first else sm[span, c] + value

    same_head = (
        lax.broadcasted_iota(jnp.int32, (d, d), 0) // HEAD
        == lax.broadcasted_iota(jnp.int32, (d, d), 1) // HEAD
    ).astype(F32).astype(BF)

    def dense_backward(l, rows, g, keep, krows, first):
        kx1, kx2, kr, kn1, kg, kgp = keep
        xh = kx2[krows, :].astype(F32)
        put_small(l, 4, row_sum(g * xh), first)
        put_small(l, 6, row_sum(g), first)
        dr2 = norm_back(g * gain(l, 1), xh, kr[krows, 1:2])
        df = dr2.astype(BF)
        put_small(l, 9, row_sum(df.astype(F32)), first)
        wgrad = dot_tn(kg[krows, :], df)
        for c in range(2):
            put(l, (12 + 2 * c) * 256, wgrad[:, c * 128 : c * 128 + 128], first)
        du = (kgp[krows, :].astype(F32) * dot_nt(df, wd[l])).astype(BF)
        dub = row_sum(du.astype(F32))
        put_small(l, 7, dub[:, :d], first)
        put_small(l, 8, dub[:, d:], first)
        wgrad = dot_tn(kn1[krows, :], du)
        for c in range(4):
            put(l, (8 + c) * 256, wgrad[:, c * 128 : c * 128 + 128], first)
        dn1 = dr2 + dot_nt(du, wu[l])
        xh = kx1[krows, :].astype(F32)
        put_small(l, 3, row_sum(dn1 * xh), first)
        put_small(l, 5, row_sum(dn1), first)
        dr1 = norm_back(dn1 * gain(l, 0), xh, kr[krows, 0:1])
        dr[rows, :] = dr1
        dy = dr1.astype(BF)
        put_small(l, 2, row_sum(dy.astype(F32)), first)
        o = oo[l, rows, :]
        wgrad = dot_tn(o.astype(BF), dy)
        for c in range(2):
            put(l, (6 + c) * 256, wgrad[:, c * 128 : c * 128 + 128], first)
        do = dot_nt(dy, wo[l])
        x = do * o
        hi = x.astype(BF)
        lo_part = (x - hi.astype(F32)).astype(BF)
        delta = dot_nn(hi, same_head) + dot_nn(lo_part, same_head)
        lane = lax.broadcasted_iota(jnp.int32, (1, d), 1) % HEAD
        for half in range(2):
            f = ff_[l, half, rows, :]
            dob = (do * f).astype(BF)
            x = -(delta * f)
            hi = x.astype(BF)
            lo_part = (x - hi.astype(F32)).astype(BF)
            extra = jnp.where(lane == 0, hi, jnp.where(lane == 1, lo_part, jnp.zeros((), BF)))
            for pair in range(2):
                c = slice(pair * 128, pair * 128 + 128)
                dox[half, pair, rows, :128] = dob[:, c]
                dox[half, pair, rows, 128:] = extra[:, c]

    dq = ff_.at[1, 0]

    def attend_back(l, pair, half, ticks):
        c = slice(pair * 128, pair * 128 + 128)
        dot_t[half] = dox[half, pair, :, :128].T
        work = [(qb, side) for qb in range(n_qb) for side in range(2)]

        def rows_of(qb):
            return slice(qb * qb_rows, (qb + 1) * qb_rows)

        def prob_grad(qb, side):
            x = jnp.where(head_lanes(side, 256), dox[half, pair, rows_of(qb), :], jnp.zeros((), BF))
            return dot_nt(x, vx[l, half, pair])

        kept = [None, None]
        dp = prob_grad(*work[0])
        for i, (qb, side) in enumerate(work):
            rows = rows_of(qb)
            hr = slice(side * HEAD, (side + 1) * HEAD)
            krw = slice(pair * d + side * HEAD, pair * d + (side + 1) * HEAD)
            vrw = slice(pair * d + 128 + side * HEAD, pair * d + 128 + (side + 1) * HEAD)
            e = probs[half, qb, 2 * pair + side]
            dv = dot_nn(dot_t[half, hr, rows], e)
            dpn = prob_grad(*work[i + 1]) if i + 1 < len(work) else None
            ds = (e.astype(F32) * dp).astype(BF)
            dk = dot_nn(q_t[pair * 128 + side * HEAD : pair * 128 + (side + 1) * HEAD, rows], ds)
            if qb == 0:
                dkv[vrw, :] = dv
                dkv[krw, :] = dk
            else:
                dkv[vrw, :] += dv
                dkv[krw, :] += dk
            kept[side] = dot_nn(ds, kk[l, half, :, c])
            dp = dpn
            if side == 1:
                value = jnp.where(head_lanes(0, 128), kept[0], kept[1])
                dq[rows, c] = value if half == 1 else dq[rows, c] + value
                ticks()

    def pair_rows(pair):
        return slice(pair * d, (pair + 1) * d)

    def back_copy(l, pair):
        span = pl.ds(pair * d, d)
        return remote(skv.at[span], rkv.at[l, span], g_send.at[l, pair], g_recv.at[l, pair], mate)

    def send_back(l, pair):
        if l == 0:
            back_copy(1, pair).wait_send()
        r = pair * d
        skv[r : r + 128, :] = (dkv[r : r + 128, :] * HEAD**-0.5).astype(BF)
        skv[r + 128 : r + d, :] = dkv[r + 128 : r + d, :].astype(BF)
        back_copy(l, pair).start()

    def post(l, pair):
        r = pair * d
        c = slice(pair * 128, pair * 128 + 128)
        dqb = (dq[:, c] * HEAD**-0.5).astype(BF)
        back_copy(l, pair).wait_recv()
        dkb = (dkv[r : r + 128, :] * HEAD**-0.5 + rkv[l, r : r + 128, :].astype(F32)).astype(BF).T
        dvb = (dkv[r + 128 : r + d, :] + rkv[l, r + 128 : r + d, :].astype(F32)).astype(BF).T
        dqk = jnp.concatenate([dqb, dkb], axis=1)
        x = hb[l]
        wgrad = dot_tn(x, dqk)
        put(l, pair * 768, wgrad[:, :128], True)
        put(l, pair * 768 + 256, wgrad[:, 128:], True)
        put(l, pair * 768 + 512, dot_tn(x, dvb), True)
        put_small(l, 0, row_sum(dqb.astype(F32)), True, c)
        put_small(l, 1, row_sum(dvb.astype(F32)), True, c)
        dox[0, pair] = dqk
        dox[1, pair, :, :128] = dvb

    def input_grad(l):
        total = dr[...]
        for pair in range(2):
            c = slice(pair * 128, pair * 128 + 128)
            w = jnp.concatenate([wqkv[l, :, c], wqkv[l, :, d + c.start : d + c.stop]], axis=1)
            total = total + dot_nt(dox[0, pair], w)
        dv = jnp.concatenate([dox[1, 0, :, :128], dox[1, 1, :, :128]], axis=1)
        return total + dot_nt(dv, wqkv[l, :, 2 * d :])

    keep0 = (x1, x2, rss, n1s, gs, gps)
    f = wu.shape[2]

    def keep1(rb):
        low = skv if rb == 0 else rkv.at[0]
        return (
            dkv.at[:, rb * d : rb * d + d], dkv.at[:, (2 + rb) * d : (3 + rb) * d], rs_last.at[rb],
            n1_last.at[rb], low.at[:, 0:f], low.at[:, f : 2 * f],
        )

    def deliver(l):
        c = swap(2 + l, hb.at[l + 1], lo.at[l])
        here = pltpu.make_async_copy(hb.at[l + 1], lo.at[l], lo_sem.at[l])

        @pl.when(swaps)
        def _():
            c.start()

        @pl.when(stays)
        def _():
            here.start()

        return c, here

    finished = []

    def reduction(l, lo_row, rows, big, sbuf, rbuf, so, ticks, back_ticks):
        i = len(groups)
        span = pl.ds(lo_row, rows)
        c = pltpu.make_async_copy(red.at[l, span], red_out.at[l, span], red_done.at[i])

        def finish():
            c.start()
            finished.append(c)

        return Reduction(
            acc, red, sbuf, rbuf, red_send.at[i], red_recv.at[i], l, lo_row, rows,
            rounds_big if big else rounds_low, ticks + (2,) * further + back_ticks, so, finish,
        ).steps()

    groups = {}
    groups[1, "dense"] = reduction(1, 1536, 2560, True, sb_e, rb_e.at[1], 0, (2, 3, 2), (2, 4, 2))
    groups[1, "qkv"] = reduction(1, 0, 1536, True, sb_q, rb_q.at[1], 0, (3, 2, 3), (2, 2, 1))
    groups[0, "dense"] = reduction(0, 1536, 2560, True, sb_e, rb_e.at[0], 0, (2, 3, 2), (2, 3, 1))
    groups[0, 0] = reduction(0, 0, 768, False, sb_q, rb_q.at[0], 0, (2, 2, 2), (2, 1))
    groups[0, 1] = reduction(0, 768, 768, False, sb_q, rb_q.at[0], rb_q.shape[1] // 2, (1, 1, 1), (1, 1))

    @pl.when(swaps)
    def _():
        for before, after in zip(arrive, arrive[1:]):
            before.wait_send()
            after.start()
        arrive_mask.wait()
        arrive[0].wait_recv()

    @pl.when(stays)
    def _():
        here_tok.wait()
        here_mask.wait()

    for c in loads:
        c.wait()
    embed(0)
    project(0, 0)

    @pl.when(stays)
    def _():
        for rb in range(1, n_rb):
            embed(rb)
            project(0, rb)
        send_kv(0)

    @pl.when(swaps)
    def _():
        take_kv(0)

    attend(0, apart, 0, None)

    @pl.when(swaps)
    def _():
        for rb in range(1, n_rb):
            arrive[rb].wait_recv()
            embed(rb)
            project(0, rb)
        send_kv(0)
        arrive_cot.start()

    for qb in range(1, n_qb):
        attend(0, apart, qb, None)
    keep_probs = [
        pltpu.make_async_copy(probs.at[half], saved.at[half], p_sem.at[i])
        for i, half in enumerate((apart, 1 - apart))
    ]
    keep_probs[0].start()

    @pl.when(stays)
    def _():
        take_kv(0)

    for qb in range(n_qb):
        attend(0, 1 - apart, qb, apart)
    keep_probs[1].start()
    for c in kv_copies(0):
        c.wait_send()
    for rb in range(n_rb):
        rows = block_rows(rb)
        dense_forward(0, rows, keep0, rows)
        project(1, rb)
    send_kv(1)
    results = [deliver(0)]
    for c in keep_probs:
        c.wait()
    for qb in range(n_qb):
        attend(1, 0, qb, None)
    take_kv(1)
    for qb in range(n_qb):
        attend(1, 1, qb, 0)
    for c in kv_copies(1):
        c.wait_send()

    @pl.when(swaps)
    def _():
        arrive[-1].wait_send()
        arrive_cot.wait()

    @pl.when(stays)
    def _():
        here_cot.wait()

    own = slice(0, rb_rows)
    for rb in range(n_rb):
        rows = block_rows(rb)
        dense_forward(1, rows, keep1(rb), own)
    for rb in range(n_rb):
        rows = block_rows(rb)
        dense_backward(1, rows, cotin[rows, :].astype(F32), keep1(rb), own, rb == 0)

    def fetch(pair, half):
        heads = pl.ds(2 * pair, 2)
        return pltpu.make_async_copy(
            saved.at[half, :, heads], probs.at[half, :, heads], p_sem.at[2 + 2 * pair + half]
        )

    queue = []
    tick = functools.partial(advance, queue)
    for l in reversed(range(LAYERS)):
        if l == 0:
            for rb in range(n_rb):
                rows = block_rows(rb)
                dense_backward(0, rows, dr[rows, :], keep0, rows, rb == 0)
                tick()
        launch(queue, groups[l, "dense"])
        q_t[...] = qs[l].T
        for pair in range(2):
            for half in (1, 0):
                if l == 0:
                    fetch(pair, half).wait()
                attend_back(l, pair, half, tick)
                if l == 1:
                    fetch(pair, half).start()
                if half == 1:
                    send_back(l, pair)
            post(l, pair)
            tick()
            if l == 0:
                launch(queue, groups[0, pair], pair == 1)
            elif pair == 0:
                results.append(deliver(1))
        if l == 1:
            launch(queue, groups[1, "qkv"])
            dr[...] = input_grad(1)
            tick()

    tg_rows = n // TG_PARTS
    tg_out = [
        swap(5 + n_rb + i, cotin.at[pl.ds(i * tg_rows, tg_rows)], tg.at[pl.ds(i * tg_rows, tg_rows)])
        for i in range(TG_PARTS)
    ]
    tg_here = pltpu.make_async_copy(cotin, tg, lo_sem.at[2])

    def send_tg(*parts):
        @pl.when(swaps)
        def _():
            for i in parts:
                tg_out[i].start()

    dh = input_grad(0)
    hi = dh.astype(BF)
    cotin[...] = hi
    send_tg(*TG_PLAN[0])

    @pl.when(stays)
    def _():
        tg_here.start()

    lo_part = (dh - hi.astype(F32)).astype(BF)
    masks = mask_rows(slice(0, n))
    sm[10:11, :] = (dot_nn(masks, hi) + dot_nn(masks, lo_part))[0:1, :]
    sm[11:16, :] = jnp.zeros((5, d), F32)
    sm[26:32, :] = jnp.zeros((6, d), F32)

    def small_steps():
        k = 0
        for _, values, peers in rounds_big:
            rsm[2 * k] = sm[...]
            copies = []
            for m in range(1, 1 << len(values)):
                c = remote(rsm.at[2 * k], rsm.at[2 * (k + m) - 1], sm_send.at[k + m - 1], sm_recv.at[k + m - 1], peers[m])
                c.start()
                copies.append(c)
            yield
            for c in copies:
                c.wait()
            if len(values) == 1:
                sm[...] += rsm[2 * k + 1]
            else:
                sm[...] = (sm[...] + rsm[2 * k + 1]) + (rsm[2 * k + 3] + rsm[2 * k + 5])
            k += (1 << len(values)) - 1

    launch(queue, small_steps())
    for parts in TG_PLAN[1:]:
        tick()
        send_tg(*parts)
    drain(*queue)
    out = pltpu.make_async_copy(sm, small, lo_sem.at[4])
    out.start()
    for pair in range(2):
        back_copy(0, pair).wait_send()

    for c in finished:
        c.wait()
    out.wait()

    @pl.when(swaps)
    def _():
        for c, _ in results:
            c.wait()
        for c in tg_out:
            c.wait()

    @pl.when(stays)
    def _():
        for _, here in results:
            here.wait()
        tg_here.wait()


def spread_kernel(
    lo_in, tg_in, red_in, small_in, msk_in,
    o_lo, o_tg, o_mv, o_qkv, o_qvb, o_wo, o_bo, o_gain, o_bias, o_wu, o_bu, o_wd, o_bd,
    lo, tg, red, small, msk, tgf, qkv, wo, wu, wd, mv, qvb, bo, gain, bias, bu, bd, sem,
):
    early, late = pl.ds(1536, 2560), pl.ds(0, 1536)
    order = [(1, early), (1, late), (0, early), (0, late)]
    pairs = [(red_in.at[l, r], red.at[l, r]) for l, r in order]
    pairs += [(msk_in, msk), (tg_in, tg), (small_in, small), (lo_in, lo)]
    takes = [pltpu.make_async_copy(a, b, sem.at[i]) for i, (a, b) in enumerate(pairs)]
    for c in takes:
        c.start()
    gives = []

    def give(a, b):
        c = pltpu.make_async_copy(a, b, sem.at[len(takes) + len(gives)])
        c.start()
        gives.append(c)

    n, d = tg.shape
    for i, (l, r) in enumerate(order):

        def block(b, rows=256, l=l):
            return red[l, b * 256 : b * 256 + rows, :].astype(F32)

        takes[i].wait()
        if r is early:
            for c in range(2):
                wd[l, :, c * 128 : c * 128 + 128] = block(12 + 2 * c, 512)
            give(wd.at[l], o_wd.at[l])
            for c in range(4):
                wu[l, :, c * 128 : c * 128 + 128] = block(8 + c)
            give(wu.at[l], o_wu.at[l])
            for c in range(2):
                wo[l, :, c * 128 : c * 128 + 128] = block(6 + c)
            give(wo.at[l], o_wo.at[l])
        else:
            for c in range(6):
                qkv[l, :, c * 128 : c * 128 + 128] = block(c % 2 * 3 + c // 2)
            give(qkv.at[l], o_qkv.at[l])
    takes[4].wait()
    takes[5].wait()
    mask_rows = jnp.broadcast_to(msk[...].astype(F32), (16, n)).astype(BF)
    first_row = (lax.broadcasted_iota(jnp.int32, (16, d), 0) == 0).astype(F32).astype(BF)
    is_masked = dot_tn(mask_rows, first_row) > 0.5
    tgf[...] = jnp.where(is_masked, 0.0, tg[...].astype(F32))
    give(tgf, o_tg.at[0])
    takes[6].wait()
    mv[...] = small[10:11, :]
    for l in range(LAYERS):

        def row(r, l=l):
            return small[16 * l + r : 16 * l + r + 1, :]

        qvb[l, 0:1, :] = row(0)
        qvb[l, 1:2, :] = row(1)
        bo[l : l + 1, :] = row(2)
        gain[l, 0:1, :] = row(3)
        gain[l, 1:2, :] = row(4)
        bias[l, 0:1, :] = row(5)
        bias[l, 1:2, :] = row(6)
        bu[l : l + 1, :d] = row(7)
        bu[l : l + 1, d:] = row(8)
        bd[l : l + 1, :] = row(9)
    for a, b in ((mv, o_mv), (qvb, o_qvb), (bo, o_bo), (gain, o_gain), (bias, o_bias), (bu, o_bu), (bd, o_bd)):
        give(a, b)
    takes[7].wait()
    give(lo, o_lo.at[:, 0])
    for c in gives:
        c.wait()


def shards(sizes, *args):
    (
        tokens, masked, mask_vector, qkv_weight, qv_bias, out_weight, out_bias, norm_gain,
        norm_bias, up_weight, up_bias, down_weight, down_bias, cotangent,
    ) = args
    _, n, d = tokens.shape
    ff = up_weight.shape[2]
    qb = min(512, n)
    rb = min(512, n)
    further = int(math.log2(sizes[0])) - 4
    n_copies = 7 + further
    hbm = pl.BlockSpec(memory_space=pl.ANY)

    def room(rows, big):
        sent = rows // 2 + 3 * (rows // 8)
        return sent + (3 * (rows // 32) + further * (rows // 32) if big else (3 + further) * (rows // 8))

    V = pltpu.VMEM
    dma = pltpu.SemaphoreType.DMA

    scratch = [
        *[
            V(w.shape, BF)
            for w in (
                mask_vector, qkv_weight, qv_bias, out_weight, out_bias, norm_gain, norm_bias, up_weight,
                up_bias, down_weight, down_bias,
            )
        ],
        V((LAYERS, 4096, 128), BF),
        V((1, n), jnp.int32), V((n, d), BF), V((LAYERS + 1, n, d), BF), V((n, d), F32),
        V((LAYERS, n, d), BF), V((LAYERS, 2, n, d), BF), V((LAYERS, 2, 2, n, 256), BF),
        V((LAYERS, n, d), F32), V((LAYERS, 2, n, d), F32),
        V((n, d), BF), V((n, d), BF), V((n, 2), F32),
        V((n, d), BF), V((n, ff), BF), V((n, ff), BF),
        V((n // rb, rb, d), BF), V((n // rb, rb, 2), F32),
        V((2, 2, n, 256), BF), V((2, 128, n), BF), V((d, n), BF),
        V((2 * d, n), F32), V((2 * d, n), BF), V((LAYERS, 2 * d, n), BF),
        V((LAYERS, 4096, 128), F32), V((32, d), F32), V((2 * n_copies, 32, d), F32),
        V((2, n // qb, 4, qb, n), BF),
        V((room(2560, True), 128), BF), V((2 * room(768, False), 128), BF),
        V((LAYERS, room(2560, True), 128), BF), V((LAYERS, 2 * room(768, False), 128), BF),
        dma((5 + n // rb + TG_PARTS,)), dma((5 + n // rb + TG_PARTS,)), dma((LAYERS, 2)), dma((LAYERS, 2)), dma((LAYERS, 2)), dma((LAYERS, 2)),
        dma((6,)), dma((5,)),
        dma((5, 14 + further)), dma((5, 14 + further)), dma((5,)), dma((n_copies,)), dma((n_copies,)),
        dma((13,)),
    ]
    lo, tg, red, small, _ = pl.pallas_call(
        functools.partial(main_kernel, sizes, qb, rb),
        out_shape=(
            jax.ShapeDtypeStruct((LAYERS, n, d), BF),
            jax.ShapeDtypeStruct((n, d), BF),
            jax.ShapeDtypeStruct((LAYERS, 4096, 128), BF),
            jax.ShapeDtypeStruct((32, d), F32),
            jax.ShapeDtypeStruct((2, n // qb, 4, qb, n), BF),
        ),
        in_specs=[hbm] * 14,
        out_specs=(hbm,) * 5,
        scratch_shapes=scratch,
        compiler_params=pltpu.CompilerParams(
            collective_id=0, has_side_effects=True, vmem_limit_bytes=63 << 20
        ),
        name="encoder",
    )(
        tokens[0], masked, mask_vector, qkv_weight, qv_bias, out_weight, out_bias,
        norm_gain, norm_bias, up_weight, up_bias, down_weight, down_bias, cotangent[0],
    )

    def f32(*shape):
        return jax.ShapeDtypeStruct(shape, F32)

    grads = (
        f32(1, d), f32(LAYERS, d, 3 * d), f32(LAYERS, 2, d), f32(LAYERS, d, d), f32(LAYERS, d),
        f32(LAYERS, 2, d), f32(LAYERS, 2, d), f32(LAYERS, d, ff), f32(LAYERS, ff),
        f32(LAYERS, ff, d), f32(LAYERS, d),
    )
    order = (1, 3, 7, 9, 0, 2, 4, 5, 6, 8, 10)
    outs = pl.pallas_call(
        spread_kernel,
        out_shape=(jax.ShapeDtypeStruct((LAYERS, 1, n, d), BF), f32(1, n, d), *grads),
        in_specs=[hbm] * 5,
        out_specs=(hbm,) * 13,
        scratch_shapes=[
            V((LAYERS, n, d), BF), V((n, d), BF), V((LAYERS, 4096, 128), BF), V((32, d), F32),
            V((1, n), jnp.int32), V((n, d), F32), *[V(grads[i].shape, F32) for i in order], dma((32,)),
        ],
        compiler_params=pltpu.CompilerParams(vmem_limit_bytes=63 << 20),
        name="spread",
    )(lo, tg, red, small, masked)
    return (*outs[:2], outs[2][0], *outs[3:])


def solution(mesh):
    rows = P("dp", "seq", None)
    in_specs = (rows, P("dp", "seq"), *[P()] * 11, rows)
    out_specs = (P(None, "dp", "seq", None), rows, *[P()] * 11)
    sizes = (mesh.shape["dp"], mesh.shape["seq"])
    return jax.shard_map(
        functools.partial(shards, sizes), mesh=mesh, in_specs=in_specs, out_specs=out_specs, check_vma=False
    )
```
